32 devices in a mesh: seq: 8 (over y, x, core), head: 4 (over z).
Axes of the slice: x: 2, y: 2, z: 4, core: 2. Of those that a mesh axis runs over, the one named last changes fastest.
Arguments:
- byte_in: bfloat16 [1024, 8, 1024], P('seq'), may hold values from -6 to 6
- local_gain: float32 [1024], replicated, may hold values from 0.25 to 1.75
- local_qkv: bfloat16 [1024, 3, 1024], P(None, None, 'head'), may hold values from -0.1875 to 0.1875
- local_out: bfloat16 [1024, 1024], P('head'), may hold values from -0.1875 to 0.1875
- mlp_up: bfloat16 [1024, 4096], P(None, 'head'), may hold values from -0.1875 to 0.1875
- mlp_down: bfloat16 [4096, 1024], P('head'), may hold values from -0.09375 to 0.09375
- local_scale: float32 [8], P('head'), may hold values from 1 to 40
- patch_proj: bfloat16 [1024, 256], replicated, may hold values from -0.1875 to 0.1875
- global_gain: float32 [2048], replicated, may hold values from 0.25 to 1.75
- global_qkv: bfloat16 [2048, 3, 2048], P(None, None, 'head'), may hold values from -0.125 to 0.125
- global_out: bfloat16 [2048, 2048], P('head'), may hold values from -0.125 to 0.125
- global_scale: float32 [16], P('head'), may hold values from 1 to 40
- back_proj: bfloat16 [256, 1024], replicated, may hold values from -0.375 to 0.375
- owners: int32 [8, 16], replicated, may hold values from 0 to 7, as said below
Outputs:
- byte_out: bfloat16 [1024, 8, 1024], P('seq', 'head')
- global_state: bfloat16 [1024, 2048], P('seq', 'head')
The draws below stay inside these ranges and needn't reach their ends.
Inputs may be any that keep to these rules, and one draw needn't show every extreme that they name: `owners`: row s names, for each of the 16 blocks of 8 patches of byte range s in order, its owner; each row names every owner exactly twice.
All inputs are finite; a program needn't handle non-finite values.
Results may differ from the reference program's by a relative error of at most 0.028.
The reference program's roundings to bfloat16 on the way count: a program that leaves them out, or rounds other values in their place, can miss the bound.
Values may be sent and summed in bfloat16 or wider, within the bound.
No kernel may reach another device: no remote copies, remote signals or barrier semaphores. Data moves between devices by JAX's collectives and lax.ppermute only.
A program may use at most 128 MiB of HBM per device.

```python
import math
import jax
import jax.numpy as jnp
from jax import lax

DL = 1024
FF = 4096
LHEADS = 8
GHEADS = 16
HEAD = 128
G = 2048
GP = 256
PATCH = 8
PATCH_DEV = 128
BLOCK = 8
SOURCES = 8
PATCHES = 1024


def draw_owners(key, part):
    subkeys = jax.random.split(jax.random.fold_in(key, 11), SOURCES)
    listed = jax.vmap(lambda subkey: jax.random.permutation(subkey, 2 * SOURCES))(subkeys)
    return (listed // 2).astype(jnp.int32)


def draw_local_scale(key, part):
    return jax.random.uniform(jax.random.fold_in(key, 22), (LHEADS,), jnp.float32, 1.0, 4.0)


def draw_global_scale(key, part):
    return jax.random.uniform(jax.random.fold_in(key, 32), (GHEADS,), jnp.float32, 1.0, 4.0)


def steps_of(stream_key, extent, shards, low, largest):
    loudness, own = 1.0, jax.random.fold_in(stream_key, 6)
    for axis_at, blocks in shards:
        steps = jnp.exp(jax.random.uniform(jax.random.fold_in(own, axis_at), (blocks,), jnp.float32, low / len(shards), largest / len(shards)))
        loudness = loudness * jnp.repeat(steps, extent[axis_at] // blocks).reshape([-1 if axis == axis_at else 1 for axis in range(len(extent))])
    return loudness


def centred(own_key, extent, scale, bound, cuts=(), kind=jnp.bfloat16):
    drawn = jax.random.normal(own_key, extent, jnp.float32) * scale
    if len(cuts) > 0:
        drawn = steps_of(own_key, extent, cuts, -0.22, 0.18) * drawn
    return jnp.clip(drawn, min=-bound, max=bound).astype(kind)


def setup_inputs(seed: int = 0) -> dict:
    streams_of = jax.random.split(jax.random.key(seed), 15)
    byte_in = centred(streams_of[0], (PATCHES, PATCH, DL), 1.0, 6.0, ((0, 8),))
    local_gain = jnp.clip(1.0 + 0.15 * jax.random.normal(streams_of[1], (DL,), jnp.float32), 0.25, 1.75)
    local_qkv = centred(streams_of[2], (DL, 3, DL), DL ** -0.5, 0.1875, ((2, 4),))
    local_out = centred(streams_of[3], (DL, DL), DL ** -0.5, 0.1875, ((0, 4),))
    mlp_up = centred(streams_of[4], (DL, FF), DL ** -0.5, 0.1875, ((1, 4),))
    mlp_down = centred(streams_of[5], (FF, DL), FF ** -0.5, 0.09375, ((0, 4),))
    local_scale = draw_local_scale(jax.random.fold_in(streams_of[14], 71), 0)
    patch_proj = centred(streams_of[7], (DL, GP), DL ** -0.5, 0.1875)
    global_gain = jnp.clip(1.0 + 0.15 * jax.random.normal(streams_of[8], (G,), jnp.float32), 0.25, 1.75)
    global_qkv = centred(streams_of[9], (G, 3, G), G ** -0.5, 0.125, ((2, 4),))
    global_out = centred(streams_of[10], (G, G), G ** -0.5, 0.125, ((0, 4),))
    global_scale = draw_global_scale(jax.random.fold_in(streams_of[14], 71), 0)
    back_proj = centred(streams_of[12], (GP, DL), GP ** -0.5, 0.375)
    owners = draw_owners(jax.random.fold_in(streams_of[14], 71), 0)
    return {"byte_in": byte_in, "local_gain": local_gain, "local_qkv": local_qkv, "local_out": local_out, "mlp_up": mlp_up, "mlp_down": mlp_down, "local_scale": local_scale, "patch_proj": patch_proj, "global_gain": global_gain, "global_qkv": global_qkv, "global_out": global_out, "global_scale": global_scale, "back_proj": back_proj, "owners": owners}


EPSILON = 1e-06
NEGATIVE = -1e+30

def rms_norm(values, gain):
    mean_square = lax.optimization_barrier(jnp.mean(values * values, axis=-1, keepdims=True))
    return values * lax.rsqrt(mean_square + EPSILON) * gain

def unit_heads(values, head_count):
    shaped = values.reshape(values.shape[0], head_count, -1)
    mean_square = lax.optimization_barrier(jnp.mean(shaped * shaped, axis=-1, keepdims=True))
    return shaped * lax.rsqrt(mean_square + EPSILON)

def through_bf16(values):
    return lax.optimization_barrier(values.astype(jnp.bfloat16)).astype(jnp.float32)

def patch_attention(queries, key_rows, values, head_scale):
    patch_span = queries.shape[1]
    scores = jnp.einsum('pihd,pjhd->phij', queries.astype(jnp.float32), key_rows.astype(jnp.float32))
    scores = scores * (head_scale[:, None, None] / math.sqrt(HEAD))
    causal = jnp.tril(jnp.ones((patch_span, patch_span), dtype=bool))
    scores = jnp.where(causal, scores, NEGATIVE)
    row_max = lax.optimization_barrier(jnp.max(scores, axis=-1, keepdims=True))
    weights = jnp.where(causal, jnp.exp(scores - row_max), 0.0)
    weight_sum = lax.optimization_barrier(jnp.sum(weights, axis=-1))
    summed = jnp.einsum('phij,pjhd->pihd', through_bf16(weights), values.astype(jnp.float32))
    return (summed / jnp.transpose(weight_sum, (0, 2, 1))[..., None]).astype(jnp.bfloat16)

def local_section(byte_block, local_gain, local_qkv, local_out, mlp_up, mlp_down, local_scale, patch_proj):
    patch_count = byte_block.shape[0]
    byte_rows = byte_block.reshape(-1, DL).astype(jnp.float32)
    normed = rms_norm(byte_rows, local_gain).astype(jnp.bfloat16)
    projected = jnp.dot(normed, local_qkv.reshape(DL, 3 * DL), preferred_element_type=jnp.float32)
    queries = unit_heads(projected[:, :DL], LHEADS).astype(jnp.bfloat16).reshape(patch_count, PATCH, LHEADS, HEAD)
    key_rows = unit_heads(projected[:, DL:2 * DL], LHEADS).astype(jnp.bfloat16).reshape(patch_count, PATCH, LHEADS, HEAD)
    values = projected[:, 2 * DL:].astype(jnp.bfloat16).reshape(patch_count, PATCH, LHEADS, HEAD)
    attended = patch_attention(queries, key_rows, values, local_scale).reshape(-1, DL)
    attn_term = jnp.dot(attended, local_out, preferred_element_type=jnp.float32)
    activated = jax.nn.gelu(jnp.dot(normed, mlp_up, preferred_element_type=jnp.float32), approximate=True).astype(jnp.bfloat16)
    mlp_term = jnp.dot(activated, mlp_down, preferred_element_type=jnp.float32)
    byte_state = (byte_rows + attn_term + mlp_term).astype(jnp.bfloat16)
    patch_in = jnp.dot(byte_state, patch_proj, preferred_element_type=jnp.float32).reshape(patch_count, PATCH * GP).astype(jnp.bfloat16)
    return (byte_state.reshape(patch_count, PATCH, DL), patch_in)

def global_head(arguments):
    head_query, head_keys, head_values, head_scale = arguments
    positions = jnp.arange(PATCHES, dtype=jnp.int32)

    def query_block(block_args):
        block_query, block_pos = block_args
        scores = jnp.dot(block_query, head_keys.T, preferred_element_type=jnp.float32) * (head_scale / math.sqrt(HEAD))
        visible = positions[None, :] <= block_pos[:, None]
        scores = jnp.where(visible, scores, NEGATIVE)
        row_max = lax.optimization_barrier(jnp.max(scores, axis=-1, keepdims=True))
        weights = jnp.where(visible, jnp.exp(scores - row_max), 0.0)
        weight_sum = lax.optimization_barrier(jnp.sum(weights, axis=-1))
        summed = jnp.dot(weights.astype(jnp.bfloat16), head_values, preferred_element_type=jnp.float32)
        return (summed / weight_sum[:, None]).astype(jnp.bfloat16)
    outputs = lax.map(query_block, (head_query.reshape(-1, PATCH_DEV, HEAD), positions.reshape(-1, PATCH_DEV)))
    return outputs.reshape(PATCHES, HEAD)

def reference(byte_in, local_gain, local_qkv, local_out, mlp_up, mlp_down, local_scale, patch_proj, global_gain, global_qkv, global_out, global_scale, back_proj, owners):

    def local_part(byte_block):
        return local_section(byte_block, local_gain, local_qkv, local_out, mlp_up, mlp_down, local_scale, patch_proj)
    byte_state, patch_in = lax.map(local_part, byte_in.reshape(-1, PATCH_DEV, PATCH, DL))
    byte_state = byte_state.reshape(PATCHES, PATCH, DL)
    patch_in = patch_in.reshape(PATCHES, G)
    gnormed = rms_norm(patch_in.astype(jnp.float32), global_gain).astype(jnp.bfloat16)
    global_proj = jnp.dot(gnormed, global_qkv.reshape(G, 3 * G), preferred_element_type=jnp.float32)
    gquery = unit_heads(global_proj[:, :G], GHEADS).astype(jnp.bfloat16)
    global_keys = unit_heads(global_proj[:, G:2 * G], GHEADS).astype(jnp.bfloat16)
    gvalues = global_proj[:, 2 * G:].astype(jnp.bfloat16).reshape(PATCHES, GHEADS, HEAD)
    attended = lax.map(global_head, (jnp.transpose(gquery, (1, 0, 2)), jnp.transpose(global_keys, (1, 0, 2)), jnp.transpose(gvalues, (1, 0, 2)), global_scale))
    attended = jnp.transpose(attended, (1, 0, 2)).reshape(PATCHES, G)
    result = (patch_in.astype(jnp.float32) + jnp.dot(attended, global_out, preferred_element_type=jnp.float32)).astype(jnp.bfloat16)
    position = jnp.arange(PATCHES, dtype=jnp.int32)
    source = (position // PATCH_DEV).astype(jnp.int32)
    column = (position % PATCH_DEV // BLOCK).astype(jnp.int32)
    listed = owners[source, column].astype(jnp.int32)
    ordering = jnp.argsort(listed * PATCHES + position)
    global_state = result[ordering]
    back_term = jnp.dot(result.reshape(PATCHES * PATCH, GP), back_proj, preferred_element_type=jnp.float32)
    byte_out = (byte_state.reshape(-1, DL).astype(jnp.float32) + back_term).reshape(PATCHES, PATCH, DL).astype(jnp.bfloat16)
    return (byte_out, global_state)
```

```python
import functools
import math

import jax
import jax.numpy as jnp
from jax import lax
from jax.experimental import pallas as pl
from jax.experimental.pallas import tpu as pltpu
from jax.sharding import PartitionSpec as P

EPSILON = 1e-06
NEGATIVE = -1e30
F32 = jnp.float32
BF16 = jnp.bfloat16
VMEM = pl.BlockSpec(memory_space=pltpu.VMEM)
SMEM = pl.BlockSpec(memory_space=pltpu.SMEM)


def dot(left, right):
    return jnp.dot(left, right, preferred_element_type=F32)


def dot_t(left, right):
    return lax.dot_general(left, right, (((1,), (1,)), ((), ())), preferred_element_type=F32)


def unit(values):
    return (values * lax.rsqrt(jnp.mean(values * values, axis=-1, keepdims=True) + EPSILON)).astype(BF16)


def gelu(values):
    inner = math.sqrt(2.0 / math.pi) * (values + 0.044715 * (values * values * values))
    return 0.5 * values * (1.0 + jnp.tanh(inner))


def local_kernel(
    span, own, me_ref, scale_ref, x_ref, gain_ref, qkv_ref, out_ref, up_ref, down_ref, proj_ref, part_ref, share_ref
):
    rows = x_ref.shape[0]
    group = rows // span
    at = lax.broadcasted_iota(jnp.int32, (rows, rows), 0)
    to = lax.broadcasted_iota(jnp.int32, (rows, rows), 1)
    order = (to == (at % group) * span + at // group).astype(F32).astype(BF16)
    x = dot(order, x_ref[...])
    normed = (
        x * lax.rsqrt(jnp.mean(x * x, axis=-1, keepdims=True) + EPSILON) * gain_ref[...]
    ).astype(BF16)
    query, key, value = (dot(normed, qkv_ref[i]) for i in range(3))
    seen = (at % group == to % group) & (to <= at)
    heads = scale_ref.shape[0]
    depth = query.shape[1] // heads
    attended = []
    for h in range(heads):
        cut = slice(h * depth, (h + 1) * depth)
        scores = dot_t(unit(query[:, cut]), unit(key[:, cut])) * (scale_ref[h] / math.sqrt(depth))
        scores = jnp.where(seen, scores, NEGATIVE)
        weights = jnp.exp(scores - jnp.max(scores, axis=-1, keepdims=True))
        total = jnp.sum(weights, axis=-1, keepdims=True)
        attended.append((dot(weights.astype(BF16), value[:, cut].astype(BF16)) / total).astype(BF16))
    act = gelu(dot(normed, up_ref[...])).astype(BF16)
    partial = dot(jnp.concatenate(attended, axis=1), out_ref[...]) + dot(act, down_ref[...])
    byte = lax.broadcasted_iota(jnp.int32, (rows, 1), 0) // group
    partial = (partial + jnp.where(byte // own == me_ref[0], x, 0.0)).astype(BF16)
    part_ref[...] = partial.reshape(part_ref.shape)
    share = dot(partial, proj_ref[...]).astype(BF16)
    width = share.shape[1]
    for b in range(span):
        share_ref[b // own, :, (b % own) * width : (b % own + 1) * width] = share[b * group : (b + 1) * group]


def local_part(me, scale, x, gain, qkv, out, up, down, proj, span, ways, group):
    rows, width = x.shape
    patches = rows // span
    own = span // ways
    once = lambda a: pl.BlockSpec(a.shape, lambda i: (0,) * a.ndim, pipeline_mode=pl.Buffered(1))
    return pl.pallas_call(
        functools.partial(local_kernel, span, own),
        grid=(patches // group,),
        in_specs=[SMEM, SMEM, pl.BlockSpec((group * span, width), lambda i: (i, 0))]
        + [once(a) for a in (gain, qkv, out, up, down, proj)],
        out_specs=(
            pl.BlockSpec((span, group, width), lambda i: (0, i, 0)),
            pl.BlockSpec((ways, group, own * proj.shape[1]), lambda i: (0, i, 0)),
        ),
        out_shape=(
            jax.ShapeDtypeStruct((span, patches, width), BF16),
            jax.ShapeDtypeStruct((ways, patches, own * proj.shape[1]), BF16),
        ),
        compiler_params=pltpu.CompilerParams(vmem_limit_bytes=48 * 2**20),
        name="local_part",
    )(me, scale, x, gain, qkv, out, up, down, proj)


def heads_kernel(kinds, depth, ids_ref, gain_ref, *refs):
    ways = gain_ref.shape[0]
    shares, weights, outs = refs[:ways], refs[ways : ways + len(kinds)], refs[ways + len(kinds) :]
    width = shares[0].shape[1]
    values = [s[...].astype(F32) for s in shares]
    square = sum(jnp.sum(v * v, axis=-1, keepdims=True) for v in values)
    factor = lax.rsqrt(square / (ways * width) + EPSILON)
    normed = [(v * factor * gain_ref[ids_ref[c]]).astype(BF16) for c, v in enumerate(values)]
    for kind, weight, out in zip(kinds, weights, outs):
        mixed = sum(
            dot(n, weight[0, pl.ds(pl.multiple_of(ids_ref[c] * width, width), width), :]) for c, n in enumerate(normed)
        )
        if kind < 2:
            for h in range(mixed.shape[1] // depth):
                out[:, h * depth : (h + 1) * depth] = unit(mixed[:, h * depth : (h + 1) * depth])
        else:
            out[...] = mixed.astype(BF16)


def global_heads(kinds, depth, ids, gain, shares, qkv):
    shape = jax.ShapeDtypeStruct((shares[0].shape[0], qkv.shape[2]), BF16)
    pick = lambda kind: pl.BlockSpec((1,) + qkv.shape[1:], lambda i: (kind, 0, 0), pipeline_mode=pl.Buffered(1))
    whole = lambda a: pl.BlockSpec(a.shape, lambda i: (0,) * a.ndim)
    return pl.pallas_call(
        functools.partial(heads_kernel, kinds, depth),
        grid=(1,),
        in_specs=[SMEM, whole(gain)] + [whole(s) for s in shares] + [pick(kind) for kind in kinds],
        out_specs=tuple(whole(shape) for _ in kinds),
        out_shape=tuple(shape for _ in kinds),
        compiler_params=pltpu.CompilerParams(vmem_limit_bytes=16 * 2**20),
        name="global_heads",
    )(ids, gain, *shares, *([qkv] * len(kinds)))


def attend_kernel(count, ids_ref, scale_ref, q_ref, *refs):
    keys, values, (proj_ref, out_ref) = refs[:count], refs[count : 2 * count], refs[2 * count :]
    rows = q_ref.shape[0]
    at = lax.broadcasted_iota(jnp.int32, (rows, rows), 0)
    to = lax.broadcasted_iota(jnp.int32, (rows, rows), 1)
    heads = scale_ref.shape[0]
    depth = q_ref.shape[1] // heads
    me = ids_ref[0]
    seen = [to + ids_ref[i] * rows <= at + me * rows for i in range(count)]
    attended = []
    for h in range(heads):
        cut = slice(h * depth, (h + 1) * depth)
        query = q_ref[:, cut]
        factor = scale_ref[h] / math.sqrt(depth)
        scores = [jnp.where(s, dot_t(query, k[:, cut]) * factor, NEGATIVE) for s, k in zip(seen, keys)]
        top = functools.reduce(jnp.maximum, [jnp.max(s, axis=-1, keepdims=True) for s in scores])
        weights = [jnp.exp(s - top) for s in scores]
        total = sum(jnp.sum(w, axis=-1, keepdims=True) for w in weights)
        summed = sum(dot(w.astype(BF16), v[:, cut]) for w, v in zip(weights, values))
        attended.append((summed / total).astype(BF16))
    update = dot(jnp.concatenate(attended, axis=1), proj_ref[...]).astype(BF16)
    width = out_ref.shape[2]
    for c in range(out_ref.shape[0]):
        out_ref[c] = update[:, c * width : (c + 1) * width]


def attend(ids, scale, query, keys, values, proj, ways):
    rows = query.shape[0]
    return pl.pallas_call(
        functools.partial(attend_kernel, len(keys)),
        in_specs=[SMEM, SMEM] + [VMEM] * (2 + 2 * len(keys)),
        out_specs=VMEM,
        out_shape=jax.ShapeDtypeStruct((ways, rows, proj.shape[1] // ways), BF16),
        compiler_params=pltpu.CompilerParams(vmem_limit_bytes=40 * 2**20),
        name="attend",
    )(ids, scale, query, *keys, *values, proj)


def result_kernel(count, order_ref, own_ref, *refs):
    pieces, (result_ref, routed_ref) = refs[:count], refs[count:]
    total = own_ref[...].astype(F32) + sum(p[...].astype(F32) for p in pieces)
    result = total.astype(BF16)
    result_ref[...] = result
    routed_ref[...] = dot(order_ref[...], result).astype(BF16)


def finish_result(order, residual, pieces):
    shape = jax.ShapeDtypeStruct(residual.shape, BF16)
    return pl.pallas_call(
        functools.partial(result_kernel, len(pieces)),
        in_specs=[VMEM] * (2 + len(pieces)),
        out_specs=(VMEM, VMEM),
        out_shape=(shape, shape),
        name="finish_result",
    )(order, residual, *pieces)


def bytes_kernel(count, result_ref, proj_ref, *refs):
    pieces, out_ref = refs[:count], refs[count]
    state = sum(p[...].astype(F32) for p in pieces).astype(BF16).astype(F32)
    rows = result_ref.shape[0]
    width = proj_ref.shape[0]
    own = state.shape[0] // rows
    mixed = [
        (state[b * rows : (b + 1) * rows] + dot(result_ref[:, b * width : (b + 1) * width], proj_ref[...])).astype(BF16)
        for b in range(own)
    ]
    at = lax.broadcasted_iota(jnp.int32, (rows * own, rows * own), 0)
    to = lax.broadcasted_iota(jnp.int32, (rows * own, rows * own), 1)
    order = (to == (at % own) * rows + at // own).astype(F32).astype(BF16)
    out_ref[...] = dot(order, jnp.concatenate(mixed, axis=0)).astype(BF16)


def finish_bytes(result, proj, pieces):
    return pl.pallas_call(
        functools.partial(bytes_kernel, len(pieces)),
        in_specs=[VMEM] * (2 + len(pieces)),
        out_specs=VMEM,
        out_shape=jax.ShapeDtypeStruct(pieces[0].shape, BF16),
        compiler_params=pltpu.CompilerParams(vmem_limit_bytes=32 * 2**20),
        name="finish_bytes",
    )(result, proj, *pieces)


def shift(value, axis, step):
    count = lax.axis_size(axis)
    return lax.ppermute(value, axis, [(i, (i + step) % count) for i in range(count)])


def scatter(chunks, axis):
    count = lax.axis_size(axis)
    me = lax.axis_index(axis)
    take = lambda step: lax.dynamic_index_in_dim(chunks, (me + step) % count, 0, keepdims=False)
    return [take(0)] + [shift(take(step), axis, step) for step in range(1, count)]


def gather(value, axis):
    return [value] + [shift(value, axis, step) for step in range(1, lax.axis_size(axis))]


def gather_chips(value, axis):
    count = lax.axis_size(axis)
    other = [(i, i ^ 1) for i in range(count)]
    pieces = [value] + [shift(value, axis, 2 * step) for step in range(1, count // 2)]
    return pieces + [lax.ppermute(p, axis, other) for p in pieces]


def chip_ids(axis):
    count = lax.axis_size(axis)
    me = lax.axis_index(axis)
    mine = (me - 2 * jnp.arange(count // 2, dtype=jnp.int32)) % count
    return jnp.concatenate([mine, mine ^ 1]).astype(jnp.int32)


def owner_order(owners, source, patches):
    listed = lax.dynamic_index_in_dim(owners, source, 0, keepdims=False)
    count = listed.shape[0]
    block = patches // count
    index = jnp.arange(count, dtype=jnp.int32)
    before = (listed[None, :] < listed[:, None]) | (
        (listed[None, :] == listed[:, None]) & (index[None, :] < index[:, None])
    )
    slot = jnp.sum(before, axis=1).astype(jnp.int32)
    row = jnp.arange(patches, dtype=jnp.int32)
    place = jnp.repeat(slot, block, total_repeat_length=patches) * block + row % block
    return (row[:, None] == place[None, :]).astype(BF16)


def on_device(
    byte_in,
    local_gain,
    local_qkv,
    local_out,
    mlp_up,
    mlp_down,
    local_scale,
    patch_proj,
    global_gain,
    global_qkv,
    global_out,
    global_scale,
    back_proj,
    owners,
):
    patches, span, width = byte_in.shape
    ways = lax.axis_size("head")
    own = span // ways
    me = lax.axis_index("head").astype(jnp.int32)
    seq = lax.axis_index("seq").astype(jnp.int32)
    depth = global_qkv.shape[2] // global_scale.shape[0]
    group = min(32, patches)

    part, share = local_part(
        me.reshape(1),
        local_scale,
        byte_in.reshape(-1, width),
        local_gain.reshape(1, -1),
        jnp.transpose(local_qkv, (1, 0, 2)),
        local_out,
        mlp_up,
        mlp_down,
        patch_proj,
        span,
        ways,
        group,
    )
    pieces = scatter(share, "head")
    residual = sum(p.astype(F32) for p in pieces).astype(BF16)
    shares = gather(residual, "head")
    ids = (me - jnp.arange(ways, dtype=jnp.int32)) % ways
    gain = global_gain.reshape(ways, 1, -1)
    qkv = jnp.transpose(global_qkv, (1, 0, 2))
    key, value = global_heads((1, 2), depth, ids, gain, shares, qkv)
    part, key, value = lax.optimization_barrier((part, key, value))
    (query,) = global_heads((0,), depth, ids, gain, shares, qkv)
    keys = gather_chips(key, "seq")
    values = gather_chips(value, "seq")
    bytes_pieces = scatter(part.reshape(ways, own * patches, width), "head")
    update = attend(chip_ids("seq"), global_scale, query, keys, values, global_out, ways)
    result, routed = finish_result(owner_order(owners, seq, patches), residual, scatter(update, "head"))
    global_state = lax.all_to_all(routed, "seq", split_axis=0, concat_axis=0, tiled=True)
    byte_out = finish_bytes(result, back_proj, bytes_pieces)
    return byte_out.reshape(patches, own, width), global_state


def solution(mesh):
    placed = (
        P("seq", None, None),
        P(),
        P(None, None, "head"),
        P("head", None),
        P(None, "head"),
        P("head", None),
        P("head"),
        P(),
        P(),
        P(None, None, "head"),
        P("head", None),
        P("head"),
        P(),
        P(),
    )
    return jax.shard_map(
        on_device,
        mesh=mesh,
        in_specs=placed,
        out_specs=(P("seq", "head", None), P("seq", "head")),
        check_vma=False,
    )
```

```python
import functools
import math

import jax
import jax.numpy as jnp
from jax import lax
from jax.experimental import pallas as pl
from jax.experimental.pallas import tpu as pltpu
from jax.sharding import PartitionSpec as P

EPSILON = 1e-06
NEGATIVE = -1e30
F32 = jnp.float32
BF16 = jnp.bfloat16
VMEM = pl.BlockSpec(memory_space=pltpu.VMEM)
HBM = pl.BlockSpec(memory_space=pltpu.HBM)
SMEM = pl.BlockSpec(memory_space=pltpu.SMEM)


def dot(left, right):
    return jnp.dot(left, right, preferred_element_type=F32)


def dot_t(left, right):
    return lax.dot_general(left, right, (((1,), (1,)), ((), ())), preferred_element_type=F32)


def unit(values):
    return (values * lax.rsqrt(jnp.mean(values * values, axis=-1, keepdims=True) + EPSILON)).astype(BF16)


def gelu(values):
    inner = math.sqrt(2.0 / math.pi) * (values + 0.044715 * (values * values * values))
    return 0.5 * values * (1.0 + jnp.tanh(inner))


def local_kernel(span, own, me_ref, scale_ref, x_ref, gain_ref, *refs):
    sources, (part_ref, share_ref), held, sems = refs[:5], refs[5:7], refs[7:12], refs[12]
    copies = [pltpu.make_async_copy(s, h, sems.at[i]) for i, (s, h) in enumerate(zip(sources, held))]
    first = pl.program_id(0) == 0

    @pl.when(first)
    def _():
        for copy in copies:
            copy.start()

    def arrived(i):
        @pl.when(first)
        def _():
            copies[i].wait()

        return held[i]

    rows = x_ref.shape[0]
    group = rows // span
    at = lax.broadcasted_iota(jnp.int32, (rows, rows), 0)
    to = lax.broadcasted_iota(jnp.int32, (rows, rows), 1)
    order = (to == (at % group) * span + at // group).astype(F32).astype(BF16)
    x = dot(order, x_ref[...])
    normed = (
        x * lax.rsqrt(jnp.mean(x * x, axis=-1, keepdims=True) + EPSILON) * gain_ref[...]
    ).astype(BF16)
    qkv_ref = arrived(0)
    query, key, value = (dot(normed, qkv_ref[i]) for i in range(3))
    seen = (at % group == to % group) & (to <= at)
    heads = scale_ref.shape[0]
    depth = query.shape[1] // heads
    attended = []
    for h in range(heads):
        cut = slice(h * depth, (h + 1) * depth)
        scores = dot_t(unit(query[:, cut]), unit(key[:, cut])) * (scale_ref[h] / math.sqrt(depth))
        scores = jnp.where(seen, scores, NEGATIVE)
        weights = jnp.exp(scores - jnp.max(scores, axis=-1, keepdims=True))
        total = jnp.sum(weights, axis=-1, keepdims=True)
        attended.append((dot(weights.astype(BF16), value[:, cut].astype(BF16)) / total).astype(BF16))
    act = gelu(dot(normed, arrived(1)[...])).astype(BF16)
    partial = dot(jnp.concatenate(attended, axis=1), arrived(2)[...]) + dot(act, arrived(3)[...])
    byte = lax.broadcasted_iota(jnp.int32, (rows, 1), 0) // group
    partial = (partial + jnp.where(byte // own == me_ref[0], x, 0.0)).astype(BF16)
    part_ref[...] = partial.reshape(part_ref.shape)
    share = dot(partial, arrived(4)[...]).astype(BF16)
    width = share.shape[1]
    for b in range(span):
        share_ref[b // own, :, (b % own) * width : (b % own + 1) * width] = share[b * group : (b + 1) * group]


def local_part(me, scale, x, gain, qkv, out, up, down, proj, span, ways, group):
    rows, width = x.shape
    patches = rows // span
    own = span // ways
    weights = (qkv, up, out, down, proj)
    return pl.pallas_call(
        functools.partial(local_kernel, span, own),
        grid=(patches // group,),
        in_specs=[SMEM, SMEM, pl.BlockSpec((group * span, width), lambda i: (i, 0))]
        + [pl.BlockSpec(gain.shape, lambda i: (0, 0))]
        + [HBM] * len(weights),
        out_specs=(
            pl.BlockSpec((span, group, width), lambda i: (0, i, 0)),
            pl.BlockSpec((ways, group, own * proj.shape[1]), lambda i: (0, i, 0)),
        ),
        out_shape=(
            jax.ShapeDtypeStruct((span, patches, width), BF16),
            jax.ShapeDtypeStruct((ways, patches, own * proj.shape[1]), BF16),
        ),
        scratch_shapes=[pltpu.VMEM(w.shape, w.dtype) for w in weights] + [pltpu.SemaphoreType.DMA((len(weights),))],
        compiler_params=pltpu.CompilerParams(vmem_limit_bytes=36 * 2**20),
        name="local_part",
    )(me, scale, x, gain, *weights)


def heads_kernel(kinds, depth, ids_ref, gain_ref, *refs):
    ways = gain_ref.shape[0]
    shares, weights, out = refs[:ways], refs[ways : ways + len(kinds)], refs[-1]
    width = shares[0].shape[1]
    values = [s[...].astype(F32) for s in shares]
    square = sum(jnp.sum(v * v, axis=-1, keepdims=True) for v in values)
    factor = lax.rsqrt(square / (ways * width) + EPSILON)
    normed = [(v * factor * gain_ref[ids_ref[c]]).astype(BF16) for c, v in enumerate(values)]
    for i, (kind, weight) in enumerate(zip(kinds, weights)):
        mixed = sum(
            dot(n, weight[0, pl.ds(pl.multiple_of(ids_ref[c] * width, width), width), :]) for c, n in enumerate(normed)
        )
        size = mixed.shape[1]
        if kind < 2:
            mixed = jnp.concatenate([unit(mixed[:, c : c + depth]) for c in range(0, size, depth)], axis=1)
        out[:, i * size : (i + 1) * size] = mixed.astype(BF16)


def global_heads(kinds, depth, ids, gain, shares, qkv):
    shape = jax.ShapeDtypeStruct((shares[0].shape[0], len(kinds) * qkv.shape[2]), BF16)
    pick = lambda kind: pl.BlockSpec((1,) + qkv.shape[1:], lambda i: (kind, 0, 0), pipeline_mode=pl.Buffered(1))
    whole = lambda a: pl.BlockSpec(a.shape, lambda i: (0,) * a.ndim)
    return pl.pallas_call(
        functools.partial(heads_kernel, kinds, depth),
        grid=(1,),
        in_specs=[SMEM, whole(gain)] + [whole(s) for s in shares] + [pick(kind) for kind in kinds],
        out_specs=whole(shape),
        out_shape=shape,
        compiler_params=pltpu.CompilerParams(vmem_limit_bytes=16 * 2**20),
        name="global_heads",
    )(ids, gain, *shares, *([qkv] * len(kinds)))


def attend_kernel(count, ids_ref, scale_ref, q_ref, *refs):
    pieces, (proj_ref, out_ref) = refs[:count], refs[count:]
    rows, size = q_ref.shape
    at = lax.broadcasted_iota(jnp.int32, (rows, rows), 0)
    to = lax.broadcasted_iota(jnp.int32, (rows, rows), 1)
    heads = scale_ref.shape[0]
    depth = size // heads
    me = ids_ref[0]
    seen = [to + ids_ref[i] * rows <= at + me * rows for i in range(count)]
    attended = []
    for h in range(heads):
        cut = slice(h * depth, (h + 1) * depth)
        query = q_ref[:, cut]
        factor = scale_ref[h] / math.sqrt(depth)
        scores = [jnp.where(s, dot_t(query, p[:, cut]) * factor, NEGATIVE) for s, p in zip(seen, pieces)]
        top = functools.reduce(jnp.maximum, [jnp.max(s, axis=-1, keepdims=True) for s in scores])
        weights = [jnp.exp(s - top) for s in scores]
        total = sum(jnp.sum(w, axis=-1, keepdims=True) for w in weights)
        cut = slice(size + h * depth, size + (h + 1) * depth)
        summed = sum(dot(w.astype(BF16), p[:, cut]) for w, p in zip(weights, pieces))
        attended.append((summed / total).astype(BF16))
    update = dot(jnp.concatenate(attended, axis=1), proj_ref[...]).astype(BF16)
    width = out_ref.shape[2]
    for c in range(out_ref.shape[0]):
        out_ref[c] = update[:, c * width : (c + 1) * width]


def attend(ids, scale, query, pieces, proj, ways):
    rows = query.shape[0]
    return pl.pallas_call(
        functools.partial(attend_kernel, len(pieces)),
        in_specs=[SMEM, SMEM] + [VMEM] * (2 + len(pieces)),
        out_specs=VMEM,
        out_shape=jax.ShapeDtypeStruct((ways, rows, proj.shape[1] // ways), BF16),
        compiler_params=pltpu.CompilerParams(vmem_limit_bytes=40 * 2**20),
        name="attend",
    )(ids, scale, query, *pieces, proj)


def result_kernel(count, order_ref, own_ref, *refs):
    pieces, (result_ref, routed_ref) = refs[:count], refs[count:]
    total = own_ref[...].astype(F32) + sum(p[...].astype(F32) for p in pieces)
    result = total.astype(BF16)
    result_ref[...] = result
    routed_ref[...] = dot(order_ref[...], result).astype(BF16)


def finish_result(order, residual, pieces):
    shape = jax.ShapeDtypeStruct(residual.shape, BF16)
    return pl.pallas_call(
        functools.partial(result_kernel, len(pieces)),
        in_specs=[VMEM] * (2 + len(pieces)),
        out_specs=(VMEM, VMEM),
        out_shape=(shape, shape),
        name="finish_result",
    )(order, residual, *pieces)


def bytes_kernel(count, kept_ref, result_ref, proj_ref, *refs):
    pieces, out_ref = refs[:count], refs[count]
    state = pieces[0][...].astype(F32)
    for i, p in enumerate(pieces[1:], 1):
        state += jnp.where(kept_ref[i] != 0, p[...].astype(F32), 0.0)
    state = state.astype(BF16).astype(F32)
    rows = result_ref.shape[0]
    width = proj_ref.shape[0]
    own = state.shape[0] // rows
    mixed = [
        (state[b * rows : (b + 1) * rows] + dot(result_ref[:, b * width : (b + 1) * width], proj_ref[...])).astype(BF16)
        for b in range(own)
    ]
    at = lax.broadcasted_iota(jnp.int32, (rows * own, rows * own), 0)
    to = lax.broadcasted_iota(jnp.int32, (rows * own, rows * own), 1)
    order = (to == (at % own) * rows + at // own).astype(F32).astype(BF16)
    out_ref[...] = dot(order, jnp.concatenate(mixed, axis=0)).astype(BF16)


def finish_bytes(kept, result, proj, pieces):
    return pl.pallas_call(
        functools.partial(bytes_kernel, len(pieces)),
        in_specs=[SMEM] + [VMEM] * (2 + len(pieces)),
        out_specs=VMEM,
        out_shape=jax.ShapeDtypeStruct(pieces[0].shape, BF16),
        compiler_params=pltpu.CompilerParams(vmem_limit_bytes=32 * 2**20),
        name="finish_bytes",
    )(kept, result, proj, *pieces)


def shift(value, axis, step):
    count = lax.axis_size(axis)
    return lax.ppermute(value, axis, [(i, (i + step) % count) for i in range(count)])


def scatter(chunks, axis):
    count = lax.axis_size(axis)
    me = lax.axis_index(axis)
    take = lambda step: lax.dynamic_index_in_dim(chunks, (me + step) % count, 0, keepdims=False)
    return [take(0)] + [shift(take(step), axis, step) for step in range(1, count)]


class Relay:
    def __init__(self, chunks, axis):
        self.chunks, self.axis = chunks, axis
        self.me = me = lax.axis_index(axis)
        self.outer = (me == 0) | (me == 3)
        take = self.take
        self.own = take(me)
        far = jnp.where(self.outer, 3 - me, me ^ 1)
        self.swapped = lax.ppermute(take(far), axis, [(0, 1), (1, 0), (2, 3), (3, 2)])
        self.middle = lax.ppermute(take(jnp.where(self.outer, me, 3 - me)), axis, [(1, 2), (2, 1)])

    def take(self, index):
        return lax.dynamic_index_in_dim(self.chunks, index, 0, keepdims=False)

    def rest(self):
        me, outer = self.me, self.outer
        inward = lax.ppermute(self.take(me ^ 1), self.axis, [(0, 1), (3, 2)])
        sent = self.take(me ^ 2).astype(F32) + jnp.where(outer, 0.0, self.swapped.astype(F32))
        crossed = lax.ppermute(sent.astype(BF16), self.axis, [(0, 2), (2, 0), (1, 3), (3, 1)])
        return [self.own, self.swapped, self.middle, inward, crossed]


def gather(value, axis):
    return [value] + [shift(value, axis, step) for step in range(1, lax.axis_size(axis))]


def gather_chips(value, axis):
    count = lax.axis_size(axis)
    other = [(i, i ^ 1) for i in range(count)]
    pieces = [value] + [shift(value, axis, 2 * step) for step in range(1, count // 2)]
    return pieces + [lax.ppermute(p, axis, other) for p in pieces]


def chip_ids(axis):
    count = lax.axis_size(axis)
    me = lax.axis_index(axis)
    mine = (me - 2 * jnp.arange(count // 2, dtype=jnp.int32)) % count
    return jnp.concatenate([mine, mine ^ 1]).astype(jnp.int32)


def owner_order(owners, source, patches):
    listed = lax.dynamic_index_in_dim(owners, source, 0, keepdims=False)
    count = listed.shape[0]
    block = patches // count
    index = jnp.arange(count, dtype=jnp.int32)
    before = (listed[None, :] < listed[:, None]) | (
        (listed[None, :] == listed[:, None]) & (index[None, :] < index[:, None])
    )
    slot = jnp.sum(before, axis=1).astype(jnp.int32)
    row = jnp.arange(patches, dtype=jnp.int32)
    spread = jnp.sum(jnp.where(row[:, None] // block == index[None, :], slot[None, :], 0), axis=1).astype(jnp.int32)
    place = spread * block + row % block
    return (row[:, None] == place[None, :]).astype(BF16)


def on_device(
    byte_in,
    local_gain,
    local_qkv,
    local_out,
    mlp_up,
    mlp_down,
    local_scale,
    patch_proj,
    global_gain,
    global_qkv,
    global_out,
    global_scale,
    back_proj,
    owners,
):
    patches, span, width = byte_in.shape
    ways = lax.axis_size("head")
    own = span // ways
    me = lax.axis_index("head").astype(jnp.int32)
    seq = lax.axis_index("seq").astype(jnp.int32)
    depth = global_qkv.shape[2] // global_scale.shape[0]
    group = min(32, patches)

    part, share = local_part(
        me.reshape(1),
        local_scale,
        byte_in.reshape(-1, width),
        local_gain.reshape(1, -1),
        jnp.transpose(local_qkv, (1, 0, 2)),
        local_out,
        mlp_up,
        mlp_down,
        patch_proj,
        span,
        ways,
        group,
    )
    pieces = scatter(share, "head")
    residual = sum(p.astype(F32) for p in pieces).astype(BF16)
    shares = gather(residual, "head")
    ids = (me - jnp.arange(ways, dtype=jnp.int32)) % ways
    gain = global_gain.reshape(ways, 1, -1)
    qkv = jnp.transpose(global_qkv, (1, 0, 2))
    keyed = global_heads((1, 2), depth, ids, gain, shares, qkv)
    part, keyed = lax.optimization_barrier((part, keyed))
    chunks = part.reshape(ways, own * patches, width)
    if ways == 4:
        relay = Relay(chunks, "head")
        relay.swapped, shares = lax.optimization_barrier((relay.swapped, shares))
        outer = relay.outer.astype(jnp.int32)
        kept = jnp.stack([1 + 0 * outer, outer, 1 - outer, 1 - outer, 1 + 0 * outer])
    query = global_heads((0,), depth, ids, gain, shares, qkv)
    update = attend(chip_ids("seq"), global_scale, query, gather_chips(keyed, "seq"), global_out, ways)
    if ways == 4:
        bytes_pieces = relay.rest()
    else:
        bytes_pieces = scatter(chunks, "head")
        kept = jnp.ones((ways,), jnp.int32)
    result, routed = finish_result(owner_order(owners, seq, patches), residual, scatter(update, "head"))
    global_state = lax.all_to_all(routed, "seq", split_axis=0, concat_axis=0, tiled=True)
    byte_out = finish_bytes(kept, result, back_proj, bytes_pieces)
    return byte_out.reshape(patches, own, width), global_state


def solution(mesh):
    placed = (
        P("seq", None, None),
        P(),
        P(None, None, "head"),
        P("head", None),
        P(None, "head"),
        P("head", None),
        P("head"),
        P(),
        P(),
        P(None, None, "head"),
        P("head", None),
        P("head"),
        P(),
        P(),
    )
    return jax.shard_map(
        on_device,
        mesh=mesh,
        in_specs=placed,
        out_specs=(P("seq", "head", None), P("seq", "head")),
        check_vma=False,
    )
```

```python
import functools
import math

import jax
import jax.numpy as jnp
from jax import lax
from jax.experimental import pallas as pl
from jax.experimental.pallas import tpu as pltpu
from jax.sharding import PartitionSpec as P

EPSILON = 1e-06
NEGATIVE = -1e30
F32 = jnp.float32
BF16 = jnp.bfloat16
VMEM = pl.BlockSpec(memory_space=pltpu.VMEM)
HBM = pl.BlockSpec(memory_space=pltpu.HBM)
SMEM = pl.BlockSpec(memory_space=pltpu.SMEM)


def dot(left, right):
    return jnp.dot(left, right, preferred_element_type=F32)


def dot_t(left, right):
    return lax.dot_general(left, right, (((1,), (1,)), ((), ())), preferred_element_type=F32)


def unit(values):
    return (values * lax.rsqrt(jnp.mean(values * values, axis=-1, keepdims=True) + EPSILON)).astype(BF16)


def gelu(values):
    inner = math.sqrt(2.0 / math.pi) * (values + 0.044715 * (values * values * values))
    return 0.5 * values * (1.0 + jnp.tanh(inner))


def local_kernel(span, piece, step, me_ref, scale_ref, slots_ref, gain_ref, x_hbm, *refs):
    ways = slots_ref.shape[1]
    sources, parts, shares = refs[:5], refs[5 : 5 + ways], refs[5 + ways : 5 + 2 * ways]
    x_ref, part_ref, share_ref = refs[5 + 2 * ways : 8 + 2 * ways]
    held, (in_sem, x_sem, part_sem, share_sem) = refs[8 + 2 * ways : 13 + 2 * ways], refs[13 + 2 * ways :]
    patches = share_ref.shape[1]
    width = x_ref.shape[1]
    own = span // ways
    rows = piece * span
    pieces = patches // piece
    loads = [pltpu.make_async_copy(s, h, in_sem.at[i]) for i, (s, h) in enumerate(zip(sources, held))]
    cuts = [slice(i * rows, (i + 1) * rows) for i in range(pieces)]
    x_loads = [pltpu.make_async_copy(x_hbm.at[pl.ds(c.start, rows)], x_ref.at[pl.ds(c.start, rows)], x_sem.at[i]) for i, c in enumerate(cuts)]
    x_loads[0].start()
    loads[0].start()
    for copy in x_loads[1:] + loads[1:]:
        copy.start()
    qkv_ref, up_ref, out_ref, down_ref, proj_ref = held
    at = lax.broadcasted_iota(jnp.int32, (rows, rows), 0)
    to = lax.broadcasted_iota(jnp.int32, (rows, rows), 1)
    order = (to == (at % piece) * span + at // piece).astype(F32).astype(BF16)
    kept = lax.broadcasted_iota(jnp.int32, (rows, 1), 0) // piece // own == me_ref[0]
    xs, normed = [], []
    for i, cut in enumerate(cuts):
        x_loads[i].wait()
        x = dot(order, x_ref[cut])
        xs.append(jnp.where(kept, x, 0.0).astype(BF16))
        factor = lax.rsqrt(jnp.mean(x * x, axis=-1, keepdims=True) + EPSILON)
        normed.append((x * factor * gain_ref[...]).astype(BF16))
    xs, normed = jnp.concatenate(xs, axis=0), jnp.concatenate(normed, axis=0)
    loads[0].wait()
    query, key, value = (dot(normed, qkv_ref[i]) for i in range(3))
    seen = (at % piece == to % piece) & (to <= at)
    heads = scale_ref.shape[0]
    depth = query.shape[1] // heads
    attended = []
    for cut in cuts:
        columns = []
        for h in range(heads):
            head = slice(h * depth, (h + 1) * depth)
            scores = dot_t(unit(query[cut, head]), unit(key[cut, head])) * (scale_ref[h] / math.sqrt(depth))
            scores = jnp.where(seen, scores, NEGATIVE)
            weights = jnp.exp(scores - jnp.max(scores, axis=-1, keepdims=True))
            total = jnp.sum(weights, axis=-1, keepdims=True)
            columns.append((dot(weights.astype(BF16), value[cut, head].astype(BF16)) / total).astype(BF16))
        attended.append(jnp.concatenate(columns, axis=1))
    attended = jnp.concatenate(attended, axis=0)
    loads[1].wait()
    act = gelu(dot(normed, up_ref[...])).astype(BF16)
    for copy in loads[2:]:
        copy.wait()
    share = 0.0
    stores = []
    for c in range(0, width, step):
        columns = slice(c, c + step)
        partial = dot(attended, out_ref[:, columns]) + dot(act, down_ref[:, columns])
        partial = (partial + xs[:, columns].astype(F32)).astype(BF16)
        for i, cut in enumerate(cuts):
            for b in range(span):
                put = (b % own) * patches + i * piece
                part_ref[b // own, put : put + piece, columns] = partial[cut][b * piece : (b + 1) * piece]
        for slot, part in enumerate(parts):
            source = part_ref.at[slots_ref[0, slot], :, pl.ds(c, step)]
            stores.append(pltpu.make_async_copy(source, part.at[:, pl.ds(c, step)], part_sem.at[len(stores)]))
            stores[-1].start()
        share += dot(partial, proj_ref[columns])
    share = share.astype(BF16)
    size = share.shape[1]
    for i, cut in enumerate(cuts):
        for b in range(span):
            put = slice((b % own) * size, (b % own + 1) * size)
            share_ref[b // own, i * piece : (i + 1) * piece, put] = share[cut][b * piece : (b + 1) * piece]
    for slot, out in enumerate(shares):
        stores.append(pltpu.make_async_copy(share_ref.at[slots_ref[1, slot]], out, share_sem.at[slot]))
        stores[-1].start()
    for copy in stores:
        copy.wait()


def local_part(me, scale, slots, x, gain, qkv, out, up, down, proj, span):
    rows, width = x.shape
    patches = rows // span
    ways = slots.shape[1]
    own = span // ways
    weights = (qkv, up, out, down, proj)
    piece = math.gcd(patches, 32)
    step = math.gcd(width, 256)
    part = (own * patches, width)
    share = (patches, own * proj.shape[1])
    outs = pl.pallas_call(
        functools.partial(local_kernel, span, piece, step),
        in_specs=[SMEM, SMEM, SMEM, VMEM] + [HBM] * (1 + len(weights)),
        out_specs=[HBM] * (2 * ways),
        out_shape=[jax.ShapeDtypeStruct(part, BF16)] * ways + [jax.ShapeDtypeStruct(share, BF16)] * ways,
        scratch_shapes=[pltpu.VMEM(x.shape, BF16), pltpu.VMEM((ways, *part), BF16), pltpu.VMEM((ways, *share), BF16)]
        + [pltpu.VMEM(w.shape, w.dtype) for w in weights]
        + [
            pltpu.SemaphoreType.DMA((len(weights),)),
            pltpu.SemaphoreType.DMA((patches // piece,)),
            pltpu.SemaphoreType.DMA((ways * (width // step),)),
            pltpu.SemaphoreType.DMA((ways,)),
        ],
        compiler_params=pltpu.CompilerParams(vmem_limit_bytes=60 * 2**20),
        name="local_part",
    )(me, scale, slots, gain, x, *weights)
    return outs[:ways], outs[ways:]


def fetch_kernel(source, held, sems):
    parts = source.shape[0]
    copies = [pltpu.make_async_copy(source.at[i], held.at[i], sems.at[i]) for i in range(parts)]
    for copy in copies:
        copy.start()
    for copy in copies:
        copy.wait()


def fetch(weight):
    return pl.pallas_call(
        fetch_kernel,
        in_specs=[HBM],
        out_specs=VMEM,
        out_shape=pltpu.VMEM(weight.shape, weight.dtype),
        scratch_shapes=[pltpu.SemaphoreType.DMA((weight.shape[0],))],
        compiler_params=pltpu.CompilerParams(vmem_limit_bytes=50 * 2**20),
        name="fetch",
    )(weight)


def heads_kernel(depth, ids_ref, gain_ref, *refs):
    ways = gain_ref.shape[0]
    shares, (weight, query_ref, keyed_ref) = refs[:ways], refs[ways:]
    width = shares[0].shape[1]
    values = [s[...].astype(F32) for s in shares]
    square = sum(jnp.sum(v * v, axis=-1, keepdims=True) for v in values)
    factor = lax.rsqrt(square / (ways * width) + EPSILON)
    normed = [(v * factor * gain_ref[ids_ref[c]]).astype(BF16) for c, v in enumerate(values)]
    for kind in range(3):
        mixed = sum(
            dot(n, weight[kind, pl.ds(pl.multiple_of(ids_ref[c] * width, width), width), :])
            for c, n in enumerate(normed)
        )
        size = mixed.shape[1]
        if kind < 2:
            mixed = jnp.concatenate([unit(mixed[:, c : c + depth]) for c in range(0, size, depth)], axis=1)
        if kind == 0:
            query_ref[...] = mixed
        else:
            keyed_ref[:, (kind - 1) * size : kind * size] = mixed.astype(BF16)


def global_heads(depth, ids, gain, shares, qkv):
    rows, size = shares[0].shape[0], qkv.shape[2]
    return pl.pallas_call(
        functools.partial(heads_kernel, depth),
        in_specs=[SMEM] + [VMEM] * (2 + len(shares)),
        out_specs=(VMEM, VMEM),
        out_shape=(jax.ShapeDtypeStruct((rows, size), BF16), jax.ShapeDtypeStruct((rows, 2 * size), BF16)),
        compiler_params=pltpu.CompilerParams(vmem_limit_bytes=8 * 2**20),
        name="global_heads",
    )(ids, gain, *shares, qkv)


def attend_kernel(count, slots_ref, ids_ref, scale_ref, q_ref, *refs):
    pieces, proj_ref, outs = refs[:count], refs[count], refs[count + 1 :]
    rows, size = q_ref.shape
    at = lax.broadcasted_iota(jnp.int32, (rows, rows), 0)
    to = lax.broadcasted_iota(jnp.int32, (rows, rows), 1)
    heads = scale_ref.shape[0]
    depth = size // heads
    me = ids_ref[0]
    seen = [to + ids_ref[i] * rows <= at + me * rows for i in range(count)]
    attended = []
    for h in range(heads):
        cut = slice(h * depth, (h + 1) * depth)
        query = q_ref[:, cut]
        factor = scale_ref[h] / math.sqrt(depth)
        scores = [jnp.where(s, dot_t(query, p[:, cut]) * factor, NEGATIVE) for s, p in zip(seen, pieces)]
        top = functools.reduce(jnp.maximum, [jnp.max(s, axis=-1, keepdims=True) for s in scores])
        weights = [jnp.exp(s - top) for s in scores]
        total = sum(jnp.sum(w, axis=-1, keepdims=True) for w in weights)
        cut = slice(size + h * depth, size + (h + 1) * depth)
        summed = sum(dot(w.astype(BF16), p[:, cut]) for w, p in zip(weights, pieces))
        attended.append((summed / total).astype(BF16))
    attended = jnp.concatenate(attended, axis=1)
    for slot, out in enumerate(outs):
        width = out.shape[1]
        out[...] = dot(attended, proj_ref[:, pl.ds(pl.multiple_of(slots_ref[slot] * width, width), width)]).astype(BF16)


def attend(slots, ids, scale, query, pieces, proj):
    rows, ways = query.shape[0], slots.shape[0]
    return pl.pallas_call(
        functools.partial(attend_kernel, len(pieces)),
        in_specs=[SMEM, SMEM, SMEM] + [VMEM] * (2 + len(pieces)),
        out_specs=[VMEM] * ways,
        out_shape=[jax.ShapeDtypeStruct((rows, proj.shape[1] // ways), BF16)] * ways,
        compiler_params=pltpu.CompilerParams(vmem_limit_bytes=16 * 2**20),
        name="attend",
    )(slots, ids, scale, query, *pieces, proj)


def result_kernel(count, order_ref, own_ref, *refs):
    pieces, (result_ref, routed_ref) = refs[:count], refs[count:]
    total = own_ref[...].astype(F32) + sum(p[...].astype(F32) for p in pieces)
    result = total.astype(BF16)
    result_ref[...] = result
    routed_ref[...] = dot(order_ref[...], result).astype(BF16)


def finish_result(order, residual, pieces):
    shape = jax.ShapeDtypeStruct(residual.shape, BF16)
    return pl.pallas_call(
        functools.partial(result_kernel, len(pieces)),
        in_specs=[VMEM] * (2 + len(pieces)),
        out_specs=(VMEM, VMEM),
        out_shape=(shape, shape),
        compiler_params=pltpu.CompilerParams(vmem_limit_bytes=4 * 2**20),
        name="finish_result",
    )(order, residual, *pieces)


def bytes_kernel(count, kept_ref, result_ref, proj_ref, *refs):
    pieces, out_ref = refs[:count], refs[count]
    state = pieces[0][...].astype(F32)
    for i, p in enumerate(pieces[1:], 1):
        state += jnp.where(kept_ref[i] != 0, p[...].astype(F32), 0.0)
    state = state.astype(BF16).astype(F32)
    rows = result_ref.shape[0]
    width = proj_ref.shape[0]
    own = state.shape[0] // rows
    mixed = [
        (state[b * rows : (b + 1) * rows] + dot(result_ref[:, b * width : (b + 1) * width], proj_ref[...])).astype(BF16)
        for b in range(own)
    ]
    at = lax.broadcasted_iota(jnp.int32, (rows * own, rows * own), 0)
    to = lax.broadcasted_iota(jnp.int32, (rows * own, rows * own), 1)
    order = (to == (at % own) * rows + at // own).astype(F32).astype(BF16)
    out_ref[...] = dot(order, jnp.concatenate(mixed, axis=0)).astype(BF16)


def finish_bytes(kept, result, proj, pieces):
    return pl.pallas_call(
        functools.partial(bytes_kernel, len(pieces)),
        in_specs=[SMEM] + [VMEM] * (2 + len(pieces)),
        out_specs=VMEM,
        out_shape=jax.ShapeDtypeStruct(pieces[0].shape, BF16),
        compiler_params=pltpu.CompilerParams(vmem_limit_bytes=16 * 2**20),
        name="finish_bytes",
    )(kept, result, proj, *pieces)


def shift(value, axis, step):
    count = lax.axis_size(axis)
    return lax.ppermute(value, axis, [(i, (i + step) % count) for i in range(count)])


def scatter(chunks, axis):
    return [chunks[0]] + [shift(chunk, axis, step) for step, chunk in enumerate(chunks[1:], 1)]


def shift_slots(axis):
    count = lax.axis_size(axis)
    return ((lax.axis_index(axis) + jnp.arange(count)) % count).astype(jnp.int32)


def relay_slots(axis):
    me = lax.axis_index(axis)
    outer = (me == 0) | (me == 3)
    beside, across = me ^ 1, 3 - me
    return jnp.stack([me, jnp.where(outer, across, beside), jnp.where(outer, beside, across), me ^ 2]).astype(jnp.int32)


def relay_first(chunks, axis):
    swapped = lax.ppermute(chunks[1], axis, [(0, 1), (1, 0), (2, 3), (3, 2)])
    middle = lax.ppermute(chunks[2], axis, [(1, 2), (2, 1)])
    return swapped, middle


def relay_rest(chunks, swapped, middle, axis):
    me = lax.axis_index(axis)
    outer = (me == 0) | (me == 3)
    sent = (chunks[3].astype(F32) + jnp.where(outer, 0.0, swapped.astype(F32))).astype(BF16)
    inward = lax.ppermute(chunks[2], axis, [(0, 1), (3, 2)])
    crossed = lax.ppermute(sent, axis, [(0, 2), (2, 0), (1, 3), (3, 1)])
    outer = outer.astype(jnp.int32)
    return jnp.stack([1 + 0 * outer, outer, 1 - outer, 1 - outer, 1 + 0 * outer]), [chunks[0], swapped, middle, inward, crossed]


def gather(value, axis):
    return [value] + [shift(value, axis, step) for step in range(1, lax.axis_size(axis))]


def gather_chips(value, axis):
    count = lax.axis_size(axis)
    other = [(i, i ^ 1) for i in range(count)]
    pieces = [value] + [shift(value, axis, 2 * step) for step in range(1, count // 2)]
    return pieces + [lax.ppermute(p, axis, other) for p in pieces]


def chip_ids(axis):
    count = lax.axis_size(axis)
    me = lax.axis_index(axis)
    mine = (me - 2 * jnp.arange(count // 2, dtype=jnp.int32)) % count
    return jnp.concatenate([mine, mine ^ 1]).astype(jnp.int32)


def owner_order(owners, source, patches):
    listed = lax.dynamic_index_in_dim(owners, source, 0, keepdims=False)
    count = listed.shape[0]
    block = patches // count
    index = jnp.arange(count, dtype=jnp.int32)
    before = (listed[None, :] < listed[:, None]) | (
        (listed[None, :] == listed[:, None]) & (index[None, :] < index[:, None])
    )
    slot = jnp.sum(before, axis=1).astype(jnp.int32)
    row = jnp.arange(patches, dtype=jnp.int32)
    spread = jnp.sum(jnp.where(row[:, None] // block == index[None, :], slot[None, :], 0), axis=1).astype(jnp.int32)
    place = spread * block + row % block
    return (row[:, None] == place[None, :]).astype(BF16)


def on_device(
    byte_in,
    local_gain,
    local_qkv,
    local_out,
    mlp_up,
    mlp_down,
    local_scale,
    patch_proj,
    global_gain,
    global_qkv,
    global_out,
    global_scale,
    back_proj,
    owners,
):
    patches, span, width = byte_in.shape
    ways = lax.axis_size("head")
    own = span // ways
    me = lax.axis_index("head").astype(jnp.int32)
    seq = lax.axis_index("seq").astype(jnp.int32)
    depth = global_qkv.shape[2] // global_scale.shape[0]

    line = ways == 4
    slots = jnp.stack([relay_slots("head") if line else shift_slots("head"), shift_slots("head")])
    parts, chunks = local_part(
        me.reshape(1),
        local_scale,
        slots,
        byte_in.reshape(-1, width),
        local_gain.reshape(1, -1),
        jnp.transpose(local_qkv, (1, 0, 2)),
        local_out,
        mlp_up,
        mlp_down,
        patch_proj,
        span,
    )
    residual = sum(p.astype(F32) for p in scatter(chunks, "head")).astype(BF16)
    weight, residual = lax.optimization_barrier((jnp.transpose(global_qkv, (1, 0, 2)), residual))
    shares = gather(residual, "head")
    ids = (me - jnp.arange(ways, dtype=jnp.int32)) % ways
    query, keyed = global_heads(depth, ids, global_gain.reshape(ways, 1, -1), shares, fetch(weight))
    parts, keyed = lax.optimization_barrier((parts, keyed))
    if line:
        swapped, middle = relay_first(parts, "head")
        query, swapped, middle = lax.optimization_barrier((query, swapped, middle))
        kept, parts = relay_rest(parts, swapped, middle, "head")
    else:
        kept, parts = jnp.ones((ways,), jnp.int32), scatter(parts, "head")
    update = attend(slots[1], chip_ids("seq"), global_scale, query, gather_chips(keyed, "seq"), global_out)
    result, routed = finish_result(owner_order(owners, seq, patches), residual, scatter(update, "head"))
    global_state = lax.all_to_all(routed, "seq", split_axis=0, concat_axis=0, tiled=True)
    byte_out = finish_bytes(kept, result, back_proj, parts)
    return byte_out.reshape(patches, own, width), global_state


def solution(mesh):
    placed = (
        P("seq", None, None),
        P(),
        P(None, None, "head"),
        P("head", None),
        P(None, "head"),
        P("head", None),
        P("head"),
        P(),
        P(),
        P(None, None, "head"),
        P("head", None),
        P("head"),
        P(),
        P(),
    )
    return jax.shard_map(
        on_device,
        mesh=mesh,
        in_specs=placed,
        out_specs=(P("seq", "head", None), P("seq", "head")),
        check_vma=False,
    )
```

```python
import functools
import math

import jax
import jax.numpy as jnp
from jax import lax
from jax.experimental import pallas as pl
from jax.experimental.pallas import tpu as pltpu
from jax.sharding import PartitionSpec as P

EPSILON = 1e-06
NEGATIVE = -1e30
F32 = jnp.float32
BF16 = jnp.bfloat16
VMEM = pl.BlockSpec(memory_space=pltpu.VMEM)
HBM = pl.BlockSpec(memory_space=pltpu.HBM)
SMEM = pl.BlockSpec(memory_space=pltpu.SMEM)


def dot(left, right):
    return jnp.dot(left, right, preferred_element_type=F32)


def dot_t(left, right):
    return lax.dot_general(left, right, (((1,), (1,)), ((), ())), preferred_element_type=F32)


def unit(values):
    return (values * lax.rsqrt(jnp.mean(values * values, axis=-1, keepdims=True) + EPSILON)).astype(BF16)


def gelu(values):
    inner = math.sqrt(2.0 / math.pi) * (values + 0.044715 * (values * values * values))
    return 0.5 * values * (1.0 + jnp.tanh(inner))


def local_kernel(span, piece, step, me_ref, scale_ref, slots_ref, gain_ref, x_hbm, *refs):
    ways = slots_ref.shape[1]
    sources, parts, shares = refs[:5], refs[5 : 5 + ways], refs[5 + ways : 5 + 2 * ways]
    x_ref, part_ref, share_ref = refs[5 + 2 * ways : 8 + 2 * ways]
    held, (in_sem, x_sem, part_sem) = refs[8 + 2 * ways : 13 + 2 * ways], refs[13 + 2 * ways :]
    patches = share_ref.shape[1]
    width = x_ref.shape[1]
    own = span // ways
    rows = piece * span
    pieces = patches // piece
    loads = [pltpu.make_async_copy(s, h, in_sem.at[i]) for i, (s, h) in enumerate(zip(sources, held))]
    cuts = [slice(i * rows, (i + 1) * rows) for i in range(pieces)]
    x_loads = [pltpu.make_async_copy(x_hbm.at[pl.ds(c.start, rows)], x_ref.at[pl.ds(c.start, rows)], x_sem.at[i]) for i, c in enumerate(cuts)]
    for copy in x_loads + loads:
        copy.start()
    qkv_ref, up_ref, out_ref, down_ref, proj_ref = held
    at = lax.broadcasted_iota(jnp.int32, (rows, rows), 0)
    to = lax.broadcasted_iota(jnp.int32, (rows, rows), 1)
    order = (to == (at % piece) * span + at // piece).astype(F32).astype(BF16)
    kept = lax.broadcasted_iota(jnp.int32, (rows, 1), 0) // piece // own == me_ref[0]
    xs, normed = [], []
    for copy in x_loads + loads:
        copy.wait()
    for i, cut in enumerate(cuts):
        x = dot(order, x_ref[cut])
        xs.append(jnp.where(kept, x, 0.0).astype(BF16))
        factor = lax.rsqrt(jnp.mean(x * x, axis=-1, keepdims=True) + EPSILON)
        normed.append((x * factor * gain_ref[...]).astype(BF16))
    xs, normed = jnp.concatenate(xs, axis=0), jnp.concatenate(normed, axis=0)
    query, key, value = (dot(normed, qkv_ref[i]) for i in range(3))
    seen = (at % piece == to % piece) & (to <= at)
    heads = scale_ref.shape[0]
    depth = query.shape[1] // heads
    attended = []
    for cut in cuts:
        columns = []
        for h in range(heads):
            head = slice(h * depth, (h + 1) * depth)
            scores = dot_t(unit(query[cut, head]), unit(key[cut, head])) * (scale_ref[h] / math.sqrt(depth))
            scores = jnp.where(seen, scores, NEGATIVE)
            weights = jnp.exp(scores - jnp.max(scores, axis=-1, keepdims=True))
            total = jnp.sum(weights, axis=-1, keepdims=True)
            columns.append((dot(weights.astype(BF16), value[cut, head].astype(BF16)) / total).astype(BF16))
        attended.append(jnp.concatenate(columns, axis=1))
    attended = jnp.concatenate(attended, axis=0)
    act = gelu(dot(normed, up_ref[...])).astype(BF16)
    mixed = jnp.concatenate([attended, act], axis=1)
    share = 0.0
    stores = []
    for c in range(0, width, step):
        columns = slice(c, c + step)
        partial = dot(mixed, jnp.concatenate([out_ref[:, columns], down_ref[:, columns]], axis=0))
        partial = (partial + xs[:, columns].astype(F32)).astype(BF16)
        for i, cut in enumerate(cuts):
            for b in range(span):
                put = (b % own) * patches + i * piece
                part_ref[b // own, put : put + piece, columns] = partial[cut][b * piece : (b + 1) * piece]
        for slot, part in enumerate(parts):
            source = part_ref.at[slots_ref[0, slot], :, pl.ds(c, step)]
            stores.append(pltpu.make_async_copy(source, part.at[:, pl.ds(c, step)], part_sem.at[len(stores)]))
            stores[-1].start()
        share += dot(partial, proj_ref[columns])
    share = share.astype(BF16)
    size = share.shape[1]
    for i, cut in enumerate(cuts):
        for b in range(span):
            put = slice((b % own) * size, (b % own + 1) * size)
            share_ref[b // own, i * piece : (i + 1) * piece, put] = share[cut][b * piece : (b + 1) * piece]
    for slot, out in enumerate(shares):
        out[...] = share_ref[slots_ref[1, slot]]
    for copy in stores:
        copy.wait()


def local_part(me, scale, slots, x, gain, qkv, out, up, down, proj, span):
    rows, width = x.shape
    patches = rows // span
    ways = slots.shape[1]
    own = span // ways
    weights = (qkv, up, out, down, proj)
    piece = math.gcd(patches, 32)
    step = math.gcd(width, 1024)
    part = (own * patches, width)
    share = (patches, own * proj.shape[1])
    outs = pl.pallas_call(
        functools.partial(local_kernel, span, piece, step),
        in_specs=[SMEM, SMEM, SMEM, VMEM] + [HBM] * (1 + len(weights)),
        out_specs=[HBM] * ways + [VMEM] * ways,
        out_shape=[jax.ShapeDtypeStruct(part, BF16)] * ways + [pltpu.VMEM(share, BF16)] * ways,
        scratch_shapes=[pltpu.VMEM(x.shape, BF16), pltpu.VMEM((ways, *part), BF16), pltpu.VMEM((ways, *share), BF16)]
        + [pltpu.VMEM(w.shape, w.dtype) for w in weights]
        + [
            pltpu.SemaphoreType.DMA((len(weights),)),
            pltpu.SemaphoreType.DMA((patches // piece,)),
            pltpu.SemaphoreType.DMA((ways * (width // step),)),
        ],
        compiler_params=pltpu.CompilerParams(vmem_limit_bytes=60 * 2**20),
        name="local_part",
    )(me, scale, slots, gain, x, *weights)
    return outs[:ways], outs[ways:]


def fetch_kernel(source, held, sems):
    parts = source.shape[0]
    copies = [pltpu.make_async_copy(source.at[i], held.at[i], sems.at[i]) for i in range(parts)]
    for copy in copies:
        copy.start()
    for copy in copies:
        copy.wait()


def fetch(weight):
    return pl.pallas_call(
        fetch_kernel,
        in_specs=[HBM],
        out_specs=VMEM,
        out_shape=pltpu.VMEM(weight.shape, weight.dtype),
        scratch_shapes=[pltpu.SemaphoreType.DMA((weight.shape[0],))],
        compiler_params=pltpu.CompilerParams(vmem_limit_bytes=50 * 2**20),
        name="fetch",
    )(weight)


def heads_kernel(depth, core_ref, ids_ref, gain_ref, *refs):
    ways = gain_ref.shape[0]
    shares, weight, outs = refs[:ways], refs[ways], refs[ways + 1 :]
    width = shares[0].shape[1]
    values = [s[...].astype(F32) for s in shares]
    square = sum(jnp.sum(v * v, axis=-1, keepdims=True) for v in values)
    factor = lax.rsqrt(square / (ways * width) + EPSILON)
    normed = [(v * factor * gain_ref[ids_ref[c]]).astype(BF16) for c, v in enumerate(values)]
    size = outs[0].shape[1] // 3
    for kind in range(3):
        for i, out in ((1, outs[1]), (0, outs[0])):
            columns = pl.ds(pl.multiple_of((core_ref[0] ^ i) * size, size), size)
            mixed = sum(
                dot(n, weight[kind, pl.ds(pl.multiple_of(ids_ref[c] * width, width), width), columns])
                for c, n in enumerate(normed)
            )
            if kind < 2:
                mixed = jnp.concatenate([unit(mixed[:, c : c + depth]) for c in range(0, size, depth)], axis=1)
            out[:, kind * size : (kind + 1) * size] = mixed.astype(BF16)


def global_heads(depth, core, ids, gain, shares, qkv):
    shape = jax.ShapeDtypeStruct((shares[0].shape[0], 3 * qkv.shape[2] // 2), BF16)
    return pl.pallas_call(
        functools.partial(heads_kernel, depth),
        in_specs=[SMEM, SMEM] + [VMEM] * (2 + len(shares)),
        out_specs=(VMEM, VMEM),
        out_shape=(shape, shape),
        compiler_params=pltpu.CompilerParams(vmem_limit_bytes=8 * 2**20),
        name="global_heads",
    )(core, ids, gain, *shares, qkv)


def attend_kernel(depth, me_ref, ids_ref, scale_ref, kept_ref, given_ref, *refs):
    pieces, (own_ref, other_ref) = refs[:-2], refs[-2:]
    rows = kept_ref.shape[0]
    size = own_ref.shape[1]
    heads = size // depth
    me = me_ref[0]

    def places(index, shape, axis):
        row = lax.broadcasted_iota(jnp.int32, shape, axis)
        return jnp.where(row < rows, index * rows + row, (index ^ 1) * rows + row - rows)

    at = places(me, (2 * rows, 1), 0)
    seen = [places(i, (1, 2 * rows), 1) <= at for i in [me] + [ids_ref[p + 1] for p in range(len(pieces))]]
    own = jnp.concatenate([kept_ref[...], given_ref[...]], axis=0)
    query = own[:, :size]
    pieces = [own[:, size:]] + [p[...] for p in pieces]
    for h in range(heads):
        cut = slice(h * depth, (h + 1) * depth)
        factor = scale_ref[(me % 2) * heads + h] / math.sqrt(depth)
        scores = [jnp.where(s, dot_t(query[:, cut], p[:, cut]) * factor, NEGATIVE) for s, p in zip(seen, pieces)]
        top = functools.reduce(jnp.maximum, [jnp.max(s, axis=-1, keepdims=True) for s in scores])
        weights = [jnp.exp(s - top) for s in scores]
        total = sum(jnp.sum(w, axis=-1, keepdims=True) for w in weights)
        values = slice(size + h * depth, size + (h + 1) * depth)
        summed = sum(dot(w.astype(BF16), p[:, values]) for w, p in zip(weights, pieces))
        attended = (summed / total).astype(BF16)
        own_ref[:, cut] = attended[:rows]
        other_ref[:, cut] = attended[rows:]


def attend(depth, me, ids, scale, kept, given, pieces):
    rows = kept.shape[0]
    shape = jax.ShapeDtypeStruct((rows, kept.shape[1] // 3), BF16)
    return pl.pallas_call(
        functools.partial(attend_kernel, depth),
        in_specs=[SMEM, SMEM, SMEM] + [VMEM] * (2 + len(pieces)),
        out_specs=(VMEM, VMEM),
        out_shape=(shape, shape),
        compiler_params=pltpu.CompilerParams(vmem_limit_bytes=20 * 2**20),
        name="attend",
    )(me, ids, scale, kept, given, *pieces)


def project_kernel(core_ref, slots_ref, own_ref, other_ref, proj_ref, *outs):
    size = own_ref.shape[1]
    own_rows = pl.ds(pl.multiple_of(core_ref[0] * size, size), size)
    other_rows = pl.ds(pl.multiple_of((core_ref[0] ^ 1) * size, size), size)
    for slot, out in enumerate(outs):
        width = out.shape[1]
        columns = pl.ds(pl.multiple_of(slots_ref[slot] * width, width), width)
        out[...] = (dot(own_ref[...], proj_ref[own_rows, columns]) + dot(other_ref[...], proj_ref[other_rows, columns])).astype(BF16)


def project(core, slots, own, other, proj):
    ways = slots.shape[0]
    return pl.pallas_call(
        project_kernel,
        in_specs=[SMEM, SMEM] + [VMEM] * 3,
        out_specs=[VMEM] * ways,
        out_shape=[jax.ShapeDtypeStruct((own.shape[0], proj.shape[1] // ways), BF16)] * ways,
        compiler_params=pltpu.CompilerParams(vmem_limit_bytes=6 * 2**20),
        name="project",
    )(core, slots, own, other, proj)


def result_kernel(count, order_ref, own_ref, *refs):
    pieces, (result_ref, routed_ref) = refs[:count], refs[count:]
    total = own_ref[...].astype(F32) + sum(p[...].astype(F32) for p in pieces)
    result = total.astype(BF16)
    result_ref[...] = result
    routed_ref[...] = dot(order_ref[...], result).astype(BF16)


def finish_result(order, residual, pieces):
    shape = jax.ShapeDtypeStruct(residual.shape, BF16)
    return pl.pallas_call(
        functools.partial(result_kernel, len(pieces)),
        in_specs=[VMEM] * (2 + len(pieces)),
        out_specs=(VMEM, VMEM),
        out_shape=(shape, shape),
        compiler_params=pltpu.CompilerParams(vmem_limit_bytes=4 * 2**20),
        name="finish_result",
    )(order, residual, *pieces)


def bytes_kernel(count, kept_ref, result_ref, proj_ref, *refs):
    pieces, out_ref = refs[:count], refs[count]
    state = pieces[0][...].astype(F32)
    for i, p in enumerate(pieces[1:], 1):
        state += jnp.where(kept_ref[i] != 0, p[...].astype(F32), 0.0)
    state = state.astype(BF16).astype(F32)
    rows = result_ref.shape[0]
    width = proj_ref.shape[0]
    own = state.shape[0] // rows
    mixed = [
        (state[b * rows : (b + 1) * rows] + dot(result_ref[:, b * width : (b + 1) * width], proj_ref[...])).astype(BF16)
        for b in range(own)
    ]
    at = lax.broadcasted_iota(jnp.int32, (rows * own, rows * own), 0)
    to = lax.broadcasted_iota(jnp.int32, (rows * own, rows * own), 1)
    order = (to == (at % own) * rows + at // own).astype(F32).astype(BF16)
    out_ref[...] = dot(order, jnp.concatenate(mixed, axis=0)).astype(BF16)


def finish_bytes(kept, result, proj, pieces):
    return pl.pallas_call(
        functools.partial(bytes_kernel, len(pieces)),
        in_specs=[SMEM] + [VMEM] * (2 + len(pieces)),
        out_specs=VMEM,
        out_shape=jax.ShapeDtypeStruct(pieces[0].shape, BF16),
        compiler_params=pltpu.CompilerParams(vmem_limit_bytes=16 * 2**20),
        name="finish_bytes",
    )(kept, result, proj, *pieces)


def shift(value, axis, step):
    count = lax.axis_size(axis)
    return lax.ppermute(value, axis, [(i, (i + step) % count) for i in range(count)])


def scatter(chunks, axis):
    return [chunks[0]] + [shift(chunk, axis, step) for step, chunk in enumerate(chunks[1:], 1)]


def shift_slots(axis):
    count = lax.axis_size(axis)
    return ((lax.axis_index(axis) + jnp.arange(count)) % count).astype(jnp.int32)


def relay_slots(axis):
    me = lax.axis_index(axis)
    outer = (me == 0) | (me == 3)
    beside, across = me ^ 1, 3 - me
    return jnp.stack([me, jnp.where(outer, across, beside), jnp.where(outer, beside, across), me ^ 2]).astype(jnp.int32)


def relay_first(chunks, axis):
    swapped = lax.ppermute(chunks[1], axis, [(0, 1), (1, 0), (2, 3), (3, 2)])
    middle = lax.ppermute(chunks[2], axis, [(1, 2), (2, 1)])
    return swapped, middle


def relay_sum(chunks, swapped, axis):
    me = lax.axis_index(axis)
    relayed = jnp.where((me == 0) | (me == 3), 0.0, swapped.astype(F32))
    return (chunks[3].astype(F32) + relayed).astype(BF16)


def relay_rest(chunks, swapped, middle, sent, axis):
    inward = lax.ppermute(chunks[2], axis, [(0, 1), (3, 2)])
    crossed = lax.ppermute(sent, axis, [(0, 2), (2, 0), (1, 3), (3, 1)])
    me = lax.axis_index(axis)
    outer = ((me == 0) | (me == 3)).astype(jnp.int32)
    return jnp.stack([1 + 0 * outer, outer, 1 - outer, 1 - outer, 1 + 0 * outer]), [chunks[0], swapped, middle, inward, crossed]


def gather(value, axis):
    return [value] + [shift(value, axis, step) for step in range(1, lax.axis_size(axis))]


def swap_cores(value, axis):
    return lax.ppermute(value, axis, [(i, i ^ 1) for i in range(lax.axis_size(axis))])


def twin_ids(axis):
    count = lax.axis_size(axis)
    return ((lax.axis_index(axis) - 2 * jnp.arange(count // 2)) % count).astype(jnp.int32)


def owner_order(owners, source, patches):
    listed = lax.dynamic_index_in_dim(owners, source, 0, keepdims=False)
    count = listed.shape[0]
    block = patches // count
    index = jnp.arange(count, dtype=jnp.int32)
    before = (listed[None, :] < listed[:, None]) | (
        (listed[None, :] == listed[:, None]) & (index[None, :] < index[:, None])
    )
    slot = jnp.sum(before, axis=1).astype(jnp.int32)
    row = jnp.arange(patches, dtype=jnp.int32)
    spread = jnp.sum(jnp.where(row[:, None] // block == index[None, :], slot[None, :], 0), axis=1).astype(jnp.int32)
    place = spread * block + row % block
    return (row[:, None] == place[None, :]).astype(BF16)


def on_device(
    byte_in,
    local_gain,
    local_qkv,
    local_out,
    mlp_up,
    mlp_down,
    local_scale,
    patch_proj,
    global_gain,
    global_qkv,
    global_out,
    global_scale,
    back_proj,
    owners,
):
    patches, span, width = byte_in.shape
    ways = lax.axis_size("head")
    own = span // ways
    me = lax.axis_index("head").astype(jnp.int32)
    seq = lax.axis_index("seq").astype(jnp.int32)
    depth = global_qkv.shape[2] // global_scale.shape[0]

    line = ways == 4
    slots = jnp.stack([relay_slots("head") if line else shift_slots("head"), shift_slots("head")])
    parts, chunks = local_part(
        me.reshape(1),
        local_scale,
        slots,
        byte_in.reshape(-1, width),
        local_gain.reshape(1, -1),
        jnp.transpose(local_qkv, (1, 0, 2)),
        local_out,
        mlp_up,
        mlp_down,
        patch_proj,
        span,
    )
    residual = sum(p.astype(F32) for p in scatter(chunks, "head")).astype(BF16)
    weight, residual = lax.optimization_barrier((jnp.transpose(global_qkv, (1, 0, 2)), residual))
    shares = gather(residual, "head")
    ids = (me - jnp.arange(ways, dtype=jnp.int32)) % ways
    core = (seq % 2).reshape(1)
    kept, given = global_heads(depth, core, ids, global_gain.reshape(ways, 1, -1), shares, fetch(weight))
    received = swap_cores(given, "seq")
    parts, received = lax.optimization_barrier((parts, received))
    half = kept.shape[1] // 3
    keyed = jnp.concatenate([kept[:, half:], received[:, half:]], axis=0)
    pieces = [shift(keyed, "seq", 2 * step) for step in range(1, lax.axis_size("seq") // 2)]
    if line:
        swapped, middle = relay_first(parts, "head")
        sent = relay_sum(parts, swapped, "head")
        kept, sent, middle = lax.optimization_barrier((kept, sent, middle))
        counted, parts = relay_rest(parts, swapped, middle, sent, "head")
    else:
        counted, parts = jnp.ones((ways,), jnp.int32), scatter(parts, "head")
    own_heads, other_heads = attend(depth, seq.reshape(1), twin_ids("seq"), global_scale, kept, received, pieces)
    update = project(core, slots[1], own_heads, swap_cores(other_heads, "seq"), global_out)
    updates, parts = lax.optimization_barrier((scatter(update, "head"), parts))
    result, routed = finish_result(owner_order(owners, seq, patches), residual, updates)
    global_state = lax.all_to_all(routed, "seq", split_axis=0, concat_axis=0, tiled=True)
    byte_out = finish_bytes(counted, result, back_proj, parts)
    return byte_out.reshape(patches, own, width), global_state


def solution(mesh):
    placed = (
        P("seq", None, None),
        P(),
        P(None, None, "head"),
        P("head", None),
        P(None, "head"),
        P("head", None),
        P("head"),
        P(),
        P(),
        P(None, None, "head"),
        P("head", None),
        P("head"),
        P(),
        P(),
    )
    return jax.shard_map(
        on_device,
        mesh=mesh,
        in_specs=placed,
        out_specs=(P("seq", "head", None), P("seq", "head")),
        check_vma=False,
    )
```

```python
import functools
import math

import jax
import jax.numpy as jnp
from jax import lax
from jax.experimental import pallas as pl
from jax.experimental.pallas import tpu as pltpu
from jax.sharding import PartitionSpec as P

EPSILON = 1e-06
NEGATIVE = -1e30
F32 = jnp.float32
BF16 = jnp.bfloat16
VMEM = pl.BlockSpec(memory_space=pltpu.VMEM)
HBM = pl.BlockSpec(memory_space=pltpu.HBM)
SMEM = pl.BlockSpec(memory_space=pltpu.SMEM)


def dot(left, right):
    return jnp.dot(left, right, preferred_element_type=F32)


def dot_t(left, right):
    return lax.dot_general(left, right, (((1,), (1,)), ((), ())), preferred_element_type=F32)


def unit(values):
    return (values * lax.rsqrt(jnp.mean(values * values, axis=-1, keepdims=True) + EPSILON)).astype(BF16)


def gelu(values):
    inner = math.sqrt(2.0 / math.pi) * (values + 0.044715 * (values * values * values))
    return 0.5 * values * (1.0 + jnp.tanh(inner))


def local_kernel(span, piece, step, me_ref, scale_ref, slots_ref, gain_ref, x_hbm, *refs):
    ways = slots_ref.shape[1]
    sources, parts, shares = refs[:5], refs[5 : 5 + ways], refs[5 + ways : 5 + 2 * ways]
    x_ref, part_ref, share_ref = refs[5 + 2 * ways : 8 + 2 * ways]
    held, (in_sem, x_sem, part_sem) = refs[8 + 2 * ways : 13 + 2 * ways], refs[13 + 2 * ways :]
    patches = share_ref.shape[1]
    width = x_ref.shape[1]
    own = span // ways
    rows = piece * span
    pieces = patches // piece
    loads = [pltpu.make_async_copy(s, h, in_sem.at[i]) for i, (s, h) in enumerate(zip(sources, held))]
    cuts = [slice(i * rows, (i + 1) * rows) for i in range(pieces)]
    x_loads = [pltpu.make_async_copy(x_hbm.at[pl.ds(c.start, rows)], x_ref.at[pl.ds(c.start, rows)], x_sem.at[i]) for i, c in enumerate(cuts)]
    for copy in x_loads + loads:
        copy.start()
    qkv_ref, up_ref, out_ref, down_ref, proj_ref = held
    at = lax.broadcasted_iota(jnp.int32, (rows, rows), 0)
    to = lax.broadcasted_iota(jnp.int32, (rows, rows), 1)
    order = (to == (at % piece) * span + at // piece).astype(F32).astype(BF16)
    kept = lax.broadcasted_iota(jnp.int32, (rows, 1), 0) // piece // own == me_ref[0]
    xs, normed = [], []
    for copy in x_loads + loads:
        copy.wait()
    for i, cut in enumerate(cuts):
        x = dot(order, x_ref[cut])
        xs.append(jnp.where(kept, x, 0.0).astype(BF16))
        factor = lax.rsqrt(jnp.mean(x * x, axis=-1, keepdims=True) + EPSILON)
        normed.append((x * factor * gain_ref[...]).astype(BF16))
    xs, normed = jnp.concatenate(xs, axis=0), jnp.concatenate(normed, axis=0)
    query, key, value = (dot(normed, qkv_ref[i]) for i in range(3))
    seen = (at % piece == to % piece) & (to <= at)
    heads = scale_ref.shape[0]
    depth = query.shape[1] // heads
    attended = []
    for cut in cuts:
        columns = []
        for h in range(heads):
            head = slice(h * depth, (h + 1) * depth)
            scores = dot_t(unit(query[cut, head]), unit(key[cut, head])) * (scale_ref[h] / math.sqrt(depth))
            scores = jnp.where(seen, scores, NEGATIVE)
            weights = jnp.exp(scores - jnp.max(scores, axis=-1, keepdims=True))
            total = jnp.sum(weights, axis=-1, keepdims=True)
            columns.append((dot(weights.astype(BF16), value[cut, head].astype(BF16)) / total).astype(BF16))
        attended.append(jnp.concatenate(columns, axis=1))
    attended = jnp.concatenate(attended, axis=0)
    act = gelu(dot(normed, up_ref[...])).astype(BF16)
    mixed = jnp.concatenate([attended, act], axis=1)
    share = 0.0
    stores = []
    for c in range(0, width, step):
        columns = slice(c, c + step)
        partial = dot(mixed, jnp.concatenate([out_ref[:, columns], down_ref[:, columns]], axis=0))
        partial = (partial + xs[:, columns].astype(F32)).astype(BF16)
        for i, cut in enumerate(cuts):
            for b in range(span):
                put = (b % own) * patches + i * piece
                part_ref[b // own, put : put + piece, columns] = partial[cut][b * piece : (b + 1) * piece]
        for slot, part in enumerate(parts):
            source = part_ref.at[slots_ref[0, slot], :, pl.ds(c, step)]
            stores.append(pltpu.make_async_copy(source, part.at[:, pl.ds(c, step)], part_sem.at[len(stores)]))
            stores[-1].start()
        share += dot(partial, proj_ref[columns])
    share = share.astype(BF16)
    size = share.shape[1]
    for i, cut in enumerate(cuts):
        for b in range(span):
            put = slice((b % own) * size, (b % own + 1) * size)
            share_ref[b // own, i * piece : (i + 1) * piece, put] = share[cut][b * piece : (b + 1) * piece]
    for slot, out in enumerate(shares):
        out[...] = share_ref[slots_ref[1, slot]]
    for copy in stores:
        copy.wait()


def local_part(me, scale, slots, x, gain, qkv, out, up, down, proj, span):
    rows, width = x.shape
    patches = rows // span
    ways = slots.shape[1]
    own = span // ways
    weights = (qkv, up, out, down, proj)
    piece = math.gcd(patches, 32)
    step = math.gcd(width, 1024)
    part = (own * patches, width)
    share = (patches, own * proj.shape[1])
    outs = pl.pallas_call(
        functools.partial(local_kernel, span, piece, step),
        in_specs=[SMEM, SMEM, SMEM, VMEM] + [HBM] * (1 + len(weights)),
        out_specs=[HBM] * ways + [VMEM] * ways,
        out_shape=[jax.ShapeDtypeStruct(part, BF16)] * ways + [pltpu.VMEM(share, BF16)] * ways,
        scratch_shapes=[pltpu.VMEM(x.shape, BF16), pltpu.VMEM((ways, *part), BF16), pltpu.VMEM((ways, *share), BF16)]
        + [pltpu.VMEM(w.shape, w.dtype) for w in weights]
        + [
            pltpu.SemaphoreType.DMA((len(weights),)),
            pltpu.SemaphoreType.DMA((patches // piece,)),
            pltpu.SemaphoreType.DMA((ways * (width // step),)),
        ],
        compiler_params=pltpu.CompilerParams(vmem_limit_bytes=60 * 2**20),
        name="local_part",
    )(me, scale, slots, gain, x, *weights)
    return outs[:ways], outs[ways:]


def fetch_kernel(source, held, sems):
    parts = source.shape[0]
    copies = [pltpu.make_async_copy(source.at[i], held.at[i], sems.at[i]) for i in range(parts)]
    for copy in copies:
        copy.start()
    for copy in copies:
        copy.wait()


def fetch(weight):
    return pl.pallas_call(
        fetch_kernel,
        in_specs=[HBM],
        out_specs=VMEM,
        out_shape=pltpu.VMEM(weight.shape, weight.dtype),
        scratch_shapes=[pltpu.SemaphoreType.DMA((weight.shape[0],))],
        compiler_params=pltpu.CompilerParams(vmem_limit_bytes=50 * 2**20),
        name="fetch",
    )(weight)


def heads_kernel(depth, core_ref, ids_ref, gain_ref, *refs):
    ways = gain_ref.shape[0]
    shares, weight, outs = refs[:ways], refs[ways], refs[ways + 1 :]
    width = shares[0].shape[1]
    values = [s[...].astype(F32) for s in shares]
    square = sum(jnp.sum(v * v, axis=-1, keepdims=True) for v in values)
    factor = lax.rsqrt(square / (ways * width) + EPSILON)
    normed = [(v * factor * gain_ref[ids_ref[c]]).astype(BF16) for c, v in enumerate(values)]
    size = outs[0].shape[1] // 3
    for kind in range(3):
        for i, out in ((1, outs[1]), (0, outs[0])):
            columns = pl.ds(pl.multiple_of((core_ref[0] ^ i) * size, size), size)
            mixed = sum(
                dot(n, weight[kind, pl.ds(pl.multiple_of(ids_ref[c] * width, width), width), columns])
                for c, n in enumerate(normed)
            )
            if kind < 2:
                mixed = jnp.concatenate([unit(mixed[:, c : c + depth]) for c in range(0, size, depth)], axis=1)
            out[:, kind * size : (kind + 1) * size] = mixed.astype(BF16)


def global_heads(depth, core, ids, gain, shares, qkv):
    shape = jax.ShapeDtypeStruct((shares[0].shape[0], 3 * qkv.shape[2] // 2), BF16)
    return pl.pallas_call(
        functools.partial(heads_kernel, depth),
        in_specs=[SMEM, SMEM] + [VMEM] * (2 + len(shares)),
        out_specs=(VMEM, VMEM),
        out_shape=(shape, shape),
        compiler_params=pltpu.CompilerParams(vmem_limit_bytes=8 * 2**20),
        name="global_heads",
    )(core, ids, gain, *shares, qkv)


def attend_kernel(depth, me_ref, ids_ref, scale_ref, kept_ref, given_ref, *refs):
    pieces, (own_ref, other_ref) = refs[:-2], refs[-2:]
    rows = kept_ref.shape[0]
    size = own_ref.shape[1]
    heads = size // depth
    me = me_ref[0]

    def places(index, shape, axis):
        row = lax.broadcasted_iota(jnp.int32, shape, axis)
        return jnp.where(row < rows, index * rows + row, (index ^ 1) * rows + row - rows)

    at = places(me, (2 * rows, 1), 0)
    seen = [places(i, (1, 2 * rows), 1) <= at for i in [me] + [ids_ref[p + 1] for p in range(len(pieces))]]
    own = jnp.concatenate([kept_ref[...], given_ref[...]], axis=0)
    query = own[:, :size]
    pieces = [own[:, size:]] + [p[...] for p in pieces]
    for h in range(heads):
        cut = slice(h * depth, (h + 1) * depth)
        factor = scale_ref[(me % 2) * heads + h] / math.sqrt(depth)
        scores = [jnp.where(s, dot_t(query[:, cut], p[:, cut]) * factor, NEGATIVE) for s, p in zip(seen, pieces)]
        top = functools.reduce(jnp.maximum, [jnp.max(s, axis=-1, keepdims=True) for s in scores])
        weights = [jnp.exp(s - top) for s in scores]
        total = sum(jnp.sum(w, axis=-1, keepdims=True) for w in weights)
        values = slice(size + h * depth, size + (h + 1) * depth)
        summed = sum(dot(w.astype(BF16), p[:, values]) for w, p in zip(weights, pieces))
        attended = (summed / total).astype(BF16)
        own_ref[:, cut] = attended[:rows]
        other_ref[:, cut] = attended[rows:]


def attend(depth, me, ids, scale, kept, given, pieces):
    rows = kept.shape[0]
    shape = jax.ShapeDtypeStruct((rows, kept.shape[1] // 3), BF16)
    return pl.pallas_call(
        functools.partial(attend_kernel, depth),
        in_specs=[SMEM, SMEM, SMEM] + [VMEM] * (2 + len(pieces)),
        out_specs=(VMEM, VMEM),
        out_shape=(shape, shape),
        compiler_params=pltpu.CompilerParams(vmem_limit_bytes=20 * 2**20),
        name="attend",
    )(me, ids, scale, kept, given, *pieces)


def project_kernel(core_ref, slots_ref, own_ref, other_ref, proj_ref, *outs):
    size = own_ref.shape[1]
    own_rows = pl.ds(pl.multiple_of(core_ref[0] * size, size), size)
    other_rows = pl.ds(pl.multiple_of((core_ref[0] ^ 1) * size, size), size)
    for slot, out in enumerate(outs):
        width = out.shape[1]
        columns = pl.ds(pl.multiple_of(slots_ref[slot] * width, width), width)
        out[...] = (dot(own_ref[...], proj_ref[own_rows, columns]) + dot(other_ref[...], proj_ref[other_rows, columns])).astype(BF16)


def project(core, slots, own, other, proj):
    ways = slots.shape[0]
    return pl.pallas_call(
        project_kernel,
        in_specs=[SMEM, SMEM] + [VMEM] * 3,
        out_specs=[VMEM] * ways,
        out_shape=[jax.ShapeDtypeStruct((own.shape[0], proj.shape[1] // ways), BF16)] * ways,
        compiler_params=pltpu.CompilerParams(vmem_limit_bytes=6 * 2**20),
        name="project",
    )(core, slots, own, other, proj)


def result_kernel(count, order_ref, own_ref, *refs):
    pieces, (result_ref, routed_ref) = refs[:count], refs[count:]
    total = own_ref[...].astype(F32) + sum(p[...].astype(F32) for p in pieces)
    result = total.astype(BF16)
    result_ref[...] = result
    routed_ref[...] = dot(order_ref[...], result).astype(BF16)


def finish_result(order, residual, pieces):
    shape = jax.ShapeDtypeStruct(residual.shape, BF16)
    return pl.pallas_call(
        functools.partial(result_kernel, len(pieces)),
        in_specs=[VMEM] * (2 + len(pieces)),
        out_specs=(VMEM, VMEM),
        out_shape=(shape, shape),
        compiler_params=pltpu.CompilerParams(vmem_limit_bytes=4 * 2**20),
        name="finish_result",
    )(order, residual, *pieces)


def bytes_kernel(count, counted_ref, result_ref, proj_ref, *refs):
    sources, out_ref, held, sems = refs[:count], refs[count], refs[count + 1], refs[count + 2]
    copies = [pltpu.make_async_copy(p, held.at[i], sems.at[i]) for i, p in enumerate(sources)]
    for copy in copies:
        copy.start()
    rows = result_ref.shape[0]
    width = proj_ref.shape[0]
    own = out_ref.shape[0] // rows
    back = jnp.concatenate([dot(result_ref[:, b * width : (b + 1) * width], proj_ref[...]) for b in range(own)], axis=0)
    at = lax.broadcasted_iota(jnp.int32, (rows * own, rows * own), 0)
    to = lax.broadcasted_iota(jnp.int32, (rows * own, rows * own), 1)
    order = (to == (at % own) * rows + at // own).astype(F32).astype(BF16)
    for copy in copies:
        copy.wait()
    state = held[0].astype(F32)
    for i in range(1, count):
        state += jnp.where(counted_ref[i] != 0, held[i].astype(F32), 0.0)
    state = state.astype(BF16).astype(F32)
    out_ref[...] = dot(order, (state + back).astype(BF16)).astype(BF16)


def finish_bytes(counted, result, proj, pieces):
    shape = pieces[0].shape
    return pl.pallas_call(
        functools.partial(bytes_kernel, len(pieces)),
        in_specs=[SMEM, VMEM, VMEM] + [pl.BlockSpec(memory_space=pl.ANY)] * len(pieces),
        out_specs=VMEM,
        out_shape=jax.ShapeDtypeStruct(shape, BF16),
        scratch_shapes=[pltpu.VMEM((len(pieces), *shape), BF16), pltpu.SemaphoreType.DMA((len(pieces),))],
        compiler_params=pltpu.CompilerParams(vmem_limit_bytes=16 * 2**20),
        name="finish_bytes",
    )(counted, result, proj, *pieces)


def shift(value, axis, step):
    count = lax.axis_size(axis)
    return lax.ppermute(value, axis, [(i, (i + step) % count) for i in range(count)])


def scatter(chunks, axis):
    return [chunks[0]] + [shift(chunk, axis, step) for step, chunk in enumerate(chunks[1:], 1)]


def shift_slots(axis):
    count = lax.axis_size(axis)
    return ((lax.axis_index(axis) + jnp.arange(count)) % count).astype(jnp.int32)


def relay_slots(axis):
    me = lax.axis_index(axis)
    outer = (me == 0) | (me == 3)
    beside, across = me ^ 1, 3 - me
    return jnp.stack([me, jnp.where(outer, across, beside), jnp.where(outer, beside, across), me ^ 2]).astype(jnp.int32)


def relay_first(chunks, axis):
    swapped = lax.ppermute(chunks[1], axis, [(0, 1), (1, 0), (2, 3), (3, 2)])
    middle = lax.ppermute(chunks[2], axis, [(1, 2), (2, 1)])
    return swapped, middle


def relay_sum(chunks, swapped, axis):
    me = lax.axis_index(axis)
    relayed = jnp.where((me == 0) | (me == 3), 0.0, swapped.astype(F32))
    return (chunks[3].astype(F32) + relayed).astype(BF16)


def relay_rest(chunks, swapped, middle, sent, axis):
    inward = lax.ppermute(chunks[2], axis, [(0, 1), (3, 2)])
    crossed = lax.ppermute(sent, axis, [(0, 2), (2, 0), (1, 3), (3, 1)])
    me = lax.axis_index(axis)
    outer = ((me == 0) | (me == 3)).astype(jnp.int32)
    return jnp.stack([1 + 0 * outer, outer, 1 - outer, 1 - outer, 1 + 0 * outer]), [chunks[0], swapped, middle, inward, crossed]


def gather(value, axis):
    return [value] + [shift(value, axis, step) for step in range(1, lax.axis_size(axis))]


def swap_cores(value, axis):
    return lax.ppermute(value, axis, [(i, i ^ 1) for i in range(lax.axis_size(axis))])


def twin_ids(axis):
    count = lax.axis_size(axis)
    return ((lax.axis_index(axis) - 2 * jnp.arange(count // 2)) % count).astype(jnp.int32)


def owner_order(owners, source, patches):
    listed = lax.dynamic_index_in_dim(owners, source, 0, keepdims=False)
    count = listed.shape[0]
    block = patches // count
    index = jnp.arange(count, dtype=jnp.int32)
    before = (listed[None, :] < listed[:, None]) | (
        (listed[None, :] == listed[:, None]) & (index[None, :] < index[:, None])
    )
    slot = jnp.sum(before, axis=1).astype(jnp.int32)
    row = jnp.arange(patches, dtype=jnp.int32)
    spread = jnp.sum(jnp.where(row[:, None] // block == index[None, :], slot[None, :], 0), axis=1).astype(jnp.int32)
    place = spread * block + row % block
    return (row[:, None] == place[None, :]).astype(BF16)


def on_device(
    byte_in,
    local_gain,
    local_qkv,
    local_out,
    mlp_up,
    mlp_down,
    local_scale,
    patch_proj,
    global_gain,
    global_qkv,
    global_out,
    global_scale,
    back_proj,
    owners,
):
    patches, span, width = byte_in.shape
    ways = lax.axis_size("head")
    own = span // ways
    me = lax.axis_index("head").astype(jnp.int32)
    seq = lax.axis_index("seq").astype(jnp.int32)
    depth = global_qkv.shape[2] // global_scale.shape[0]

    line = ways == 4
    slots = jnp.stack([relay_slots("head") if line else shift_slots("head"), shift_slots("head")])
    parts, chunks = local_part(
        me.reshape(1),
        local_scale,
        slots,
        byte_in.reshape(-1, width),
        local_gain.reshape(1, -1),
        jnp.transpose(local_qkv, (1, 0, 2)),
        local_out,
        mlp_up,
        mlp_down,
        patch_proj,
        span,
    )
    chunks = scatter(chunks, "head")
    if line:
        swapped, middle = relay_first(parts, "head")
        chunks, swapped, middle = lax.optimization_barrier((chunks, swapped, middle))
        sent = relay_sum(parts, swapped, "head")
    residual = sum(p.astype(F32) for p in chunks).astype(BF16)
    weight, residual = lax.optimization_barrier((jnp.transpose(global_qkv, (1, 0, 2)), residual))
    shares = gather(residual, "head")
    ids = (me - jnp.arange(ways, dtype=jnp.int32)) % ways
    core = (seq % 2).reshape(1)
    kept, given = global_heads(depth, core, ids, global_gain.reshape(ways, 1, -1), shares, fetch(weight))
    received = swap_cores(given, "seq")
    half = kept.shape[1] // 3
    keyed = jnp.concatenate([kept[:, half:], received[:, half:]], axis=0)
    pieces = [shift(keyed, "seq", 2 * step) for step in range(1, lax.axis_size("seq") // 2)]
    if line:
        parts, sent, received = lax.optimization_barrier((parts, sent, received))
        counted, parts = relay_rest(parts, swapped, middle, sent, "head")
    else:
        counted, parts = jnp.ones((ways,), jnp.int32), scatter(parts, "head")
    own_heads, other_heads = attend(depth, seq.reshape(1), twin_ids("seq"), global_scale, kept, received, pieces)
    update = project(core, slots[1], own_heads, swap_cores(other_heads, "seq"), global_out)
    updates, parts = lax.optimization_barrier((scatter(update, "head"), parts))
    result, routed = finish_result(owner_order(owners, seq, patches), residual, updates)
    global_state = lax.all_to_all(routed, "seq", split_axis=0, concat_axis=0, tiled=True)
    byte_out = finish_bytes(counted, result, back_proj, parts)
    return byte_out.reshape(patches, own, width), global_state


def solution(mesh):
    placed = (
        P("seq", None, None),
        P(),
        P(None, None, "head"),
        P("head", None),
        P(None, "head"),
        P("head", None),
        P("head"),
        P(),
        P(),
        P(None, None, "head"),
        P("head", None),
        P("head"),
        P(),
        P(),
    )
    return jax.shard_map(
        on_device,
        mesh=mesh,
        in_specs=placed,
        out_specs=(P("seq", "head", None), P("seq", "head")),
        check_vma=False,
    )
```

```python
import functools
import math

import jax
import jax.numpy as jnp
from jax import lax
from jax.experimental import pallas as pl
from jax.experimental.pallas import tpu as pltpu
from jax.sharding import PartitionSpec as P

EPSILON = 1e-06
NEGATIVE = -1e30
F32 = jnp.float32
BF16 = jnp.bfloat16
VMEM = pl.BlockSpec(memory_space=pltpu.VMEM)
HBM = pl.BlockSpec(memory_space=pltpu.HBM)
SMEM = pl.BlockSpec(memory_space=pltpu.SMEM)


def dot(left, right):
    return jnp.dot(left, right, preferred_element_type=F32)


def dot_t(left, right):
    return lax.dot_general(left, right, (((1,), (1,)), ((), ())), preferred_element_type=F32)


def unit(values):
    return (values * lax.rsqrt(jnp.mean(values * values, axis=-1, keepdims=True) + EPSILON)).astype(BF16)


def gelu(values):
    inner = math.sqrt(2.0 / math.pi) * (values + 0.044715 * (values * values * values))
    return 0.5 * values * (1.0 + jnp.tanh(inner))


def local_kernel(span, piece, step, me_ref, scale_ref, slots_ref, gain_ref, x_hbm, *refs):
    ways = slots_ref.shape[1]
    sources, parts, shares = refs[:5], refs[5 : 5 + ways], refs[5 + ways : 5 + 2 * ways]
    x_ref, part_ref, share_ref = refs[5 + 2 * ways : 8 + 2 * ways]
    held, (in_sem, x_sem, part_sem) = refs[8 + 2 * ways : 13 + 2 * ways], refs[13 + 2 * ways :]
    patches = share_ref.shape[1]
    width = x_ref.shape[1]
    own = span // ways
    rows = piece * span
    pieces = patches // piece
    loads = [pltpu.make_async_copy(s, h, in_sem.at[i]) for i, (s, h) in enumerate(zip(sources, held))]
    cuts = [slice(i * rows, (i + 1) * rows) for i in range(pieces)]
    x_loads = [pltpu.make_async_copy(x_hbm.at[pl.ds(c.start, rows)], x_ref.at[pl.ds(c.start, rows)], x_sem.at[i]) for i, c in enumerate(cuts)]
    for copy in x_loads + loads:
        copy.start()
    qkv_ref, up_ref, out_ref, down_ref, proj_ref = held
    at = lax.broadcasted_iota(jnp.int32, (rows, rows), 0)
    to = lax.broadcasted_iota(jnp.int32, (rows, rows), 1)
    order = (to == (at % piece) * span + at // piece).astype(F32).astype(BF16)
    kept = lax.broadcasted_iota(jnp.int32, (rows, 1), 0) // piece // own == me_ref[0]
    xs, normed = [], []
    for copy in x_loads + loads:
        copy.wait()
    for i, cut in enumerate(cuts):
        x = dot(order, x_ref[cut])
        xs.append(jnp.where(kept, x, 0.0).astype(BF16))
        factor = lax.rsqrt(jnp.mean(x * x, axis=-1, keepdims=True) + EPSILON)
        normed.append((x * factor * gain_ref[...]).astype(BF16))
    xs, normed = jnp.concatenate(xs, axis=0), jnp.concatenate(normed, axis=0)
    query, key, value = (dot(normed, qkv_ref[i]) for i in range(3))
    seen = (at % piece == to % piece) & (to <= at)
    heads = scale_ref.shape[0]
    depth = query.shape[1] // heads
    attended = []
    for cut in cuts:
        columns = []
        for h in range(heads):
            head = slice(h * depth, (h + 1) * depth)
            scores = dot_t(unit(query[cut, head]), unit(key[cut, head])) * (scale_ref[h] / math.sqrt(depth))
            scores = jnp.where(seen, scores, NEGATIVE)
            weights = jnp.exp(scores - jnp.max(scores, axis=-1, keepdims=True))
            total = jnp.sum(weights, axis=-1, keepdims=True)
            columns.append((dot(weights.astype(BF16), value[cut, head].astype(BF16)) / total).astype(BF16))
        attended.append(jnp.concatenate(columns, axis=1))
    attended = jnp.concatenate(attended, axis=0)
    act = gelu(dot(normed, up_ref[...])).astype(BF16)
    mixed = jnp.concatenate([attended, act], axis=1)
    share = 0.0
    stores = []
    for c in range(0, width, step):
        columns = slice(c, c + step)
        partial = dot(mixed, jnp.concatenate([out_ref[:, columns], down_ref[:, columns]], axis=0))
        partial = (partial + xs[:, columns].astype(F32)).astype(BF16)
        for i, cut in enumerate(cuts):
            for b in range(span):
                put = (b % own) * patches + i * piece
                part_ref[b // own, put : put + piece, columns] = partial[cut][b * piece : (b + 1) * piece]
        for slot, part in enumerate(parts):
            source = part_ref.at[slots_ref[0, slot], :, pl.ds(c, step)]
            stores.append(pltpu.make_async_copy(source, part.at[:, pl.ds(c, step)], part_sem.at[len(stores)]))
            stores[-1].start()
        share += dot(partial, proj_ref[columns])
    share = share.astype(BF16)
    size = share.shape[1]
    for i, cut in enumerate(cuts):
        for b in range(span):
            put = slice((b % own) * size, (b % own + 1) * size)
            share_ref[b // own, i * piece : (i + 1) * piece, put] = share[cut][b * piece : (b + 1) * piece]
    for slot, out in enumerate(shares):
        out[...] = share_ref[slots_ref[1, slot]]
    for copy in stores:
        copy.wait()


def local_part(me, scale, slots, x, gain, qkv, out, up, down, proj, span):
    rows, width = x.shape
    patches = rows // span
    ways = slots.shape[1]
    own = span // ways
    weights = (qkv, up, out, down, proj)
    piece = math.gcd(patches, 32)
    step = math.gcd(width, 1024)
    part = (own * patches, width)
    share = (patches, own * proj.shape[1])
    outs = pl.pallas_call(
        functools.partial(local_kernel, span, piece, step),
        in_specs=[SMEM, SMEM, SMEM, VMEM] + [HBM] * (1 + len(weights)),
        out_specs=[HBM] * ways + [VMEM] * ways,
        out_shape=[jax.ShapeDtypeStruct(part, BF16)] * ways + [pltpu.VMEM(share, BF16)] * ways,
        scratch_shapes=[pltpu.VMEM(x.shape, BF16), pltpu.VMEM((ways, *part), BF16), pltpu.VMEM((ways, *share), BF16)]
        + [pltpu.VMEM(w.shape, w.dtype) for w in weights]
        + [
            pltpu.SemaphoreType.DMA((len(weights),)),
            pltpu.SemaphoreType.DMA((patches // piece,)),
            pltpu.SemaphoreType.DMA((ways * (width // step),)),
        ],
        compiler_params=pltpu.CompilerParams(vmem_limit_bytes=60 * 2**20),
        name="local_part",
    )(me, scale, slots, gain, x, *weights)
    return outs[:ways], outs[ways:]


def fetch_kernel(source, held, sems):
    parts = source.shape[0]
    copies = [pltpu.make_async_copy(source.at[i], held.at[i], sems.at[i]) for i in range(parts)]
    for copy in copies:
        copy.start()
    for copy in copies:
        copy.wait()


def fetch(weight):
    return pl.pallas_call(
        fetch_kernel,
        in_specs=[HBM],
        out_specs=VMEM,
        out_shape=pltpu.VMEM(weight.shape, weight.dtype),
        scratch_shapes=[pltpu.SemaphoreType.DMA((weight.shape[0],))],
        compiler_params=pltpu.CompilerParams(vmem_limit_bytes=50 * 2**20),
        name="fetch",
    )(weight)


def heads_kernel(depth, core_ref, ids_ref, gain_ref, *refs):
    ways = gain_ref.shape[0]
    shares, weight, outs = refs[:ways], refs[ways], refs[ways + 1 :]
    width = shares[0].shape[1]
    values = [s[...].astype(F32) for s in shares]
    square = sum(jnp.sum(v * v, axis=-1, keepdims=True) for v in values)
    factor = lax.rsqrt(square / (ways * width) + EPSILON)
    normed = [(v * factor * gain_ref[ids_ref[c]]).astype(BF16) for c, v in enumerate(values)]
    size = outs[0].shape[1] // 3
    for kind in range(3):
        for i, out in ((1, outs[1]), (0, outs[0])):
            columns = pl.ds(pl.multiple_of((core_ref[0] ^ i) * size, size), size)
            mixed = sum(
                dot(n, weight[kind, pl.ds(pl.multiple_of(ids_ref[c] * width, width), width), columns])
                for c, n in enumerate(normed)
            )
            if kind < 2:
                mixed = jnp.concatenate([unit(mixed[:, c : c + depth]) for c in range(0, size, depth)], axis=1)
            out[:, kind * size : (kind + 1) * size] = mixed.astype(BF16)


def global_heads(depth, core, ids, gain, shares, qkv):
    shape = jax.ShapeDtypeStruct((shares[0].shape[0], 3 * qkv.shape[2] // 2), BF16)
    return pl.pallas_call(
        functools.partial(heads_kernel, depth),
        in_specs=[SMEM, SMEM] + [VMEM] * (2 + len(shares)),
        out_specs=(VMEM, VMEM),
        out_shape=(shape, shape),
        compiler_params=pltpu.CompilerParams(vmem_limit_bytes=8 * 2**20),
        name="global_heads",
    )(core, ids, gain, *shares, qkv)


def attend_kernel(depth, me_ref, ids_ref, scale_ref, kept_ref, given_ref, *refs):
    pieces, (own_ref, other_ref) = refs[:-2], refs[-2:]
    rows = kept_ref.shape[0]
    size = own_ref.shape[1]
    heads = size // depth
    me = me_ref[0]

    def places(index, shape, axis):
        row = lax.broadcasted_iota(jnp.int32, shape, axis)
        return jnp.where(row < rows, index * rows + row, (index ^ 1) * rows + row - rows)

    at = places(me, (2 * rows, 1), 0)
    seen = [places(i, (1, 2 * rows), 1) <= at for i in [me] + [ids_ref[p + 1] for p in range(len(pieces))]]
    own = jnp.concatenate([kept_ref[...], given_ref[...]], axis=0)
    query = own[:, :size]
    pieces = [own[:, size:]] + [p[...] for p in pieces]
    for h in range(heads):
        cut = slice(h * depth, (h + 1) * depth)
        factor = scale_ref[(me % 2) * heads + h] / math.sqrt(depth)
        scores = [jnp.where(s, dot_t(query[:, cut], p[:, cut]) * factor, NEGATIVE) for s, p in zip(seen, pieces)]
        top = functools.reduce(jnp.maximum, [jnp.max(s, axis=-1, keepdims=True) for s in scores])
        weights = [jnp.exp(s - top) for s in scores]
        total = sum(jnp.sum(w, axis=-1, keepdims=True) for w in weights)
        values = slice(size + h * depth, size + (h + 1) * depth)
        summed = sum(dot(w.astype(BF16), p[:, values]) for w, p in zip(weights, pieces))
        attended = (summed / total).astype(BF16)
        own_ref[:, cut] = attended[:rows]
        other_ref[:, cut] = attended[rows:]


def attend(depth, me, ids, scale, kept, given, pieces):
    rows = kept.shape[0]
    shape = jax.ShapeDtypeStruct((rows, kept.shape[1] // 3), BF16)
    return pl.pallas_call(
        functools.partial(attend_kernel, depth),
        in_specs=[SMEM, SMEM, SMEM] + [VMEM] * (2 + len(pieces)),
        out_specs=(VMEM, VMEM),
        out_shape=(shape, shape),
        compiler_params=pltpu.CompilerParams(vmem_limit_bytes=20 * 2**20),
        name="attend",
    )(me, ids, scale, kept, given, *pieces)


def project_kernel(core_ref, slots_ref, own_ref, other_ref, proj_ref, *outs):
    size = own_ref.shape[1]
    own_rows = pl.ds(pl.multiple_of(core_ref[0] * size, size), size)
    other_rows = pl.ds(pl.multiple_of((core_ref[0] ^ 1) * size, size), size)
    for slot, out in enumerate(outs):
        width = out.shape[1]
        columns = pl.ds(pl.multiple_of(slots_ref[slot] * width, width), width)
        out[...] = (dot(own_ref[...], proj_ref[own_rows, columns]) + dot(other_ref[...], proj_ref[other_rows, columns])).astype(BF16)


def project(core, slots, own, other, proj):
    ways = slots.shape[0]
    return pl.pallas_call(
        project_kernel,
        in_specs=[SMEM, SMEM] + [VMEM] * 3,
        out_specs=[VMEM] * ways,
        out_shape=[jax.ShapeDtypeStruct((own.shape[0], proj.shape[1] // ways), BF16)] * ways,
        compiler_params=pltpu.CompilerParams(vmem_limit_bytes=6 * 2**20),
        name="project",
    )(core, slots, own, other, proj)


def result_kernel(count, order_ref, own_ref, *refs):
    pieces, (result_ref, routed_ref) = refs[:count], refs[count:]
    total = own_ref[...].astype(F32) + sum(p[...].astype(F32) for p in pieces)
    result = total.astype(BF16)
    result_ref[...] = result
    routed_ref[...] = dot(order_ref[...], result).astype(BF16)


def finish_result(order, residual, pieces):
    shape = jax.ShapeDtypeStruct(residual.shape, BF16)
    return pl.pallas_call(
        functools.partial(result_kernel, len(pieces)),
        in_specs=[VMEM] * (2 + len(pieces)),
        out_specs=(VMEM, VMEM),
        out_shape=(shape, shape),
        compiler_params=pltpu.CompilerParams(vmem_limit_bytes=4 * 2**20),
        name="finish_result",
    )(order, residual, *pieces)


def bytes_kernel(cuts, counted_ref, result_ref, proj_ref, *refs):
    sources, (out_ref, held, sems) = refs[: sum(cuts)], refs[sum(cuts) :]
    count = len(cuts)
    copies = []
    for i, cut in enumerate(cuts):
        rows = held.shape[1] // cut
        for c in range(cut):
            at = len(copies)
            copies.append(pltpu.make_async_copy(sources[at], held.at[i, pl.ds(c * rows, rows)], sems.at[at]))
    for copy in copies:
        copy.start()
    rows = result_ref.shape[0]
    width = proj_ref.shape[0]
    own = out_ref.shape[0] // rows
    back = jnp.concatenate([dot(result_ref[:, b * width : (b + 1) * width], proj_ref[...]) for b in range(own)], axis=0)
    at = lax.broadcasted_iota(jnp.int32, (rows * own, rows * own), 0)
    to = lax.broadcasted_iota(jnp.int32, (rows * own, rows * own), 1)
    order = (to == (at % own) * rows + at // own).astype(F32).astype(BF16)
    for copy in copies:
        copy.wait()
    state = held[0].astype(F32)
    for i in range(1, count):
        state += jnp.where(counted_ref[i] != 0, held[i].astype(F32), 0.0)
    state = state.astype(BF16).astype(F32)
    out_ref[...] = dot(order, (state + back).astype(BF16)).astype(BF16)


def finish_bytes(counted, result, proj, pieces):
    shape = pieces[0][0].shape
    flat = [part for piece in pieces for part in piece]
    return pl.pallas_call(
        functools.partial(bytes_kernel, tuple(len(piece) for piece in pieces)),
        in_specs=[SMEM, VMEM, VMEM] + [pl.BlockSpec(memory_space=pl.ANY)] * len(flat),
        out_specs=VMEM,
        out_shape=jax.ShapeDtypeStruct(shape, BF16),
        scratch_shapes=[pltpu.VMEM((len(pieces), *shape), BF16), pltpu.SemaphoreType.DMA((len(flat),))],
        compiler_params=pltpu.CompilerParams(vmem_limit_bytes=16 * 2**20),
        name="finish_bytes",
    )(counted, result, proj, *flat)


def shift(value, axis, step):
    count = lax.axis_size(axis)
    return lax.ppermute(value, axis, [(i, (i + step) % count) for i in range(count)])


def scatter(chunks, axis):
    return [chunks[0]] + [shift(chunk, axis, step) for step, chunk in enumerate(chunks[1:], 1)]


def shift_slots(axis):
    count = lax.axis_size(axis)
    return ((lax.axis_index(axis) + jnp.arange(count)) % count).astype(jnp.int32)


def relay_slots(axis):
    me = lax.axis_index(axis)
    outer = (me == 0) | (me == 3)
    beside, across = me ^ 1, 3 - me
    return jnp.stack([me, jnp.where(outer, across, beside), jnp.where(outer, beside, across), me ^ 2]).astype(jnp.int32)


def relay_first(chunks, axis):
    swapped = lax.ppermute(chunks[1], axis, [(0, 1), (1, 0), (2, 3), (3, 2)])
    middle = lax.ppermute(chunks[2], axis, [(1, 2), (2, 1)])
    return swapped, middle


def relay_sum(chunks, swapped, axis):
    me = lax.axis_index(axis)
    relayed = jnp.where((me == 0) | (me == 3), 0.0, swapped.astype(F32))
    return (chunks[3].astype(F32) + relayed).astype(BF16)


def relay_inward(chunks, axis):
    return lax.ppermute(chunks[2], axis, [(0, 1), (3, 2)])


def relay_cross(sent, axis):
    return lax.ppermute(sent, axis, [(0, 2), (2, 0), (1, 3), (3, 1)])


def relay_counted(axis):
    me = lax.axis_index(axis)
    outer = ((me == 0) | (me == 3)).astype(jnp.int32)
    return jnp.stack([1 + 0 * outer, outer, 1 - outer, 1 - outer, 1 + 0 * outer])


def gather(value, axis):
    return [value] + [shift(value, axis, step) for step in range(1, lax.axis_size(axis))]


def swap_cores(value, axis):
    return lax.ppermute(value, axis, [(i, i ^ 1) for i in range(lax.axis_size(axis))])


def twin_ids(axis):
    count = lax.axis_size(axis)
    return ((lax.axis_index(axis) - 2 * jnp.arange(count // 2)) % count).astype(jnp.int32)


def owner_order(owners, source, patches):
    listed = lax.dynamic_index_in_dim(owners, source, 0, keepdims=False)
    count = listed.shape[0]
    block = patches // count
    index = jnp.arange(count, dtype=jnp.int32)
    before = (listed[None, :] < listed[:, None]) | (
        (listed[None, :] == listed[:, None]) & (index[None, :] < index[:, None])
    )
    slot = jnp.sum(before, axis=1).astype(jnp.int32)
    row = jnp.arange(patches, dtype=jnp.int32)
    spread = jnp.sum(jnp.where(row[:, None] // block == index[None, :], slot[None, :], 0), axis=1).astype(jnp.int32)
    place = spread * block + row % block
    return (row[:, None] == place[None, :]).astype(BF16)


def on_device(
    byte_in,
    local_gain,
    local_qkv,
    local_out,
    mlp_up,
    mlp_down,
    local_scale,
    patch_proj,
    global_gain,
    global_qkv,
    global_out,
    global_scale,
    back_proj,
    owners,
):
    patches, span, width = byte_in.shape
    ways = lax.axis_size("head")
    own = span // ways
    me = lax.axis_index("head").astype(jnp.int32)
    seq = lax.axis_index("seq").astype(jnp.int32)
    depth = global_qkv.shape[2] // global_scale.shape[0]

    line = ways == 4
    slots = jnp.stack([relay_slots("head") if line else shift_slots("head"), shift_slots("head")])
    parts, chunks = local_part(
        me.reshape(1),
        local_scale,
        slots,
        byte_in.reshape(-1, width),
        local_gain.reshape(1, -1),
        jnp.transpose(local_qkv, (1, 0, 2)),
        local_out,
        mlp_up,
        mlp_down,
        patch_proj,
        span,
    )
    residual = sum(p.astype(F32) for p in scatter(chunks, "head")).astype(BF16)
    weight, residual = lax.optimization_barrier((jnp.transpose(global_qkv, (1, 0, 2)), residual))
    shares = gather(residual, "head")
    ids = (me - jnp.arange(ways, dtype=jnp.int32)) % ways
    core = (seq % 2).reshape(1)
    kept, given = global_heads(depth, core, ids, global_gain.reshape(ways, 1, -1), shares, fetch(weight))
    received = swap_cores(given, "seq")
    parts, received = lax.optimization_barrier((parts, received))
    half = kept.shape[1] // 3
    keyed = jnp.concatenate([kept[:, half:], received[:, half:]], axis=0)
    pieces = [shift(keyed, "seq", 2 * step) for step in range(1, lax.axis_size("seq") // 2)]
    if line:
        swapped, middle = relay_first(parts, "head")
        sent = relay_sum(parts, swapped, "head")
        cut = sent.shape[0] // 2
        early, late = sent[:cut], sent[cut:]
        kept, early, middle = lax.optimization_barrier((kept, early, middle))
        early = relay_cross(early, "head")
    own_heads, other_heads = attend(depth, seq.reshape(1), twin_ids("seq"), global_scale, kept, received, pieces)
    update = project(core, slots[1], own_heads, swap_cores(other_heads, "seq"), global_out)
    updates = scatter(update, "head")
    if line:
        updates, early, parts, late = lax.optimization_barrier((updates, early, parts, late))
        counted = relay_counted("head")
        byte_pieces = [(parts[0],), (swapped,), (middle,), (relay_inward(parts, "head"),), (early, relay_cross(late, "head"))]
    else:
        counted = jnp.ones((ways,), jnp.int32)
        byte_pieces = [(part,) for part in scatter(parts, "head")]
    result, routed = finish_result(owner_order(owners, seq, patches), residual, updates)
    global_state = lax.all_to_all(routed, "seq", split_axis=0, concat_axis=0, tiled=True)
    byte_out = finish_bytes(counted, result, back_proj, byte_pieces)
    return byte_out.reshape(patches, own, width), global_state


def solution(mesh):
    placed = (
        P("seq", None, None),
        P(),
        P(None, None, "head"),
        P("head", None),
        P(None, "head"),
        P("head", None),
        P("head"),
        P(),
        P(),
        P(None, None, "head"),
        P("head", None),
        P("head"),
        P(),
        P(),
    )
    return jax.shard_map(
        on_device,
        mesh=mesh,
        in_specs=placed,
        out_specs=(P("seq", "head", None), P("seq", "head")),
        check_vma=False,
    )
```

```python
import functools
import math

import jax
import jax.numpy as jnp
from jax import lax
from jax.experimental import pallas as pl
from jax.experimental.pallas import tpu as pltpu
from jax.sharding import PartitionSpec as P

EPSILON = 1e-06
NEGATIVE = -1e30
F32 = jnp.float32
BF16 = jnp.bfloat16
BRIEF = pl.CostEstimate(flops=1, bytes_accessed=1, transcendentals=0)
VMEM = pl.BlockSpec(memory_space=pltpu.VMEM)
HBM = pl.BlockSpec(memory_space=pltpu.HBM)
SMEM = pl.BlockSpec(memory_space=pltpu.SMEM)


def dot(left, right):
    return jnp.dot(left, right, preferred_element_type=F32)


def dot_t(left, right):
    return lax.dot_general(left, right, (((1,), (1,)), ((), ())), preferred_element_type=F32)


def unit(values):
    return (values * lax.rsqrt(jnp.mean(values * values, axis=-1, keepdims=True) + EPSILON)).astype(BF16)


def gelu(values):
    inner = math.sqrt(2.0 / math.pi) * (values + 0.044715 * (values * values * values))
    return 0.5 * values * (1.0 + jnp.tanh(inner))


def local_kernel(span, piece, step, me_ref, scale_ref, slots_ref, gain_ref, x_hbm, *refs):
    ways = slots_ref.shape[0]
    sources, parts, shares = refs[:5], refs[5 : 5 + ways], refs[5 + ways : 5 + 2 * ways]
    x_ref, part_ref, share_ref = refs[5 + 2 * ways : 8 + 2 * ways]
    held, (in_sem, x_sem, part_sem) = refs[8 + 2 * ways : 13 + 2 * ways], refs[13 + 2 * ways :]
    patches = share_ref.shape[1]
    width = x_ref.shape[1]
    own = span // ways
    rows = piece * span
    pieces = patches // piece
    loads = [pltpu.make_async_copy(s, h, in_sem.at[i]) for i, (s, h) in enumerate(zip(sources, held))]
    cuts = [slice(i * rows, (i + 1) * rows) for i in range(pieces)]
    x_loads = [pltpu.make_async_copy(x_hbm.at[pl.ds(c.start, rows)], x_ref.at[pl.ds(c.start, rows)], x_sem.at[i]) for i, c in enumerate(cuts)]
    for copy in x_loads + loads:
        copy.start()
    qkv_ref, up_ref, out_ref, down_ref, proj_ref = held
    at = lax.broadcasted_iota(jnp.int32, (rows, rows), 0)
    to = lax.broadcasted_iota(jnp.int32, (rows, rows), 1)
    order = (to == (at % piece) * span + at // piece).astype(F32).astype(BF16)
    kept = lax.broadcasted_iota(jnp.int32, (rows, 1), 0) // piece // own == me_ref[0]
    xs, normed = [], []
    for copy in x_loads + loads:
        copy.wait()
    for i, cut in enumerate(cuts):
        x = dot(order, x_ref[cut])
        xs.append(jnp.where(kept, x, 0.0).astype(BF16))
        factor = lax.rsqrt(jnp.mean(x * x, axis=-1, keepdims=True) + EPSILON)
        normed.append((x * factor * gain_ref[...]).astype(BF16))
    xs, normed = jnp.concatenate(xs, axis=0), jnp.concatenate(normed, axis=0)
    query, key, value = (dot(normed, qkv_ref[i]) for i in range(3))
    seen = (at % piece == to % piece) & (to <= at)
    heads = scale_ref.shape[0]
    depth = query.shape[1] // heads
    attended = []
    for cut in cuts:
        columns = []
        for h in range(heads):
            head = slice(h * depth, (h + 1) * depth)
            scores = dot_t(unit(query[cut, head]), unit(key[cut, head])) * (scale_ref[h] / math.sqrt(depth))
            scores = jnp.where(seen, scores, NEGATIVE)
            weights = jnp.exp(scores - jnp.max(scores, axis=-1, keepdims=True))
            total = jnp.sum(weights, axis=-1, keepdims=True)
            columns.append((dot(weights.astype(BF16), value[cut, head].astype(BF16)) / total).astype(BF16))
        attended.append(jnp.concatenate(columns, axis=1))
    attended = jnp.concatenate(attended, axis=0)
    act = gelu(dot(normed, up_ref[...])).astype(BF16)
    mixed = jnp.concatenate([attended, act], axis=1)
    share = 0.0
    stores = []
    for c in range(0, width, step):
        columns = slice(c, c + step)
        partial = dot(mixed, jnp.concatenate([out_ref[:, columns], down_ref[:, columns]], axis=0))
        partial = (partial + xs[:, columns].astype(F32)).astype(BF16)
        for i, cut in enumerate(cuts):
            for b in range(span):
                put = (b % own) * patches + i * piece
                part_ref[b // own, put : put + piece, columns] = partial[cut][b * piece : (b + 1) * piece]
        for slot, part in enumerate(parts):
            source = part_ref.at[slots_ref[slot], :, pl.ds(c, step)]
            stores.append(pltpu.make_async_copy(source, part.at[:, pl.ds(c, step)], part_sem.at[len(stores)]))
            stores[-1].start()
        share += dot(partial, proj_ref[columns])
    share = share.astype(BF16)
    size = share.shape[1]
    for i, cut in enumerate(cuts):
        for b in range(span):
            put = slice((b % own) * size, (b % own + 1) * size)
            share_ref[b // own, i * piece : (i + 1) * piece, put] = share[cut][b * piece : (b + 1) * piece]
    for slot, out in enumerate(shares):
        out[...] = share_ref[slots_ref[slot]]
    for copy in stores:
        copy.wait()


def local_part(me, scale, slots, x, gain, qkv, out, up, down, proj, span):
    rows, width = x.shape
    patches = rows // span
    ways = slots.shape[0]
    own = span // ways
    weights = (qkv, up, out, down, proj)
    piece = math.gcd(patches, 32)
    step = math.gcd(width, 1024)
    part = (own * patches, width)
    share = (patches, own * proj.shape[1])
    outs = pl.pallas_call(
        functools.partial(local_kernel, span, piece, step),
        in_specs=[SMEM, SMEM, SMEM, VMEM] + [HBM] * (1 + len(weights)),
        out_specs=[HBM] * ways + [VMEM] * ways,
        out_shape=[jax.ShapeDtypeStruct(part, BF16)] * ways + [pltpu.VMEM(share, BF16)] * ways,
        scratch_shapes=[pltpu.VMEM(x.shape, BF16), pltpu.VMEM((ways, *part), BF16), pltpu.VMEM((ways, *share), BF16)]
        + [pltpu.VMEM(w.shape, w.dtype) for w in weights]
        + [
            pltpu.SemaphoreType.DMA((len(weights),)),
            pltpu.SemaphoreType.DMA((patches // piece,)),
            pltpu.SemaphoreType.DMA((ways * (width // step),)),
        ],
        compiler_params=pltpu.CompilerParams(vmem_limit_bytes=60 * 2**20),
        name="local_part",
    )(me, scale, slots, gain, x, *weights)
    return outs[:ways], outs[ways:]


def fetch_kernel(source, held, sems):
    parts = source.shape[0]
    copies = [pltpu.make_async_copy(source.at[i], held.at[i], sems.at[i]) for i in range(parts)]
    for copy in copies:
        copy.start()
    for copy in copies:
        copy.wait()


def fetch(weight):
    return pl.pallas_call(
        fetch_kernel,
        in_specs=[HBM],
        out_specs=VMEM,
        out_shape=pltpu.VMEM(weight.shape, weight.dtype),
        scratch_shapes=[pltpu.SemaphoreType.DMA((weight.shape[0],))],
        compiler_params=pltpu.CompilerParams(vmem_limit_bytes=50 * 2**20),
        name="fetch",
    )(weight)


def heads_kernel(depth, core_ref, ids_ref, gain_ref, *refs):
    ways = gain_ref.shape[0]
    shares, weight, outs = refs[:ways], refs[ways], refs[ways + 1 :]
    width = shares[0].shape[1]
    values = [s[...].astype(F32) for s in shares]
    square = sum(jnp.sum(v * v, axis=-1, keepdims=True) for v in values)
    factor = lax.rsqrt(square / (ways * width) + EPSILON)
    normed = [(v * factor * gain_ref[ids_ref[c]]).astype(BF16) for c, v in enumerate(values)]
    size = outs[0].shape[1] // 3
    for kind in range(3):
        for i, out in ((1, outs[1]), (0, outs[0])):
            columns = pl.ds(pl.multiple_of((core_ref[0] ^ i) * size, size), size)
            mixed = sum(
                dot(n, weight[kind, pl.ds(pl.multiple_of(ids_ref[c] * width, width), width), columns])
                for c, n in enumerate(normed)
            )
            if kind < 2:
                mixed = jnp.concatenate([unit(mixed[:, c : c + depth]) for c in range(0, size, depth)], axis=1)
            out[:, kind * size : (kind + 1) * size] = mixed.astype(BF16)


def global_heads(depth, core, ids, gain, shares, qkv):
    shape = jax.ShapeDtypeStruct((shares[0].shape[0], 3 * qkv.shape[2] // 2), BF16)
    return pl.pallas_call(
        functools.partial(heads_kernel, depth),
        in_specs=[SMEM, SMEM] + [VMEM] * (2 + len(shares)),
        out_specs=(VMEM, VMEM),
        out_shape=(shape, shape),
        compiler_params=pltpu.CompilerParams(vmem_limit_bytes=8 * 2**20),
        name="global_heads",
    )(core, ids, gain, *shares, qkv)


def attend_kernel(depth, me_ref, ids_ref, scale_ref, kept_ref, given_ref, *refs):
    pieces, (own_ref, other_ref) = refs[:-2], refs[-2:]
    rows = kept_ref.shape[0]
    size = own_ref.shape[1]
    heads = size // depth
    me = me_ref[0]

    def places(index, shape, axis):
        row = lax.broadcasted_iota(jnp.int32, shape, axis)
        return jnp.where(row < rows, index * rows + row, (index ^ 1) * rows + row - rows)

    at = places(me, (2 * rows, 1), 0)
    seen = [places(i, (1, 2 * rows), 1) <= at for i in [me] + [ids_ref[p + 1] for p in range(len(pieces))]]
    own = jnp.concatenate([kept_ref[...], given_ref[...]], axis=0)
    query = own[:, :size]
    pieces = [own[:, size:]] + [p[...] for p in pieces]
    for h in range(heads):
        cut = slice(h * depth, (h + 1) * depth)
        factor = scale_ref[(me % 2) * heads + h] / math.sqrt(depth)
        scores = [jnp.where(s, dot_t(query[:, cut], p[:, cut]) * factor, NEGATIVE) for s, p in zip(seen, pieces)]
        top = functools.reduce(jnp.maximum, [jnp.max(s, axis=-1, keepdims=True) for s in scores])
        weights = [jnp.exp(s - top) for s in scores]
        total = sum(jnp.sum(w, axis=-1, keepdims=True) for w in weights)
        values = slice(size + h * depth, size + (h + 1) * depth)
        summed = sum(dot(w.astype(BF16), p[:, values]) for w, p in zip(weights, pieces))
        attended = (summed / total).astype(BF16)
        own_ref[:, cut] = attended[:rows]
        other_ref[:, cut] = attended[rows:]


def attend(depth, me, ids, scale, kept, given, pieces):
    rows = kept.shape[0]
    shape = jax.ShapeDtypeStruct((rows, kept.shape[1] // 3), BF16)
    return pl.pallas_call(
        functools.partial(attend_kernel, depth),
        in_specs=[SMEM, SMEM, SMEM] + [VMEM] * (2 + len(pieces)),
        out_specs=(VMEM, VMEM),
        out_shape=(shape, shape),
        compiler_params=pltpu.CompilerParams(vmem_limit_bytes=20 * 2**20),
        cost_estimate=BRIEF,
        name="attend",
    )(me, ids, scale, kept, given, *pieces)


def project_kernel(core_ref, slots_ref, own_ref, other_ref, proj_ref, *outs):
    size = own_ref.shape[1]
    own_rows = pl.ds(pl.multiple_of(core_ref[0] * size, size), size)
    other_rows = pl.ds(pl.multiple_of((core_ref[0] ^ 1) * size, size), size)
    for slot, out in enumerate(outs):
        width = out.shape[1]
        columns = pl.ds(pl.multiple_of(slots_ref[slot] * width, width), width)
        out[...] = (dot(own_ref[...], proj_ref[own_rows, columns]) + dot(other_ref[...], proj_ref[other_rows, columns])).astype(BF16)


def project(core, slots, own, other, proj):
    ways = slots.shape[0]
    return pl.pallas_call(
        project_kernel,
        in_specs=[SMEM, SMEM] + [VMEM] * 3,
        out_specs=[VMEM] * ways,
        out_shape=[jax.ShapeDtypeStruct((own.shape[0], proj.shape[1] // ways), BF16)] * ways,
        compiler_params=pltpu.CompilerParams(vmem_limit_bytes=6 * 2**20),
        cost_estimate=BRIEF,
        name="project",
    )(core, slots, own, other, proj)


def result_kernel(count, order_ref, own_ref, *refs):
    pieces, (result_ref, routed_ref) = refs[:count], refs[count:]
    total = own_ref[...].astype(F32) + sum(p[...].astype(F32) for p in pieces)
    result = total.astype(BF16)
    result_ref[...] = result
    routed_ref[...] = dot(order_ref[...], result).astype(BF16)


def finish_result(order, residual, pieces):
    shape = jax.ShapeDtypeStruct(residual.shape, BF16)
    return pl.pallas_call(
        functools.partial(result_kernel, len(pieces)),
        in_specs=[VMEM] * (2 + len(pieces)),
        out_specs=(VMEM, VMEM),
        out_shape=(shape, shape),
        compiler_params=pltpu.CompilerParams(vmem_limit_bytes=4 * 2**20),
        cost_estimate=BRIEF,
        name="finish_result",
    )(order, residual, *pieces)


def bytes_kernel(count, result_ref, proj_ref, *refs):
    sources, (out_ref, held, sems) = refs[:count], refs[count:]
    copies = [pltpu.make_async_copy(p, held.at[i], sems.at[i]) for i, p in enumerate(sources)]
    for copy in copies:
        copy.start()
    rows = result_ref.shape[0]
    width = proj_ref.shape[0]
    own = out_ref.shape[0] // rows
    back = jnp.concatenate([dot(result_ref[:, b * width : (b + 1) * width], proj_ref[...]) for b in range(own)], axis=0)
    at = lax.broadcasted_iota(jnp.int32, (rows * own, rows * own), 0)
    to = lax.broadcasted_iota(jnp.int32, (rows * own, rows * own), 1)
    order = (to == (at % own) * rows + at // own).astype(F32).astype(BF16)
    for copy in copies:
        copy.wait()
    state = sum(held[i].astype(F32) for i in range(count)).astype(BF16).astype(F32)
    out_ref[...] = dot(order, (state + back).astype(BF16)).astype(BF16)


def finish_bytes(result, proj, pieces):
    shape = pieces[0].shape
    return pl.pallas_call(
        functools.partial(bytes_kernel, len(pieces)),
        in_specs=[VMEM, VMEM] + [pl.BlockSpec(memory_space=pl.ANY)] * len(pieces),
        out_specs=VMEM,
        out_shape=jax.ShapeDtypeStruct(shape, BF16),
        scratch_shapes=[pltpu.VMEM((len(pieces), *shape), BF16), pltpu.SemaphoreType.DMA((len(pieces),))],
        compiler_params=pltpu.CompilerParams(vmem_limit_bytes=16 * 2**20),
        cost_estimate=BRIEF,
        name="finish_bytes",
    )(result, proj, *pieces)


def shift(value, axis, step):
    count = lax.axis_size(axis)
    return lax.ppermute(value, axis, [(i, (i + step) % count) for i in range(count)])


def scatter(chunks, axis):
    return [chunks[0]] + [shift(chunk, axis, step) for step, chunk in enumerate(chunks[1:], 1)]


def shift_slots(axis):
    count = lax.axis_size(axis)
    return ((lax.axis_index(axis) + jnp.arange(count)) % count).astype(jnp.int32)


def gather(value, axis):
    return [value] + [shift(value, axis, step) for step in range(1, lax.axis_size(axis))]


def swap_cores(value, axis):
    return lax.ppermute(value, axis, [(i, i ^ 1) for i in range(lax.axis_size(axis))])


def twin_ids(axis):
    count = lax.axis_size(axis)
    return ((lax.axis_index(axis) - 2 * jnp.arange(count // 2)) % count).astype(jnp.int32)


def owner_order(owners, source, patches):
    listed = lax.dynamic_index_in_dim(owners, source, 0, keepdims=False)
    count = listed.shape[0]
    block = patches // count
    index = jnp.arange(count, dtype=jnp.int32)
    before = (listed[None, :] < listed[:, None]) | (
        (listed[None, :] == listed[:, None]) & (index[None, :] < index[:, None])
    )
    slot = jnp.sum(before, axis=1).astype(jnp.int32)
    row = jnp.arange(patches, dtype=jnp.int32)
    spread = jnp.sum(jnp.where(row[:, None] // block == index[None, :], slot[None, :], 0), axis=1).astype(jnp.int32)
    place = spread * block + row % block
    return (row[:, None] == place[None, :]).astype(BF16)


def on_device(
    byte_in,
    local_gain,
    local_qkv,
    local_out,
    mlp_up,
    mlp_down,
    local_scale,
    patch_proj,
    global_gain,
    global_qkv,
    global_out,
    global_scale,
    back_proj,
    owners,
):
    patches, span, width = byte_in.shape
    ways = lax.axis_size("head")
    own = span // ways
    me = lax.axis_index("head").astype(jnp.int32)
    seq = lax.axis_index("seq").astype(jnp.int32)
    depth = global_qkv.shape[2] // global_scale.shape[0]

    slots = shift_slots("head")
    parts, chunks = local_part(
        me.reshape(1),
        local_scale,
        slots,
        byte_in.reshape(-1, width),
        local_gain.reshape(1, -1),
        jnp.transpose(local_qkv, (1, 0, 2)),
        local_out,
        mlp_up,
        mlp_down,
        patch_proj,
        span,
    )
    residual = sum(p.astype(F32) for p in scatter(chunks, "head")).astype(BF16)
    weight, residual = lax.optimization_barrier((jnp.transpose(global_qkv, (1, 0, 2)), residual))
    shares = gather(residual, "head")
    ids = (me - jnp.arange(ways, dtype=jnp.int32)) % ways
    core = (seq % 2).reshape(1)
    kept, given = global_heads(depth, core, ids, global_gain.reshape(ways, 1, -1), shares, fetch(weight))
    received = swap_cores(given, "seq")
    parts, received = lax.optimization_barrier((parts, received))
    half = kept.shape[1] // 3
    keyed = jnp.concatenate([kept[:, half:], received[:, half:]], axis=0)
    pieces = [shift(keyed, "seq", 2 * step) for step in range(1, lax.axis_size("seq") // 2)]
    parts = scatter(parts, "head")
    own_heads, other_heads = attend(depth, seq.reshape(1), twin_ids("seq"), global_scale, kept, received, pieces)
    other_heads, parts[1] = lax.optimization_barrier((swap_cores(other_heads, "seq"), parts[1]))
    updates = scatter(project(core, slots, own_heads, other_heads, global_out), "head")
    updates, parts[2] = lax.optimization_barrier((updates, parts[2]))
    result, routed = finish_result(owner_order(owners, seq, patches), residual, updates)
    global_state = lax.all_to_all(routed, "seq", split_axis=0, concat_axis=0, tiled=True)
    byte_out = finish_bytes(result, back_proj, parts)
    return byte_out.reshape(patches, own, width), global_state


def solution(mesh):
    placed = (
        P("seq", None, None),
        P(),
        P(None, None, "head"),
        P("head", None),
        P(None, "head"),
        P("head", None),
        P("head"),
        P(),
        P(),
        P(None, None, "head"),
        P("head", None),
        P("head"),
        P(),
        P(),
    )
    return jax.shard_map(
        on_device,
        mesh=mesh,
        in_specs=placed,
        out_specs=(P("seq", "head", None), P("seq", "head")),
        check_vma=False,
    )
```

```python
import functools
import math

import jax
import jax.numpy as jnp
from jax import lax
from jax.experimental import pallas as pl
from jax.experimental.pallas import tpu as pltpu
from jax.sharding import PartitionSpec as P

EPSILON = 1e-06
NEGATIVE = -1e30
F32 = jnp.float32
BF16 = jnp.bfloat16
BRIEF = pl.CostEstimate(flops=1, bytes_accessed=1, transcendentals=0)
VMEM = pl.BlockSpec(memory_space=pltpu.VMEM)
HBM = pl.BlockSpec(memory_space=pltpu.HBM)
SMEM = pl.BlockSpec(memory_space=pltpu.SMEM)


def dot(left, right):
    return jnp.dot(left, right, preferred_element_type=F32)


def dot_t(left, right):
    return lax.dot_general(left, right, (((1,), (1,)), ((), ())), preferred_element_type=F32)


def unit(values):
    return (values * lax.rsqrt(jnp.mean(values * values, axis=-1, keepdims=True) + EPSILON)).astype(BF16)


def gelu(values):
    inner = math.sqrt(2.0 / math.pi) * (values + 0.044715 * (values * values * values))
    return 0.5 * values * (1.0 + jnp.tanh(inner))


def local_kernel(span, ways, piece, last, scale_ref, gain_ref, x_hbm, *refs):
    sources, parts, others = refs[:5], refs[5 : 5 + ways], refs[5 + ways : -11]
    held, (x_ref, part_ref, share_ref, in_sem, x_sem, part_sem) = refs[-11:-6], refs[-6:]
    patches = share_ref.shape[1]
    own = span // ways
    rows = piece * span
    pieces = patches // piece
    cuts = [slice(i * rows, (i + 1) * rows) for i in range(pieces)]
    skip = x_ref.shape[0] if last else 0
    loads = [
        pltpu.make_async_copy(x_hbm.at[pl.ds(skip + c.start, rows)], x_ref.at[pl.ds(c.start, rows)], x_sem.at[i])
        for i, c in enumerate(cuts)
    ]
    loads += [pltpu.make_async_copy(s, h, in_sem.at[i]) for i, (s, h) in enumerate(zip(sources, held))]
    for copy in loads:
        copy.start()
    me = lax.axis_index("head")
    at = lax.broadcasted_iota(jnp.int32, (rows, rows), 0)
    to = lax.broadcasted_iota(jnp.int32, (rows, rows), 1)
    order = (to == (at % piece) * span + at // piece).astype(F32).astype(BF16)
    kept = lax.broadcasted_iota(jnp.int32, (rows, 1), 0) // piece // own == me
    for copy in loads:
        copy.wait()
    qkv_ref, up_ref, out_ref, down_ref, proj_ref = held
    xs, normed = [], []
    for cut in cuts:
        x = dot(order, x_ref[cut])
        xs.append(jnp.where(kept, x, 0.0).astype(BF16))
        factor = lax.rsqrt(jnp.mean(x * x, axis=-1, keepdims=True) + EPSILON)
        normed.append((x * factor * gain_ref[...]).astype(BF16))
    xs, normed = jnp.concatenate(xs, axis=0), jnp.concatenate(normed, axis=0)
    query, key, value = (dot(normed, qkv_ref[i]) for i in range(3))
    seen = (at % piece == to % piece) & (to <= at)
    heads = scale_ref.shape[0]
    depth = query.shape[1] // heads
    attended = []
    for cut in cuts:
        columns = []
        for h in range(heads):
            head = slice(h * depth, (h + 1) * depth)
            scores = dot_t(unit(query[cut, head]), unit(key[cut, head])) * (scale_ref[h] / math.sqrt(depth))
            scores = jnp.where(seen, scores, NEGATIVE)
            weights = jnp.exp(scores - jnp.max(scores, axis=-1, keepdims=True))
            total = jnp.sum(weights, axis=-1, keepdims=True)
            columns.append((dot(weights.astype(BF16), value[cut, head].astype(BF16)) / total).astype(BF16))
        attended.append(jnp.concatenate(columns, axis=1))
    act = gelu(dot(normed, up_ref[...])).astype(BF16)
    mixed = jnp.concatenate([jnp.concatenate(attended, axis=0), act], axis=1)
    partial = dot(mixed, jnp.concatenate([out_ref[...], down_ref[...]], axis=0)) + xs.astype(F32)
    partial = partial.astype(BF16)
    for i, cut in enumerate(cuts):
        for b in range(span):
            put = (b % own) * patches + i * piece
            part_ref[b // own, put : put + piece] = partial[cut][b * piece : (b + 1) * piece]
    stores = []
    for slot, part in enumerate(parts):
        stores.append(pltpu.make_async_copy(part_ref.at[lax.rem(me + slot, ways)], part, part_sem.at[slot]))
        stores[-1].start()
    if last:
        share = dot(partial, proj_ref[...]).astype(BF16)
        size = share.shape[1]
        for i, cut in enumerate(cuts):
            for b in range(span):
                put = slice((b % own) * size, (b % own + 1) * size)
                share_ref[b // own, i * piece : (i + 1) * piece, put] = share[cut][b * piece : (b + 1) * piece]
        for slot, out in enumerate(others):
            out[...] = share_ref[lax.rem(me + slot, ways)]
    for copy in stores:
        copy.wait()


def local_part(scale, x, gain, weights, span, ways, last):
    rows, width = x.shape[0] // 2, x.shape[1]
    patches = rows // span
    own = span // ways
    piece = math.gcd(patches, 32)
    part = (own * patches, width)
    share = (patches, own * weights[-1].shape[1])
    others = [pltpu.VMEM(share, BF16)] * (ways if last else 0)
    outs = pl.pallas_call(
        functools.partial(local_kernel, span, ways, piece, last),
        in_specs=[SMEM, VMEM, HBM] + [HBM] * len(weights),
        out_specs=[HBM] * ways + [VMEM] * len(others),
        out_shape=[jax.ShapeDtypeStruct(part, BF16)] * ways + others,
        scratch_shapes=[pltpu.VMEM(w.shape, w.dtype) for w in weights]
        + [
            pltpu.VMEM((rows, width), BF16),
            pltpu.VMEM((ways, *part), BF16),
            pltpu.VMEM((ways, *share), BF16),
            pltpu.SemaphoreType.DMA((len(weights),)),
            pltpu.SemaphoreType.DMA((patches // piece,)),
            pltpu.SemaphoreType.DMA((ways,)),
        ],
        compiler_params=pltpu.CompilerParams(vmem_limit_bytes=60 * 2**20),
        cost_estimate=pl.CostEstimate(flops=8 * rows * width * width, bytes_accessed=10 * 2**20, transcendentals=rows * width),
        name="local_part",
    )(scale, gain, x, *weights)
    return list(outs[:ways]), list(outs[ways:])


def state_kernel(count, proj_ref, *refs):
    pieces, (state_ref, share_ref) = refs[:count], refs[count:]
    state = sum(p[...].astype(F32) for p in pieces).astype(BF16)
    state_ref[...] = state
    patches = share_ref.shape[0]
    width = proj_ref.shape[1]
    for b in range(state.shape[0] // patches):
        share_ref[:, b * width : (b + 1) * width] = dot(state[b * patches : (b + 1) * patches], proj_ref[...]).astype(BF16)


def finish_state(proj, pieces, own):
    rows, width = pieces[0].shape
    return pl.pallas_call(
        functools.partial(state_kernel, len(pieces)),
        in_specs=[VMEM] * (1 + len(pieces)),
        out_specs=(VMEM, VMEM),
        out_shape=(
            jax.ShapeDtypeStruct((rows, width), BF16),
            jax.ShapeDtypeStruct((rows // own, own * proj.shape[1]), BF16),
        ),
        compiler_params=pltpu.CompilerParams(vmem_limit_bytes=8 * 2**20),
        name="finish_state",
    )(proj, *pieces)


def fetch_kernel(source, held, sems):
    parts = source.shape[0]
    copies = [pltpu.make_async_copy(source.at[i], held.at[i], sems.at[i]) for i in range(parts)]
    for copy in copies:
        copy.start()
    for copy in copies:
        copy.wait()


def fetch(weight):
    return pl.pallas_call(
        fetch_kernel,
        in_specs=[HBM],
        out_specs=VMEM,
        out_shape=pltpu.VMEM(weight.shape, weight.dtype),
        scratch_shapes=[pltpu.SemaphoreType.DMA((weight.shape[0],))],
        compiler_params=pltpu.CompilerParams(vmem_limit_bytes=50 * 2**20),
        name="fetch",
    )(weight)


def heads_kernel(depth, core_ref, ids_ref, gain_ref, *refs):
    ways = gain_ref.shape[0]
    shares, weight, outs = refs[:ways], refs[ways], refs[ways + 1 :]
    width = shares[0].shape[1]
    values = [s[...].astype(F32) for s in shares]
    square = sum(jnp.sum(v * v, axis=-1, keepdims=True) for v in values)
    factor = lax.rsqrt(square / (ways * width) + EPSILON)
    normed = [(v * factor * gain_ref[ids_ref[c]]).astype(BF16) for c, v in enumerate(values)]
    size = outs[0].shape[1] // 3
    for kind in range(3):
        for i, out in ((1, outs[1]), (0, outs[0])):
            columns = pl.ds(pl.multiple_of((core_ref[0] ^ i) * size, size), size)
            mixed = sum(
                dot(n, weight[kind, pl.ds(pl.multiple_of(ids_ref[c] * width, width), width), columns])
                for c, n in enumerate(normed)
            )
            if kind < 2:
                mixed = jnp.concatenate([unit(mixed[:, c : c + depth]) for c in range(0, size, depth)], axis=1)
            out[:, kind * size : (kind + 1) * size] = mixed.astype(BF16)


def global_heads(depth, core, ids, gain, shares, qkv):
    shape = jax.ShapeDtypeStruct((shares[0].shape[0], 3 * qkv.shape[2] // 2), BF16)
    return pl.pallas_call(
        functools.partial(heads_kernel, depth),
        in_specs=[SMEM, SMEM] + [VMEM] * (2 + len(shares)),
        out_specs=(VMEM, VMEM),
        out_shape=(shape, shape),
        compiler_params=pltpu.CompilerParams(vmem_limit_bytes=8 * 2**20),
        name="global_heads",
    )(core, ids, gain, *shares, qkv)


def attend_kernel(depth, me_ref, ids_ref, scale_ref, kept_ref, given_ref, *refs):
    pieces, (own_ref, other_ref) = refs[:-2], refs[-2:]
    rows = kept_ref.shape[0]
    size = own_ref.shape[1]
    heads = size // depth
    me = me_ref[0]

    def places(index, shape, axis):
        row = lax.broadcasted_iota(jnp.int32, shape, axis)
        return jnp.where(row < rows, index * rows + row, (index ^ 1) * rows + row - rows)

    at = places(me, (2 * rows, 1), 0)
    seen = [places(i, (1, 2 * rows), 1) <= at for i in [me] + [ids_ref[p + 1] for p in range(len(pieces))]]
    own = jnp.concatenate([kept_ref[...], given_ref[...]], axis=0)
    query = own[:, :size]
    pieces = [own[:, size:]] + [p[...] for p in pieces]
    for h in range(heads):
        cut = slice(h * depth, (h + 1) * depth)
        factor = scale_ref[(me % 2) * heads + h] / math.sqrt(depth)
        scores = [jnp.where(s, dot_t(query[:, cut], p[:, cut]) * factor, NEGATIVE) for s, p in zip(seen, pieces)]
        top = functools.reduce(jnp.maximum, [jnp.max(s, axis=-1, keepdims=True) for s in scores])
        weights = [jnp.exp(s - top) for s in scores]
        total = sum(jnp.sum(w, axis=-1, keepdims=True) for w in weights)
        values = slice(size + h * depth, size + (h + 1) * depth)
        summed = sum(dot(w.astype(BF16), p[:, values]) for w, p in zip(weights, pieces))
        attended = (summed / total).astype(BF16)
        own_ref[:, cut] = attended[:rows]
        other_ref[:, cut] = attended[rows:]


def attend(depth, me, ids, scale, kept, given, pieces):
    rows = kept.shape[0]
    shape = jax.ShapeDtypeStruct((rows, kept.shape[1] // 3), BF16)
    return pl.pallas_call(
        functools.partial(attend_kernel, depth),
        in_specs=[SMEM, SMEM, SMEM] + [VMEM] * (2 + len(pieces)),
        out_specs=(VMEM, VMEM),
        out_shape=(shape, shape),
        compiler_params=pltpu.CompilerParams(vmem_limit_bytes=20 * 2**20),
        cost_estimate=BRIEF,
        name="attend",
    )(me, ids, scale, kept, given, *pieces)


def project_kernel(core_ref, slots_ref, own_ref, other_ref, proj_ref, *outs):
    size = own_ref.shape[1]
    own_rows = pl.ds(pl.multiple_of(core_ref[0] * size, size), size)
    other_rows = pl.ds(pl.multiple_of((core_ref[0] ^ 1) * size, size), size)
    for slot, out in enumerate(outs):
        width = out.shape[1]
        columns = pl.ds(pl.multiple_of(slots_ref[slot] * width, width), width)
        out[...] = (dot(own_ref[...], proj_ref[own_rows, columns]) + dot(other_ref[...], proj_ref[other_rows, columns])).astype(BF16)


def project(core, slots, own, other, proj):
    ways = slots.shape[0]
    return pl.pallas_call(
        project_kernel,
        in_specs=[SMEM, SMEM] + [VMEM] * 3,
        out_specs=[VMEM] * ways,
        out_shape=[jax.ShapeDtypeStruct((own.shape[0], proj.shape[1] // ways), BF16)] * ways,
        compiler_params=pltpu.CompilerParams(vmem_limit_bytes=6 * 2**20),
        cost_estimate=BRIEF,
        name="project",
    )(core, slots, own, other, proj)


def result_kernel(count, order_ref, own_ref, *refs):
    pieces, (result_ref, routed_ref) = refs[:count], refs[count:]
    total = own_ref[...].astype(F32) + sum(p[...].astype(F32) for p in pieces)
    result = total.astype(BF16)
    result_ref[...] = result
    routed_ref[...] = dot(order_ref[...], result).astype(BF16)


def finish_result(order, residual, pieces):
    shape = jax.ShapeDtypeStruct(residual.shape, BF16)
    return pl.pallas_call(
        functools.partial(result_kernel, len(pieces)),
        in_specs=[VMEM] * (2 + len(pieces)),
        out_specs=(VMEM, VMEM),
        out_shape=(shape, shape),
        compiler_params=pltpu.CompilerParams(vmem_limit_bytes=4 * 2**20),
        cost_estimate=BRIEF,
        name="finish_result",
    )(order, residual, *pieces)


def bytes_kernel(count, result_ref, proj_ref, *refs):
    sources, (out_ref, held, sems) = refs[:count], refs[count:]
    copies = [pltpu.make_async_copy(p, held.at[i], sems.at[i]) for i, p in enumerate(sources)]
    for copy in copies:
        copy.start()
    rows = result_ref.shape[0]
    half = rows // 2
    width = proj_ref.shape[0]
    own = out_ref.shape[0] // rows
    back = [dot(result_ref[:, b * width : (b + 1) * width], proj_ref[...]) for b in range(own)]
    back = jnp.concatenate([b[:half] for b in back] + [b[half:] for b in back], axis=0)
    at = lax.broadcasted_iota(jnp.int32, (rows * own, rows * own), 0)
    to = lax.broadcasted_iota(jnp.int32, (rows * own, rows * own), 1)
    patch = at // own
    order = (to == patch // half * half * own + at % own * half + patch % half).astype(F32).astype(BF16)
    for copy in copies:
        copy.wait()
    late = sum(held[i].astype(F32) for i in range(1, count)).astype(BF16)
    state = jnp.concatenate([held[0], late], axis=0).astype(F32)
    out_ref[...] = dot(order, (state + back).astype(BF16)).astype(BF16)


def finish_bytes(result, proj, pieces):
    rows, width = pieces[0].shape
    return pl.pallas_call(
        functools.partial(bytes_kernel, len(pieces)),
        in_specs=[VMEM, VMEM] + [pl.BlockSpec(memory_space=pl.ANY)] * len(pieces),
        out_specs=VMEM,
        out_shape=jax.ShapeDtypeStruct((2 * rows, width), BF16),
        scratch_shapes=[pltpu.VMEM((len(pieces), rows, width), BF16), pltpu.SemaphoreType.DMA((len(pieces),))],
        compiler_params=pltpu.CompilerParams(vmem_limit_bytes=16 * 2**20),
        cost_estimate=BRIEF,
        name="finish_bytes",
    )(result, proj, *pieces)


def shift(value, axis, step):
    count = lax.axis_size(axis)
    return lax.ppermute(value, axis, [(i, (i + step) % count) for i in range(count)])


def scatter(chunks, axis):
    return [chunks[0]] + [shift(chunk, axis, step) for step, chunk in enumerate(chunks[1:], 1)]


def shift_slots(axis):
    count = lax.axis_size(axis)
    return ((lax.axis_index(axis) + jnp.arange(count)) % count).astype(jnp.int32)


def gather(value, axis):
    return [value] + [shift(value, axis, step) for step in range(1, lax.axis_size(axis))]


def swap_cores(value, axis):
    return lax.ppermute(value, axis, [(i, i ^ 1) for i in range(lax.axis_size(axis))])


def twin_ids(axis):
    count = lax.axis_size(axis)
    return ((lax.axis_index(axis) - 2 * jnp.arange(count // 2)) % count).astype(jnp.int32)


def owner_order(owners, source, patches):
    listed = lax.dynamic_index_in_dim(owners, source, 0, keepdims=False)
    count = listed.shape[0]
    block = patches // count
    index = jnp.arange(count, dtype=jnp.int32)
    before = (listed[None, :] < listed[:, None]) | (
        (listed[None, :] == listed[:, None]) & (index[None, :] < index[:, None])
    )
    slot = jnp.sum(before, axis=1).astype(jnp.int32)
    row = jnp.arange(patches, dtype=jnp.int32)
    spread = jnp.sum(jnp.where(row[:, None] // block == index[None, :], slot[None, :], 0), axis=1).astype(jnp.int32)
    place = spread * block + row % block
    return (row[:, None] == place[None, :]).astype(BF16)


def on_device(
    byte_in,
    local_gain,
    local_qkv,
    local_out,
    mlp_up,
    mlp_down,
    local_scale,
    patch_proj,
    global_gain,
    global_qkv,
    global_out,
    global_scale,
    back_proj,
    owners,
):
    patches, span, width = byte_in.shape
    ways = lax.axis_size("head")
    own = span // ways
    me = lax.axis_index("head").astype(jnp.int32)
    seq = lax.axis_index("seq").astype(jnp.int32)
    depth = global_qkv.shape[2] // global_scale.shape[0]

    slots = shift_slots("head")
    rows = byte_in.reshape(-1, width)
    weights = [jnp.transpose(local_qkv, (1, 0, 2)), mlp_up, local_out, mlp_down, patch_proj]
    gain = local_gain.reshape(1, -1)
    early, _ = local_part(local_scale, rows, gain, weights, span, ways, False)
    early = scatter(early, "head")
    parts, chunks = local_part(local_scale, rows, gain, weights, span, ways, True)
    chunks, early[1], early[2] = lax.optimization_barrier((chunks, early[1], early[2]))
    chunks = scatter(chunks, "head")
    early, early_share = finish_state(patch_proj, early, own)
    late_share = sum(p.astype(F32) for p in chunks).astype(BF16)
    residual = jnp.concatenate([early_share, late_share], axis=0)
    weight, residual = lax.optimization_barrier((jnp.transpose(global_qkv, (1, 0, 2)), residual))
    shares = gather(residual, "head")
    ids = (me - jnp.arange(ways, dtype=jnp.int32)) % ways
    core = (seq % 2).reshape(1)
    kept, given = global_heads(depth, core, ids, global_gain.reshape(ways, 1, -1), shares, fetch(weight))
    received = swap_cores(given, "seq")
    parts, received = lax.optimization_barrier((parts, received))
    half = kept.shape[1] // 3
    keyed = jnp.concatenate([kept[:, half:], received[:, half:]], axis=0)
    pieces = [shift(keyed, "seq", 2 * step) for step in range(1, lax.axis_size("seq") // 2)]
    parts = scatter(parts, "head")
    own_heads, other_heads = attend(depth, seq.reshape(1), twin_ids("seq"), global_scale, kept, received, pieces)
    other_heads, parts[1] = lax.optimization_barrier((swap_cores(other_heads, "seq"), parts[1]))
    updates = scatter(project(core, slots, own_heads, other_heads, global_out), "head")
    updates, parts[2] = lax.optimization_barrier((updates, parts[2]))
    result, routed = finish_result(owner_order(owners, seq, patches), residual, updates)
    global_state = lax.all_to_all(routed, "seq", split_axis=0, concat_axis=0, tiled=True)
    byte_out = finish_bytes(result, back_proj, [early] + parts)
    return byte_out.reshape(patches, own, width), global_state


def solution(mesh):
    placed = (
        P("seq", None, None),
        P(),
        P(None, None, "head"),
        P("head", None),
        P(None, "head"),
        P("head", None),
        P("head"),
        P(),
        P(),
        P(None, None, "head"),
        P("head", None),
        P("head"),
        P(),
        P(),
    )
    return jax.shard_map(
        on_device,
        mesh=mesh,
        in_specs=placed,
        out_specs=(P("seq", "head", None), P("seq", "head")),
        check_vma=False,
    )
```

```python
import functools
import math

import jax
import jax.numpy as jnp
from jax import lax
from jax.experimental import pallas as pl
from jax.experimental.pallas import tpu as pltpu
from jax.sharding import PartitionSpec as P

EPSILON = 1e-06
NEGATIVE = -1e30
F32 = jnp.float32
BF16 = jnp.bfloat16
BRIEF = pl.CostEstimate(flops=1, bytes_accessed=1, transcendentals=0)
VMEM = pl.BlockSpec(memory_space=pltpu.VMEM)
HBM = pl.BlockSpec(memory_space=pltpu.HBM)
SMEM = pl.BlockSpec(memory_space=pltpu.SMEM)


def dot(left, right):
    return jnp.dot(left, right, preferred_element_type=F32)


def dot_t(left, right):
    return lax.dot_general(left, right, (((1,), (1,)), ((), ())), preferred_element_type=F32)


def unit(values):
    return (values * lax.rsqrt(jnp.mean(values * values, axis=-1, keepdims=True) + EPSILON)).astype(BF16)


def gelu(values):
    inner = math.sqrt(2.0 / math.pi) * (values + 0.044715 * (values * values * values))
    return 0.5 * values * (1.0 + jnp.tanh(inner))


def local_kernel(span, ways, piece, last, scale_ref, gain_ref, x_hbm, *refs):
    sources, parts, others = refs[:5], refs[5 : 5 + ways], refs[5 + ways : -11]
    held, (x_ref, part_ref, share_ref, in_sem, x_sem, part_sem) = refs[-11:-6], refs[-6:]
    patches = share_ref.shape[1]
    own = span // ways
    rows = piece * span
    pieces = patches // piece
    cuts = [slice(i * rows, (i + 1) * rows) for i in range(pieces)]
    skip = x_ref.shape[0] if last else 0
    loads = [
        pltpu.make_async_copy(x_hbm.at[pl.ds(skip + c.start, rows)], x_ref.at[pl.ds(c.start, rows)], x_sem.at[i])
        for i, c in enumerate(cuts)
    ]
    loads += [pltpu.make_async_copy(s, h, in_sem.at[i]) for i, (s, h) in enumerate(zip(sources, held))]
    for copy in loads:
        copy.start()
    me = lax.axis_index("head")
    at = lax.broadcasted_iota(jnp.int32, (rows, rows), 0)
    to = lax.broadcasted_iota(jnp.int32, (rows, rows), 1)
    order = (to == (at % piece) * span + at // piece).astype(F32).astype(BF16)
    kept = lax.broadcasted_iota(jnp.int32, (rows, 1), 0) // piece // own == me
    for copy in loads:
        copy.wait()
    qkv_ref, up_ref, out_ref, down_ref, proj_ref = held
    xs, normed = [], []
    for cut in cuts:
        x = dot(order, x_ref[cut])
        xs.append(jnp.where(kept, x, 0.0).astype(BF16))
        factor = lax.rsqrt(jnp.mean(x * x, axis=-1, keepdims=True) + EPSILON)
        normed.append((x * factor * gain_ref[...]).astype(BF16))
    xs, normed = jnp.concatenate(xs, axis=0), jnp.concatenate(normed, axis=0)
    query, key, value = (dot(normed, qkv_ref[i]) for i in range(3))
    seen = (at % piece == to % piece) & (to <= at)
    heads = scale_ref.shape[0]
    depth = query.shape[1] // heads
    attended = []
    for cut in cuts:
        columns = []
        for h in range(heads):
            head = slice(h * depth, (h + 1) * depth)
            scores = dot_t(unit(query[cut, head]), unit(key[cut, head])) * (scale_ref[h] / math.sqrt(depth))
            scores = jnp.where(seen, scores, NEGATIVE)
            weights = jnp.exp(scores - jnp.max(scores, axis=-1, keepdims=True))
            total = jnp.sum(weights, axis=-1, keepdims=True)
            columns.append((dot(weights.astype(BF16), value[cut, head].astype(BF16)) / total).astype(BF16))
        attended.append(jnp.concatenate(columns, axis=1))
    act = gelu(dot(normed, up_ref[...])).astype(BF16)
    mixed = jnp.concatenate([jnp.concatenate(attended, axis=0), act], axis=1)
    partial = dot(mixed, jnp.concatenate([out_ref[...], down_ref[...]], axis=0)) + xs.astype(F32)
    partial = partial.astype(BF16)
    for i, cut in enumerate(cuts):
        for b in range(span):
            put = (b % own) * patches + i * piece
            part_ref[b // own, put : put + piece] = partial[cut][b * piece : (b + 1) * piece]
    stores = []
    for slot, part in enumerate(parts):
        stores.append(pltpu.make_async_copy(part_ref.at[lax.rem(me + slot, ways)], part, part_sem.at[slot]))
        stores[-1].start()
    if last:
        share = dot(partial, proj_ref[...]).astype(BF16)
        size = share.shape[1]
        for i, cut in enumerate(cuts):
            for b in range(span):
                put = slice((b % own) * size, (b % own + 1) * size)
                share_ref[b // own, i * piece : (i + 1) * piece, put] = share[cut][b * piece : (b + 1) * piece]
        for slot, out in enumerate(others):
            out[...] = share_ref[lax.rem(me + slot, ways)]
    for copy in stores:
        copy.wait()


def local_part(scale, x, gain, weights, span, ways, last):
    rows, width = x.shape[0] // 2, x.shape[1]
    patches = rows // span
    own = span // ways
    piece = math.gcd(patches, 32)
    part = (own * patches, width)
    share = (patches, own * weights[-1].shape[1])
    others = [pltpu.VMEM(share, BF16)] * (ways if last else 0)
    outs = pl.pallas_call(
        functools.partial(local_kernel, span, ways, piece, last),
        in_specs=[SMEM, VMEM, HBM] + [HBM] * len(weights),
        out_specs=[HBM] * ways + [VMEM] * len(others),
        out_shape=[jax.ShapeDtypeStruct(part, BF16)] * ways + others,
        scratch_shapes=[pltpu.VMEM(w.shape, w.dtype) for w in weights]
        + [
            pltpu.VMEM((rows, width), BF16),
            pltpu.VMEM((ways, *part), BF16),
            pltpu.VMEM((ways, *share), BF16),
            pltpu.SemaphoreType.DMA((len(weights),)),
            pltpu.SemaphoreType.DMA((patches // piece,)),
            pltpu.SemaphoreType.DMA((ways,)),
        ],
        compiler_params=pltpu.CompilerParams(vmem_limit_bytes=60 * 2**20),
        cost_estimate=pl.CostEstimate(flops=8 * rows * width * width, bytes_accessed=10 * 2**20, transcendentals=rows * width),
        name="local_part",
    )(scale, gain, x, *weights)
    return list(outs[:ways]), list(outs[ways:])


def state_kernel(count, proj_ref, *refs):
    pieces, (state_ref, share_ref) = refs[:count], refs[count:]
    state = sum(p[...].astype(F32) for p in pieces).astype(BF16)
    state_ref[...] = state
    patches = share_ref.shape[0]
    width = proj_ref.shape[1]
    for b in range(state.shape[0] // patches):
        share_ref[:, b * width : (b + 1) * width] = dot(state[b * patches : (b + 1) * patches], proj_ref[...]).astype(BF16)


def finish_state(proj, pieces, own):
    rows, width = pieces[0].shape
    return pl.pallas_call(
        functools.partial(state_kernel, len(pieces)),
        in_specs=[VMEM] * (1 + len(pieces)),
        out_specs=(VMEM, VMEM),
        out_shape=(
            jax.ShapeDtypeStruct((rows, width), BF16),
            jax.ShapeDtypeStruct((rows // own, own * proj.shape[1]), BF16),
        ),
        compiler_params=pltpu.CompilerParams(vmem_limit_bytes=8 * 2**20),
        name="finish_state",
    )(proj, *pieces)


def fetch_kernel(source, held, sems):
    parts = source.shape[0]
    copies = [pltpu.make_async_copy(source.at[i], held.at[i], sems.at[i]) for i in range(parts)]
    for copy in copies:
        copy.start()
    for copy in copies:
        copy.wait()


def fetch(weight):
    return pl.pallas_call(
        fetch_kernel,
        in_specs=[HBM],
        out_specs=VMEM,
        out_shape=pltpu.VMEM(weight.shape, weight.dtype),
        scratch_shapes=[pltpu.SemaphoreType.DMA((weight.shape[0],))],
        compiler_params=pltpu.CompilerParams(vmem_limit_bytes=50 * 2**20),
        name="fetch",
    )(weight)


def heads_kernel(depth, core_ref, ids_ref, gain_ref, *refs):
    ways = gain_ref.shape[0]
    early, late, weight, outs = refs[:ways], refs[ways : 2 * ways], refs[2 * ways], refs[2 * ways + 1 :]
    width = early[0].shape[1]
    values = [jnp.concatenate([a[...], b[...]], axis=0).astype(F32) for a, b in zip(early, late)]
    square = sum(jnp.sum(v * v, axis=-1, keepdims=True) for v in values)
    factor = lax.rsqrt(square / (ways * width) + EPSILON)
    normed = [(v * factor * gain_ref[ids_ref[c]]).astype(BF16) for c, v in enumerate(values)]
    size = outs[0].shape[1] // 3
    for kind in range(3):
        for i, out in ((1, outs[1]), (0, outs[0])):
            columns = pl.ds(pl.multiple_of((core_ref[0] ^ i) * size, size), size)
            mixed = sum(
                dot(n, weight[kind, pl.ds(pl.multiple_of(ids_ref[c] * width, width), width), columns])
                for c, n in enumerate(normed)
            )
            if kind < 2:
                mixed = jnp.concatenate([unit(mixed[:, c : c + depth]) for c in range(0, size, depth)], axis=1)
            out[:, kind * size : (kind + 1) * size] = mixed.astype(BF16)


def global_heads(depth, core, ids, gain, early, late, qkv):
    shape = jax.ShapeDtypeStruct((2 * early[0].shape[0], 3 * qkv.shape[2] // 2), BF16)
    return pl.pallas_call(
        functools.partial(heads_kernel, depth),
        in_specs=[SMEM, SMEM] + [VMEM] * (2 + len(early) + len(late)),
        out_specs=(VMEM, VMEM),
        out_shape=(shape, shape),
        compiler_params=pltpu.CompilerParams(vmem_limit_bytes=8 * 2**20),
        name="global_heads",
    )(core, ids, gain, *early, *late, qkv)


def attend_kernel(depth, me_ref, ids_ref, scale_ref, kept_ref, given_ref, *refs):
    pieces, (own_ref, other_ref) = refs[:-2], refs[-2:]
    rows = kept_ref.shape[0]
    size = own_ref.shape[1]
    heads = size // depth
    me = me_ref[0]

    def places(index, shape, axis):
        row = lax.broadcasted_iota(jnp.int32, shape, axis)
        return jnp.where(row < rows, index * rows + row, (index ^ 1) * rows + row - rows)

    at = places(me, (2 * rows, 1), 0)
    seen = [places(i, (1, 2 * rows), 1) <= at for i in [me] + [ids_ref[p + 1] for p in range(len(pieces))]]
    own = jnp.concatenate([kept_ref[...], given_ref[...]], axis=0)
    query = own[:, :size]
    pieces = [own[:, size:]] + [p[...] for p in pieces]
    for h in range(heads):
        cut = slice(h * depth, (h + 1) * depth)
        factor = scale_ref[(me % 2) * heads + h] / math.sqrt(depth)
        scores = [jnp.where(s, dot_t(query[:, cut], p[:, cut]) * factor, NEGATIVE) for s, p in zip(seen, pieces)]
        top = functools.reduce(jnp.maximum, [jnp.max(s, axis=-1, keepdims=True) for s in scores])
        weights = [jnp.exp(s - top) for s in scores]
        total = sum(jnp.sum(w, axis=-1, keepdims=True) for w in weights)
        values = slice(size + h * depth, size + (h + 1) * depth)
        summed = sum(dot(w.astype(BF16), p[:, values]) for w, p in zip(weights, pieces))
        attended = (summed / total).astype(BF16)
        own_ref[:, cut] = attended[:rows]
        other_ref[:, cut] = attended[rows:]


def attend(depth, me, ids, scale, kept, given, pieces):
    rows = kept.shape[0]
    shape = jax.ShapeDtypeStruct((rows, kept.shape[1] // 3), BF16)
    return pl.pallas_call(
        functools.partial(attend_kernel, depth),
        in_specs=[SMEM, SMEM, SMEM] + [VMEM] * (2 + len(pieces)),
        out_specs=(VMEM, VMEM),
        out_shape=(shape, shape),
        compiler_params=pltpu.CompilerParams(vmem_limit_bytes=20 * 2**20),
        cost_estimate=BRIEF,
        name="attend",
    )(me, ids, scale, kept, given, *pieces)


def project_kernel(core_ref, slots_ref, own_ref, other_ref, proj_ref, *outs):
    size = own_ref.shape[1]
    own_rows = pl.ds(pl.multiple_of(core_ref[0] * size, size), size)
    other_rows = pl.ds(pl.multiple_of((core_ref[0] ^ 1) * size, size), size)
    for slot, out in enumerate(outs):
        width = out.shape[1]
        columns = pl.ds(pl.multiple_of(slots_ref[slot] * width, width), width)
        out[...] = (dot(own_ref[...], proj_ref[own_rows, columns]) + dot(other_ref[...], proj_ref[other_rows, columns])).astype(BF16)


def project(core, slots, own, other, proj):
    ways = slots.shape[0]
    return pl.pallas_call(
        project_kernel,
        in_specs=[SMEM, SMEM] + [VMEM] * 3,
        out_specs=[VMEM] * ways,
        out_shape=[jax.ShapeDtypeStruct((own.shape[0], proj.shape[1] // ways), BF16)] * ways,
        compiler_params=pltpu.CompilerParams(vmem_limit_bytes=6 * 2**20),
        cost_estimate=BRIEF,
        name="project",
    )(core, slots, own, other, proj)


def result_kernel(count, order_ref, own_ref, *refs):
    pieces, (result_ref, routed_ref) = refs[:count], refs[count:]
    total = own_ref[...].astype(F32) + sum(p[...].astype(F32) for p in pieces)
    result = total.astype(BF16)
    result_ref[...] = result
    routed_ref[...] = dot(order_ref[...], result).astype(BF16)


def finish_result(order, residual, pieces):
    shape = jax.ShapeDtypeStruct(residual.shape, BF16)
    return pl.pallas_call(
        functools.partial(result_kernel, len(pieces)),
        in_specs=[VMEM] * (2 + len(pieces)),
        out_specs=(VMEM, VMEM),
        out_shape=(shape, shape),
        compiler_params=pltpu.CompilerParams(vmem_limit_bytes=4 * 2**20),
        cost_estimate=BRIEF,
        name="finish_result",
    )(order, residual, *pieces)


def bytes_kernel(count, result_ref, proj_ref, *refs):
    sources, (out_ref, held, sems) = refs[:count], refs[count:]
    copies = [pltpu.make_async_copy(p, held.at[i], sems.at[i]) for i, p in enumerate(sources)]
    for copy in copies:
        copy.start()
    rows = result_ref.shape[0]
    half = rows // 2
    width = proj_ref.shape[0]
    own = out_ref.shape[0] // rows
    back = [dot(result_ref[:, b * width : (b + 1) * width], proj_ref[...]) for b in range(own)]
    back = jnp.concatenate([b[:half] for b in back] + [b[half:] for b in back], axis=0)
    at = lax.broadcasted_iota(jnp.int32, (rows * own, rows * own), 0)
    to = lax.broadcasted_iota(jnp.int32, (rows * own, rows * own), 1)
    patch = at // own
    order = (to == patch // half * half * own + at % own * half + patch % half).astype(F32).astype(BF16)
    for copy in copies:
        copy.wait()
    late = sum(held[i].astype(F32) for i in range(1, count)).astype(BF16)
    state = jnp.concatenate([held[0], late], axis=0).astype(F32)
    out_ref[...] = dot(order, (state + back).astype(BF16)).astype(BF16)


def finish_bytes(result, proj, pieces):
    rows, width = pieces[0].shape
    return pl.pallas_call(
        functools.partial(bytes_kernel, len(pieces)),
        in_specs=[VMEM, VMEM] + [pl.BlockSpec(memory_space=pl.ANY)] * len(pieces),
        out_specs=VMEM,
        out_shape=jax.ShapeDtypeStruct((2 * rows, width), BF16),
        scratch_shapes=[pltpu.VMEM((len(pieces), rows, width), BF16), pltpu.SemaphoreType.DMA((len(pieces),))],
        compiler_params=pltpu.CompilerParams(vmem_limit_bytes=16 * 2**20),
        cost_estimate=BRIEF,
        name="finish_bytes",
    )(result, proj, *pieces)


def shift(value, axis, step):
    count = lax.axis_size(axis)
    return lax.ppermute(value, axis, [(i, (i + step) % count) for i in range(count)])


def scatter(chunks, axis):
    return [chunks[0]] + [shift(chunk, axis, step) for step, chunk in enumerate(chunks[1:], 1)]


def shift_slots(axis):
    count = lax.axis_size(axis)
    return ((lax.axis_index(axis) + jnp.arange(count)) % count).astype(jnp.int32)


def gather(value, axis):
    return [value] + [shift(value, axis, step) for step in range(1, lax.axis_size(axis))]


def swap_cores(value, axis):
    return lax.ppermute(value, axis, [(i, i ^ 1) for i in range(lax.axis_size(axis))])


def twin_ids(axis):
    count = lax.axis_size(axis)
    return ((lax.axis_index(axis) - 2 * jnp.arange(count // 2)) % count).astype(jnp.int32)


def owner_order(owners, source, patches):
    listed = lax.dynamic_index_in_dim(owners, source, 0, keepdims=False)
    count = listed.shape[0]
    block = patches // count
    index = jnp.arange(count, dtype=jnp.int32)
    before = (listed[None, :] < listed[:, None]) | (
        (listed[None, :] == listed[:, None]) & (index[None, :] < index[:, None])
    )
    slot = jnp.sum(before, axis=1).astype(jnp.int32)
    row = jnp.arange(patches, dtype=jnp.int32)
    spread = jnp.sum(jnp.where(row[:, None] // block == index[None, :], slot[None, :], 0), axis=1).astype(jnp.int32)
    place = spread * block + row % block
    return (row[:, None] == place[None, :]).astype(BF16)


def on_device(
    byte_in,
    local_gain,
    local_qkv,
    local_out,
    mlp_up,
    mlp_down,
    local_scale,
    patch_proj,
    global_gain,
    global_qkv,
    global_out,
    global_scale,
    back_proj,
    owners,
):
    patches, span, width = byte_in.shape
    ways = lax.axis_size("head")
    own = span // ways
    me = lax.axis_index("head").astype(jnp.int32)
    seq = lax.axis_index("seq").astype(jnp.int32)
    depth = global_qkv.shape[2] // global_scale.shape[0]

    slots = shift_slots("head")
    rows = byte_in.reshape(-1, width)
    weights = [jnp.transpose(local_qkv, (1, 0, 2)), mlp_up, local_out, mlp_down, patch_proj]
    gain = local_gain.reshape(1, -1)
    early, _ = local_part(local_scale, rows, gain, weights, span, ways, False)
    early = scatter(early, "head")
    parts, chunks = local_part(local_scale, rows, gain, weights, span, ways, True)
    chunks, early[1] = lax.optimization_barrier((chunks, early[1]))
    chunks = scatter(chunks, "head")
    early, early_share = finish_state(patch_proj, early, own)
    early_shares = gather(early_share, "head")
    late_share = sum(p.astype(F32) for p in chunks).astype(BF16)
    weight, late_share = lax.optimization_barrier((jnp.transpose(global_qkv, (1, 0, 2)), late_share))
    late_shares = gather(late_share, "head")
    residual = jnp.concatenate([early_share, late_share], axis=0)
    ids = (me - jnp.arange(ways, dtype=jnp.int32)) % ways
    core = (seq % 2).reshape(1)
    kept, given = global_heads(depth, core, ids, global_gain.reshape(ways, 1, -1), early_shares, late_shares, fetch(weight))
    received = swap_cores(given, "seq")
    parts, received = lax.optimization_barrier((parts, received))
    half = kept.shape[1] // 3
    keyed = jnp.concatenate([kept[:, half:], received[:, half:]], axis=0)
    pieces = [shift(keyed, "seq", 2 * step) for step in range(1, lax.axis_size("seq") // 2)]
    parts = scatter(parts, "head")
    own_heads, other_heads = attend(depth, seq.reshape(1), twin_ids("seq"), global_scale, kept, received, pieces)
    other_heads, parts[1] = lax.optimization_barrier((swap_cores(other_heads, "seq"), parts[1]))
    updates = scatter(project(core, slots, own_heads, other_heads, global_out), "head")
    updates, parts[2] = lax.optimization_barrier((updates, parts[2]))
    result, routed = finish_result(owner_order(owners, seq, patches), residual, updates)
    global_state = lax.all_to_all(routed, "seq", split_axis=0, concat_axis=0, tiled=True)
    byte_out = finish_bytes(result, back_proj, [early] + parts)
    return byte_out.reshape(patches, own, width), global_state


def solution(mesh):
    placed = (
        P("seq", None, None),
        P(),
        P(None, None, "head"),
        P("head", None),
        P(None, "head"),
        P("head", None),
        P("head"),
        P(),
        P(),
        P(None, None, "head"),
        P("head", None),
        P("head"),
        P(),
        P(),
    )
    return jax.shard_map(
        on_device,
        mesh=mesh,
        in_specs=placed,
        out_specs=(P("seq", "head", None), P("seq", "head")),
        check_vma=False,
    )
```

```python
import functools
import math

import jax
import jax.numpy as jnp
from jax import lax
from jax.experimental import pallas as pl
from jax.experimental.pallas import tpu as pltpu
from jax.sharding import PartitionSpec as P

EPSILON = 1e-06
NEGATIVE = -1e30
F32 = jnp.float32
BF16 = jnp.bfloat16
BRIEF = pl.CostEstimate(flops=1, bytes_accessed=1, transcendentals=0)
VMEM = pl.BlockSpec(memory_space=pltpu.VMEM)
HBM = pl.BlockSpec(memory_space=pltpu.HBM)
SMEM = pl.BlockSpec(memory_space=pltpu.SMEM)


def dot(left, right):
    return jnp.dot(left, right, preferred_element_type=F32)


def dot_t(left, right):
    return lax.dot_general(left, right, (((1,), (1,)), ((), ())), preferred_element_type=F32)


def unit(values):
    return (values * lax.rsqrt(jnp.mean(values * values, axis=-1, keepdims=True) + EPSILON)).astype(BF16)


def gelu(values):
    inner = math.sqrt(2.0 / math.pi) * (values + 0.044715 * (values * values * values))
    return 0.5 * values * (1.0 + jnp.tanh(inner))


def local_kernel(span, ways, piece, last, scale_ref, gain_ref, x_hbm, *refs):
    sources, parts, others = refs[:5], refs[5 : 5 + ways], refs[5 + ways : -11]
    held, (x_ref, part_ref, share_ref, in_sem, x_sem, part_sem) = refs[-11:-6], refs[-6:]
    patches = share_ref.shape[1]
    own = span // ways
    rows = piece * span
    pieces = patches // piece
    cuts = [slice(i * rows, (i + 1) * rows) for i in range(pieces)]
    skip = x_ref.shape[0] if last else 0
    loads = [
        pltpu.make_async_copy(x_hbm.at[pl.ds(skip + c.start, rows)], x_ref.at[pl.ds(c.start, rows)], x_sem.at[i])
        for i, c in enumerate(cuts)
    ]
    loads += [pltpu.make_async_copy(s, h, in_sem.at[i]) for i, (s, h) in enumerate(zip(sources, held))]
    for copy in loads:
        copy.start()
    me = lax.axis_index("head")
    at = lax.broadcasted_iota(jnp.int32, (rows, rows), 0)
    to = lax.broadcasted_iota(jnp.int32, (rows, rows), 1)
    order = (to == (at % piece) * span + at // piece).astype(F32).astype(BF16)
    kept = lax.broadcasted_iota(jnp.int32, (rows, 1), 0) // piece // own == me
    for copy in loads:
        copy.wait()
    qkv_ref, up_ref, out_ref, down_ref, proj_ref = held
    xs, normed = [], []
    for cut in cuts:
        x = dot(order, x_ref[cut])
        xs.append(jnp.where(kept, x, 0.0).astype(BF16))
        factor = lax.rsqrt(jnp.mean(x * x, axis=-1, keepdims=True) + EPSILON)
        normed.append((x * factor * gain_ref[...]).astype(BF16))
    xs, normed = jnp.concatenate(xs, axis=0), jnp.concatenate(normed, axis=0)
    query, key, value = (dot(normed, qkv_ref[i]) for i in range(3))
    seen = (at % piece == to % piece) & (to <= at)
    heads = scale_ref.shape[0]
    depth = query.shape[1] // heads
    attended = []
    for cut in cuts:
        columns = []
        for h in range(heads):
            head = slice(h * depth, (h + 1) * depth)
            scores = dot_t(unit(query[cut, head]), unit(key[cut, head])) * (scale_ref[h] / math.sqrt(depth))
            scores = jnp.where(seen, scores, NEGATIVE)
            weights = jnp.exp(scores - jnp.max(scores, axis=-1, keepdims=True))
            total = jnp.sum(weights, axis=-1, keepdims=True)
            columns.append((dot(weights.astype(BF16), value[cut, head].astype(BF16)) / total).astype(BF16))
        attended.append(jnp.concatenate(columns, axis=1))
    act = gelu(dot(normed, up_ref[...])).astype(BF16)
    mixed = jnp.concatenate([jnp.concatenate(attended, axis=0), act], axis=1)
    partial = dot(mixed, jnp.concatenate([out_ref[...], down_ref[...]], axis=0)) + xs.astype(F32)
    partial = partial.astype(BF16)
    for i, cut in enumerate(cuts):
        for b in range(span):
            put = (b % own) * patches + i * piece
            part_ref[b // own, put : put + piece] = partial[cut][b * piece : (b + 1) * piece]
    stores = []
    for slot, part in enumerate(parts):
        stores.append(pltpu.make_async_copy(part_ref.at[lax.rem(me + slot, ways)], part, part_sem.at[slot]))
        stores[-1].start()
    if last:
        share = dot(partial, proj_ref[...]).astype(BF16)
        size = share.shape[1]
        for i, cut in enumerate(cuts):
            for b in range(span):
                put = slice((b % own) * size, (b % own + 1) * size)
                share_ref[b // own, i * piece : (i + 1) * piece, put] = share[cut][b * piece : (b + 1) * piece]
        for slot, out in enumerate(others):
            out[...] = share_ref[lax.rem(me + slot, ways)]
    for copy in stores:
        copy.wait()


def local_part(scale, x, gain, weights, span, ways, last):
    rows, width = x.shape[0] // 2, x.shape[1]
    patches = rows // span
    own = span // ways
    piece = math.gcd(patches, 32)
    part = (own * patches, width)
    share = (patches, own * weights[-1].shape[1])
    others = [pltpu.VMEM(share, BF16)] * (ways if last else 0)
    outs = pl.pallas_call(
        functools.partial(local_kernel, span, ways, piece, last),
        in_specs=[SMEM, VMEM, HBM] + [HBM] * len(weights),
        out_specs=[HBM] * ways + [VMEM] * len(others),
        out_shape=[jax.ShapeDtypeStruct(part, BF16)] * ways + others,
        scratch_shapes=[pltpu.VMEM(w.shape, w.dtype) for w in weights]
        + [
            pltpu.VMEM((rows, width), BF16),
            pltpu.VMEM((ways, *part), BF16),
            pltpu.VMEM((ways, *share), BF16),
            pltpu.SemaphoreType.DMA((len(weights),)),
            pltpu.SemaphoreType.DMA((patches // piece,)),
            pltpu.SemaphoreType.DMA((ways,)),
        ],
        compiler_params=pltpu.CompilerParams(vmem_limit_bytes=60 * 2**20),
        cost_estimate=pl.CostEstimate(flops=8 * rows * width * width, bytes_accessed=10 * 2**20, transcendentals=rows * width),
        name="local_part",
    )(scale, gain, x, *weights)
    return list(outs[:ways]), list(outs[ways:])


def state_kernel(count, proj_ref, *refs):
    pieces, (state_ref, share_ref) = refs[:count], refs[count:]
    state = sum(p[...].astype(F32) for p in pieces).astype(BF16)
    state_ref[...] = state
    patches = share_ref.shape[0]
    width = proj_ref.shape[1]
    for b in range(state.shape[0] // patches):
        share_ref[:, b * width : (b + 1) * width] = dot(state[b * patches : (b + 1) * patches], proj_ref[...]).astype(BF16)


def finish_state(proj, pieces, own):
    rows, width = pieces[0].shape
    return pl.pallas_call(
        functools.partial(state_kernel, len(pieces)),
        in_specs=[VMEM] * (1 + len(pieces)),
        out_specs=(VMEM, VMEM),
        out_shape=(
            jax.ShapeDtypeStruct((rows, width), BF16),
            jax.ShapeDtypeStruct((rows // own, own * proj.shape[1]), BF16),
        ),
        compiler_params=pltpu.CompilerParams(vmem_limit_bytes=8 * 2**20),
        name="finish_state",
    )(proj, *pieces)


def fetch_kernel(source, held, sems):
    parts = source.shape[0]
    copies = [pltpu.make_async_copy(source.at[i], held.at[i], sems.at[i]) for i in range(parts)]
    for copy in copies:
        copy.start()
    for copy in copies:
        copy.wait()


def fetch(weight):
    return pl.pallas_call(
        fetch_kernel,
        in_specs=[HBM],
        out_specs=VMEM,
        out_shape=pltpu.VMEM(weight.shape, weight.dtype),
        scratch_shapes=[pltpu.SemaphoreType.DMA((weight.shape[0],))],
        compiler_params=pltpu.CompilerParams(vmem_limit_bytes=50 * 2**20),
        name="fetch",
    )(weight)


def heads_kernel(depth, core_ref, ids_ref, gain_ref, *refs):
    ways = gain_ref.shape[0]
    early, late, weight, outs = refs[:ways], refs[ways : 2 * ways], refs[2 * ways], refs[2 * ways + 1 :]
    width = early[0].shape[1]
    values = [jnp.concatenate([a[...], b[...]], axis=0).astype(F32) for a, b in zip(early, late)]
    square = sum(jnp.sum(v * v, axis=-1, keepdims=True) for v in values)
    factor = lax.rsqrt(square / (ways * width) + EPSILON)
    normed = [(v * factor * gain_ref[ids_ref[c]]).astype(BF16) for c, v in enumerate(values)]
    size = outs[0].shape[1] // 3
    for kind in range(3):
        for i, out in ((1, outs[1]), (0, outs[0])):
            columns = pl.ds(pl.multiple_of((core_ref[0] ^ i) * size, size), size)
            mixed = sum(
                dot(n, weight[kind, pl.ds(pl.multiple_of(ids_ref[c] * width, width), width), columns])
                for c, n in enumerate(normed)
            )
            if kind < 2:
                mixed = jnp.concatenate([unit(mixed[:, c : c + depth]) for c in range(0, size, depth)], axis=1)
            out[:, kind * size : (kind + 1) * size] = mixed.astype(BF16)


def global_heads(depth, core, ids, gain, early, late, qkv):
    shape = jax.ShapeDtypeStruct((2 * early[0].shape[0], 3 * qkv.shape[2] // 2), BF16)
    return pl.pallas_call(
        functools.partial(heads_kernel, depth),
        in_specs=[SMEM, SMEM] + [VMEM] * (2 + len(early) + len(late)),
        out_specs=(VMEM, VMEM),
        out_shape=(shape, shape),
        compiler_params=pltpu.CompilerParams(vmem_limit_bytes=8 * 2**20),
        name="global_heads",
    )(core, ids, gain, *early, *late, qkv)


def attend_kernel(depth, me_ref, ids_ref, scale_ref, kept_ref, given_ref, *refs):
    pieces, (own_ref, other_ref) = refs[:-2], refs[-2:]
    rows = kept_ref.shape[0]
    size = own_ref.shape[1]
    heads = size // depth
    me = me_ref[0]

    def places(index, shape, axis):
        row = lax.broadcasted_iota(jnp.int32, shape, axis)
        return jnp.where(row < rows, index * rows + row, (index ^ 1) * rows + row - rows)

    at = places(me, (2 * rows, 1), 0)
    seen = [places(i, (1, 2 * rows), 1) <= at for i in [me] + [ids_ref[p + 1] for p in range(len(pieces))]]
    own = jnp.concatenate([kept_ref[...], given_ref[...]], axis=0)
    query = own[:, :size]
    pieces = [own[:, size:]] + [p[...] for p in pieces]
    for h in range(heads):
        cut = slice(h * depth, (h + 1) * depth)
        factor = scale_ref[(me % 2) * heads + h] / math.sqrt(depth)
        scores = [jnp.where(s, dot_t(query[:, cut], p[:, cut]) * factor, NEGATIVE) for s, p in zip(seen, pieces)]
        top = functools.reduce(jnp.maximum, [jnp.max(s, axis=-1, keepdims=True) for s in scores])
        weights = [jnp.exp(s - top) for s in scores]
        total = sum(jnp.sum(w, axis=-1, keepdims=True) for w in weights)
        values = slice(size + h * depth, size + (h + 1) * depth)
        summed = sum(dot(w.astype(BF16), p[:, values]) for w, p in zip(weights, pieces))
        attended = (summed / total).astype(BF16)
        own_ref[:, cut] = attended[:rows]
        other_ref[:, cut] = attended[rows:]


def attend(depth, me, ids, scale, kept, given, pieces):
    rows = kept.shape[0]
    shape = jax.ShapeDtypeStruct((rows, kept.shape[1] // 3), BF16)
    return pl.pallas_call(
        functools.partial(attend_kernel, depth),
        in_specs=[SMEM, SMEM, SMEM] + [VMEM] * (2 + len(pieces)),
        out_specs=(VMEM, VMEM),
        out_shape=(shape, shape),
        compiler_params=pltpu.CompilerParams(vmem_limit_bytes=20 * 2**20),
        cost_estimate=BRIEF,
        name="attend",
    )(me, ids, scale, kept, given, *pieces)


def project_kernel(core_ref, slots_ref, own_ref, other_ref, proj_ref, *outs):
    size = own_ref.shape[1]
    own_rows = pl.ds(pl.multiple_of(core_ref[0] * size, size), size)
    other_rows = pl.ds(pl.multiple_of((core_ref[0] ^ 1) * size, size), size)
    for slot, out in enumerate(outs):
        width = out.shape[1]
        columns = pl.ds(pl.multiple_of(slots_ref[slot] * width, width), width)
        out[...] = (dot(own_ref[...], proj_ref[own_rows, columns]) + dot(other_ref[...], proj_ref[other_rows, columns])).astype(BF16)


def project(core, slots, own, other, proj):
    ways = slots.shape[0]
    return pl.pallas_call(
        project_kernel,
        in_specs=[SMEM, SMEM] + [VMEM] * 3,
        out_specs=[VMEM] * ways,
        out_shape=[jax.ShapeDtypeStruct((own.shape[0], proj.shape[1] // ways), BF16)] * ways,
        compiler_params=pltpu.CompilerParams(vmem_limit_bytes=6 * 2**20),
        cost_estimate=BRIEF,
        name="project",
    )(core, slots, own, other, proj)


def result_kernel(count, order_ref, own_ref, *refs):
    pieces, (result_ref, routed_ref) = refs[:count], refs[count:]
    total = own_ref[...].astype(F32) + sum(p[...].astype(F32) for p in pieces)
    result = total.astype(BF16)
    result_ref[...] = result
    routed_ref[...] = dot(order_ref[...], result).astype(BF16)


def finish_result(order, residual, pieces):
    shape = jax.ShapeDtypeStruct(residual.shape, BF16)
    return pl.pallas_call(
        functools.partial(result_kernel, len(pieces)),
        in_specs=[VMEM] * (2 + len(pieces)),
        out_specs=(VMEM, VMEM),
        out_shape=(shape, shape),
        compiler_params=pltpu.CompilerParams(vmem_limit_bytes=4 * 2**20),
        cost_estimate=BRIEF,
        name="finish_result",
    )(order, residual, *pieces)


def bytes_kernel(count, result_ref, proj_ref, *refs):
    sources, (out_ref, held, sems) = refs[:count], refs[count:]
    copies = [pltpu.make_async_copy(p, held.at[i], sems.at[i]) for i, p in enumerate(sources)]
    for copy in copies:
        copy.start()
    rows = result_ref.shape[0]
    half = rows // 2
    width = proj_ref.shape[0]
    own = out_ref.shape[0] // rows
    back = [dot(result_ref[:, b * width : (b + 1) * width], proj_ref[...]) for b in range(own)]
    back = jnp.concatenate([b[:half] for b in back] + [b[half:] for b in back], axis=0)
    at = lax.broadcasted_iota(jnp.int32, (rows * own, rows * own), 0)
    to = lax.broadcasted_iota(jnp.int32, (rows * own, rows * own), 1)
    patch = at // own
    order = (to == patch // half * half * own + at % own * half + patch % half).astype(F32).astype(BF16)
    for copy in copies:
        copy.wait()
    late = sum(held[i].astype(F32) for i in range(1, count)).astype(BF16)
    state = jnp.concatenate([held[0], late], axis=0).astype(F32)
    out_ref[...] = dot(order, (state + back).astype(BF16)).astype(BF16)


def finish_bytes(result, proj, pieces):
    rows, width = pieces[0].shape
    return pl.pallas_call(
        functools.partial(bytes_kernel, len(pieces)),
        in_specs=[VMEM, VMEM] + [pl.BlockSpec(memory_space=pl.ANY)] * len(pieces),
        out_specs=VMEM,
        out_shape=jax.ShapeDtypeStruct((2 * rows, width), BF16),
        scratch_shapes=[pltpu.VMEM((len(pieces), rows, width), BF16), pltpu.SemaphoreType.DMA((len(pieces),))],
        compiler_params=pltpu.CompilerParams(vmem_limit_bytes=16 * 2**20),
        cost_estimate=BRIEF,
        name="finish_bytes",
    )(result, proj, *pieces)


def shift(value, axis, step):
    count = lax.axis_size(axis)
    return lax.ppermute(value, axis, [(i, (i + step) % count) for i in range(count)])


def scatter(chunks, axis):
    return [chunks[0]] + [shift(chunk, axis, step) for step, chunk in enumerate(chunks[1:], 1)]


def shift_slots(axis):
    count = lax.axis_size(axis)
    return ((lax.axis_index(axis) + jnp.arange(count)) % count).astype(jnp.int32)


def gather(value, axis):
    return [value] + [shift(value, axis, step) for step in range(1, lax.axis_size(axis))]


def swap_cores(value, axis):
    return lax.ppermute(value, axis, [(i, i ^ 1) for i in range(lax.axis_size(axis))])


def twin_ids(axis):
    count = lax.axis_size(axis)
    return ((lax.axis_index(axis) - 2 * jnp.arange(count // 2)) % count).astype(jnp.int32)


def owner_order(owners, source, patches):
    listed = lax.dynamic_index_in_dim(owners, source, 0, keepdims=False)
    count = listed.shape[0]
    block = patches // count
    index = jnp.arange(count, dtype=jnp.int32)
    before = (listed[None, :] < listed[:, None]) | (
        (listed[None, :] == listed[:, None]) & (index[None, :] < index[:, None])
    )
    slot = jnp.sum(before, axis=1).astype(jnp.int32)
    row = jnp.arange(patches, dtype=jnp.int32)
    spread = jnp.sum(jnp.where(row[:, None] // block == index[None, :], slot[None, :], 0), axis=1).astype(jnp.int32)
    place = spread * block + row % block
    return (row[:, None] == place[None, :]).astype(BF16)


def on_device(
    byte_in,
    local_gain,
    local_qkv,
    local_out,
    mlp_up,
    mlp_down,
    local_scale,
    patch_proj,
    global_gain,
    global_qkv,
    global_out,
    global_scale,
    back_proj,
    owners,
):
    patches, span, width = byte_in.shape
    ways = lax.axis_size("head")
    own = span // ways
    me = lax.axis_index("head").astype(jnp.int32)
    seq = lax.axis_index("seq").astype(jnp.int32)
    depth = global_qkv.shape[2] // global_scale.shape[0]

    slots = shift_slots("head")
    rows = byte_in.reshape(-1, width)
    weights = [jnp.transpose(local_qkv, (1, 0, 2)), mlp_up, local_out, mlp_down, patch_proj]
    gain = local_gain.reshape(1, -1)
    early, _ = local_part(local_scale, rows, gain, weights, span, ways, False)
    early = scatter(early, "head")
    parts, chunks = local_part(local_scale, rows, gain, weights, span, ways, True)
    chunks, early[1] = lax.optimization_barrier((chunks, early[1]))
    chunks = scatter(chunks, "head")
    early, early_share = finish_state(patch_proj, early, own)
    early_shares = gather(early_share, "head")
    late_share = sum(p.astype(F32) for p in chunks).astype(BF16)
    weight = jnp.transpose(global_qkv, (1, 0, 2))
    weight, late_share, parts = lax.optimization_barrier((weight, late_share, parts))
    late_shares = gather(late_share, "head")
    residual = jnp.concatenate([early_share, late_share], axis=0)
    ids = (me - jnp.arange(ways, dtype=jnp.int32)) % ways
    core = (seq % 2).reshape(1)
    kept, given = global_heads(depth, core, ids, global_gain.reshape(ways, 1, -1), early_shares, late_shares, fetch(weight))
    received = swap_cores(given, "seq")
    parts = scatter(parts, "head")
    received, parts[1] = lax.optimization_barrier((received, parts[1]))
    half = kept.shape[1] // 3
    keyed = jnp.concatenate([kept[:, half:], received[:, half:]], axis=0)
    pieces = [shift(keyed, "seq", 2 * step) for step in range(1, lax.axis_size("seq") // 2)]
    kept, parts[2] = lax.optimization_barrier((kept, parts[2]))
    own_heads, other_heads = attend(depth, seq.reshape(1), twin_ids("seq"), global_scale, kept, received, pieces)
    other_heads, parts[3:] = lax.optimization_barrier((swap_cores(other_heads, "seq"), parts[3:]))
    updates = scatter(project(core, slots, own_heads, other_heads, global_out), "head")
    result, routed = finish_result(owner_order(owners, seq, patches), residual, updates)
    global_state = lax.all_to_all(routed, "seq", split_axis=0, concat_axis=0, tiled=True)
    byte_out = finish_bytes(result, back_proj, [early] + parts)
    return byte_out.reshape(patches, own, width), global_state


def solution(mesh):
    placed = (
        P("seq", None, None),
        P(),
        P(None, None, "head"),
        P("head", None),
        P(None, "head"),
        P("head", None),
        P("head"),
        P(),
        P(),
        P(None, None, "head"),
        P("head", None),
        P("head"),
        P(),
        P(),
    )
    return jax.shard_map(
        on_device,
        mesh=mesh,
        in_specs=placed,
        out_specs=(P("seq", "head", None), P("seq", "head")),
        check_vma=False,
    )
```

```python
import functools
import math

import jax
import jax.numpy as jnp
from jax import lax
from jax.experimental import pallas as pl
from jax.experimental.pallas import tpu as pltpu
from jax.sharding import PartitionSpec as P

EPSILON = 1e-06
NEGATIVE = -1e30
F32 = jnp.float32
BF16 = jnp.bfloat16
BRIEF = pl.CostEstimate(flops=1, bytes_accessed=1, transcendentals=0)
VMEM = pl.BlockSpec(memory_space=pltpu.VMEM)
HBM = pl.BlockSpec(memory_space=pltpu.HBM)
SMEM = pl.BlockSpec(memory_space=pltpu.SMEM)


def dot(left, right):
    return jnp.dot(left, right, preferred_element_type=F32)


def dot_t(left, right):
    return lax.dot_general(left, right, (((1,), (1,)), ((), ())), preferred_element_type=F32)


def unit(values):
    return (values * lax.rsqrt(jnp.mean(values * values, axis=-1, keepdims=True) + EPSILON)).astype(BF16)


def gelu(values):
    inner = math.sqrt(2.0 / math.pi) * (values + 0.044715 * (values * values * values))
    return 0.5 * values * (1.0 + jnp.tanh(inner))


def local_kernel(span, ways, piece, last, scale_ref, gain_ref, x_hbm, *refs):
    sources, parts, others = refs[:5], refs[5 : 5 + ways], refs[5 + ways : -11]
    held, (x_ref, part_ref, share_ref, in_sem, x_sem, part_sem) = refs[-11:-6], refs[-6:]
    patches = share_ref.shape[1]
    own = span // ways
    rows = piece * span
    pieces = patches // piece
    cuts = [slice(i * rows, (i + 1) * rows) for i in range(pieces)]
    skip = x_ref.shape[0] if last else 0
    loads = [
        pltpu.make_async_copy(x_hbm.at[pl.ds(skip + c.start, rows)], x_ref.at[pl.ds(c.start, rows)], x_sem.at[i])
        for i, c in enumerate(cuts)
    ]
    loads += [pltpu.make_async_copy(s, h, in_sem.at[i]) for i, (s, h) in enumerate(zip(sources, held))]
    for copy in loads:
        copy.start()
    me = lax.axis_index("head")
    at = lax.broadcasted_iota(jnp.int32, (rows, rows), 0)
    to = lax.broadcasted_iota(jnp.int32, (rows, rows), 1)
    order = (to == (at % piece) * span + at // piece).astype(F32).astype(BF16)
    kept = lax.broadcasted_iota(jnp.int32, (rows, 1), 0) // piece // own == me
    for copy in loads:
        copy.wait()
    qkv_ref, up_ref, out_ref, down_ref, proj_ref = held
    xs, normed = [], []
    for cut in cuts:
        x = dot(order, x_ref[cut])
        xs.append(jnp.where(kept, x, 0.0).astype(BF16))
        factor = lax.rsqrt(jnp.mean(x * x, axis=-1, keepdims=True) + EPSILON)
        normed.append((x * factor * gain_ref[...]).astype(BF16))
    xs, normed = jnp.concatenate(xs, axis=0), jnp.concatenate(normed, axis=0)
    query, key, value = (dot(normed, qkv_ref[i]) for i in range(3))
    seen = (at % piece == to % piece) & (to <= at)
    heads = scale_ref.shape[0]
    depth = query.shape[1] // heads
    attended = []
    for cut in cuts:
        columns = []
        for h in range(heads):
            head = slice(h * depth, (h + 1) * depth)
            scores = dot_t(unit(query[cut, head]), unit(key[cut, head])) * (scale_ref[h] / math.sqrt(depth))
            scores = jnp.where(seen, scores, NEGATIVE)
            weights = jnp.exp(scores - jnp.max(scores, axis=-1, keepdims=True))
            total = jnp.sum(weights, axis=-1, keepdims=True)
            columns.append((dot(weights.astype(BF16), value[cut, head].astype(BF16)) / total).astype(BF16))
        attended.append(jnp.concatenate(columns, axis=1))
    act = gelu(dot(normed, up_ref[...])).astype(BF16)
    mixed = jnp.concatenate([jnp.concatenate(attended, axis=0), act], axis=1)
    partial = dot(mixed, jnp.concatenate([out_ref[...], down_ref[...]], axis=0)) + xs.astype(F32)
    partial = partial.astype(BF16)
    for i, cut in enumerate(cuts):
        for b in range(span):
            put = (b % own) * patches + i * piece
            part_ref[b // own, put : put + piece] = partial[cut][b * piece : (b + 1) * piece]
    stores = []
    for slot, part in enumerate(parts):
        stores.append(pltpu.make_async_copy(part_ref.at[lax.rem(me + slot, ways)], part, part_sem.at[slot]))
        stores[-1].start()
    if last:
        share = dot(partial, proj_ref[...]).astype(BF16)
        size = share.shape[1]
        for i, cut in enumerate(cuts):
            for b in range(span):
                put = slice((b % own) * size, (b % own + 1) * size)
                share_ref[b // own, i * piece : (i + 1) * piece, put] = share[cut][b * piece : (b + 1) * piece]
        for slot, out in enumerate(others):
            out[...] = share_ref[lax.rem(me + slot, ways)]
    for copy in stores:
        copy.wait()


def local_part(scale, x, gain, weights, span, ways, last):
    rows, width = x.shape[0] // 2, x.shape[1]
    patches = rows // span
    own = span // ways
    piece = math.gcd(patches, 32)
    part = (own * patches, width)
    share = (patches, own * weights[-1].shape[1])
    others = [pltpu.VMEM(share, BF16)] * (ways if last else 0)
    outs = pl.pallas_call(
        functools.partial(local_kernel, span, ways, piece, last),
        in_specs=[SMEM, VMEM, HBM] + [HBM] * len(weights),
        out_specs=[HBM] * ways + [VMEM] * len(others),
        out_shape=[jax.ShapeDtypeStruct(part, BF16)] * ways + others,
        scratch_shapes=[pltpu.VMEM(w.shape, w.dtype) for w in weights]
        + [
            pltpu.VMEM((rows, width), BF16),
            pltpu.VMEM((ways, *part), BF16),
            pltpu.VMEM((ways, *share), BF16),
            pltpu.SemaphoreType.DMA((len(weights),)),
            pltpu.SemaphoreType.DMA((patches // piece,)),
            pltpu.SemaphoreType.DMA((ways,)),
        ],
        compiler_params=pltpu.CompilerParams(vmem_limit_bytes=60 * 2**20),
        cost_estimate=pl.CostEstimate(flops=8 * rows * width * width, bytes_accessed=10 * 2**20, transcendentals=rows * width),
        name="local_part",
    )(scale, gain, x, *weights)
    return list(outs[:ways]), list(outs[ways:])


def state_kernel(count, proj_ref, *refs):
    pieces, (state_ref, share_ref) = refs[:count], refs[count:]
    state = sum(p[...].astype(F32) for p in pieces).astype(BF16)
    state_ref[...] = state
    patches = share_ref.shape[0]
    width = proj_ref.shape[1]
    for b in range(state.shape[0] // patches):
        share_ref[:, b * width : (b + 1) * width] = dot(state[b * patches : (b + 1) * patches], proj_ref[...]).astype(BF16)


def finish_state(proj, pieces, own):
    rows, width = pieces[0].shape
    return pl.pallas_call(
        functools.partial(state_kernel, len(pieces)),
        in_specs=[VMEM] * (1 + len(pieces)),
        out_specs=(VMEM, VMEM),
        out_shape=(
            jax.ShapeDtypeStruct((rows, width), BF16),
            jax.ShapeDtypeStruct((rows // own, own * proj.shape[1]), BF16),
        ),
        compiler_params=pltpu.CompilerParams(vmem_limit_bytes=8 * 2**20),
        name="finish_state",
    )(proj, *pieces)


def fetch_kernel(source, held, sems):
    parts = source.shape[0]
    copies = [pltpu.make_async_copy(source.at[i], held.at[i], sems.at[i]) for i in range(parts)]
    for copy in copies:
        copy.start()
    for copy in copies:
        copy.wait()


def fetch(weight):
    return pl.pallas_call(
        fetch_kernel,
        in_specs=[HBM],
        out_specs=VMEM,
        out_shape=pltpu.VMEM(weight.shape, weight.dtype),
        scratch_shapes=[pltpu.SemaphoreType.DMA((weight.shape[0],))],
        compiler_params=pltpu.CompilerParams(vmem_limit_bytes=50 * 2**20),
        name="fetch",
    )(weight)


def heads_kernel(depth, core_ref, ids_ref, gain_ref, *refs):
    ways = gain_ref.shape[0]
    early, late, weight, outs = refs[:ways], refs[ways : 2 * ways], refs[2 * ways], refs[2 * ways + 1 :]
    width = early[0].shape[1]
    values = [jnp.concatenate([a[...], b[...]], axis=0).astype(F32) for a, b in zip(early, late)]
    square = sum(jnp.sum(v * v, axis=-1, keepdims=True) for v in values)
    factor = lax.rsqrt(square / (ways * width) + EPSILON)
    normed = [(v * factor * gain_ref[ids_ref[c]]).astype(BF16) for c, v in enumerate(values)]
    size = outs[0].shape[1] // 3
    for kind in range(3):
        for i, out in ((1, outs[1]), (0, outs[0])):
            columns = pl.ds(pl.multiple_of((core_ref[0] ^ i) * size, size), size)
            mixed = sum(
                dot(n, weight[kind, pl.ds(pl.multiple_of(ids_ref[c] * width, width), width), columns])
                for c, n in enumerate(normed)
            )
            if kind < 2:
                mixed = jnp.concatenate([unit(mixed[:, c : c + depth]) for c in range(0, size, depth)], axis=1)
            out[:, kind * size : (kind + 1) * size] = mixed.astype(BF16)


def global_heads(depth, core, ids, gain, early, late, qkv):
    shape = jax.ShapeDtypeStruct((2 * early[0].shape[0], 3 * qkv.shape[2] // 2), BF16)
    return pl.pallas_call(
        functools.partial(heads_kernel, depth),
        in_specs=[SMEM, SMEM] + [VMEM] * (2 + len(early) + len(late)),
        out_specs=(VMEM, VMEM),
        out_shape=(shape, shape),
        compiler_params=pltpu.CompilerParams(vmem_limit_bytes=8 * 2**20),
        name="global_heads",
    )(core, ids, gain, *early, *late, qkv)


def attend_kernel(depth, me_ref, ids_ref, scale_ref, kept_ref, given_ref, *refs):
    pieces, (own_ref, other_ref) = refs[:-2], refs[-2:]
    rows = kept_ref.shape[0]
    size = own_ref.shape[1]
    heads = size // depth
    me = me_ref[0]

    def places(index, shape, axis):
        row = lax.broadcasted_iota(jnp.int32, shape, axis)
        return jnp.where(row < rows, index * rows + row, (index ^ 1) * rows + row - rows)

    at = places(me, (2 * rows, 1), 0)
    seen = [places(i, (1, 2 * rows), 1) <= at for i in [me] + [ids_ref[p + 1] for p in range(len(pieces))]]
    own = jnp.concatenate([kept_ref[...], given_ref[...]], axis=0)
    query = own[:, :size]
    pieces = [own[:, size:]] + [p[...] for p in pieces]
    for h in range(heads):
        cut = slice(h * depth, (h + 1) * depth)
        factor = scale_ref[(me % 2) * heads + h] / math.sqrt(depth)
        scores = [jnp.where(s, dot_t(query[:, cut], p[:, cut]) * factor, NEGATIVE) for s, p in zip(seen, pieces)]
        top = functools.reduce(jnp.maximum, [jnp.max(s, axis=-1, keepdims=True) for s in scores])
        weights = [jnp.exp(s - top) for s in scores]
        total = sum(jnp.sum(w, axis=-1, keepdims=True) for w in weights)
        values = slice(size + h * depth, size + (h + 1) * depth)
        summed = sum(dot(w.astype(BF16), p[:, values]) for w, p in zip(weights, pieces))
        attended = (summed / total).astype(BF16)
        own_ref[:, cut] = attended[:rows]
        other_ref[:, cut] = attended[rows:]


def attend(depth, me, ids, scale, kept, given, pieces):
    rows = kept.shape[0]
    shape = jax.ShapeDtypeStruct((rows, kept.shape[1] // 3), BF16)
    return pl.pallas_call(
        functools.partial(attend_kernel, depth),
        in_specs=[SMEM, SMEM, SMEM] + [VMEM] * (2 + len(pieces)),
        out_specs=(VMEM, VMEM),
        out_shape=(shape, shape),
        compiler_params=pltpu.CompilerParams(vmem_limit_bytes=20 * 2**20),
        cost_estimate=BRIEF,
        name="attend",
    )(me, ids, scale, kept, given, *pieces)


def project_kernel(core_ref, slots_ref, own_ref, other_ref, proj_ref, *outs):
    size = own_ref.shape[1]
    own_rows = pl.ds(pl.multiple_of(core_ref[0] * size, size), size)
    other_rows = pl.ds(pl.multiple_of((core_ref[0] ^ 1) * size, size), size)
    for slot, out in enumerate(outs):
        width = out.shape[1]
        columns = pl.ds(pl.multiple_of(slots_ref[slot] * width, width), width)
        out[...] = (dot(own_ref[...], proj_ref[own_rows, columns]) + dot(other_ref[...], proj_ref[other_rows, columns])).astype(BF16)


def project(core, slots, own, other, proj):
    ways = slots.shape[0]
    return pl.pallas_call(
        project_kernel,
        in_specs=[SMEM, SMEM] + [VMEM] * 3,
        out_specs=[VMEM] * ways,
        out_shape=[jax.ShapeDtypeStruct((own.shape[0], proj.shape[1] // ways), BF16)] * ways,
        compiler_params=pltpu.CompilerParams(vmem_limit_bytes=6 * 2**20),
        cost_estimate=BRIEF,
        name="project",
    )(core, slots, own, other, proj)


def result_kernel(count, order_ref, own_ref, *refs):
    pieces, (result_ref, routed_ref) = refs[:count], refs[count:]
    total = own_ref[...].astype(F32) + sum(p[...].astype(F32) for p in pieces)
    result = total.astype(BF16)
    result_ref[...] = result
    routed_ref[...] = dot(order_ref[...], result).astype(BF16)


def finish_result(order, residual, pieces):
    shape = jax.ShapeDtypeStruct(residual.shape, BF16)
    return pl.pallas_call(
        functools.partial(result_kernel, len(pieces)),
        in_specs=[VMEM] * (2 + len(pieces)),
        out_specs=(VMEM, VMEM),
        out_shape=(shape, shape),
        compiler_params=pltpu.CompilerParams(vmem_limit_bytes=4 * 2**20),
        cost_estimate=BRIEF,
        name="finish_result",
    )(order, residual, *pieces)


def bytes_kernel(count, result_ref, proj_ref, *refs):
    sources, (out_ref, held, sems) = refs[:count], refs[count:]
    copies = [pltpu.make_async_copy(p, held.at[i], sems.at[i]) for i, p in enumerate(sources)]
    for copy in copies:
        copy.start()
    rows = result_ref.shape[0]
    half = rows // 2
    width = proj_ref.shape[0]
    own = out_ref.shape[0] // rows
    back = [dot(result_ref[:, b * width : (b + 1) * width], proj_ref[...]) for b in range(own)]
    back = jnp.concatenate([b[:half] for b in back] + [b[half:] for b in back], axis=0)
    at = lax.broadcasted_iota(jnp.int32, (rows * own, rows * own), 0)
    to = lax.broadcasted_iota(jnp.int32, (rows * own, rows * own), 1)
    patch = at // own
    order = (to == patch // half * half * own + at % own * half + patch % half).astype(F32).astype(BF16)
    for copy in copies:
        copy.wait()
    late = sum(held[i].astype(F32) for i in range(1, count)).astype(BF16)
    state = jnp.concatenate([held[0], late], axis=0).astype(F32)
    out_ref[...] = dot(order, (state + back).astype(BF16)).astype(BF16)


def finish_bytes(result, proj, pieces):
    rows, width = pieces[0].shape
    return pl.pallas_call(
        functools.partial(bytes_kernel, len(pieces)),
        in_specs=[VMEM, VMEM] + [pl.BlockSpec(memory_space=pl.ANY)] * len(pieces),
        out_specs=VMEM,
        out_shape=jax.ShapeDtypeStruct((2 * rows, width), BF16),
        scratch_shapes=[pltpu.VMEM((len(pieces), rows, width), BF16), pltpu.SemaphoreType.DMA((len(pieces),))],
        compiler_params=pltpu.CompilerParams(vmem_limit_bytes=16 * 2**20),
        cost_estimate=BRIEF,
        name="finish_bytes",
    )(result, proj, *pieces)


def shift(value, axis, step):
    count = lax.axis_size(axis)
    return lax.ppermute(value, axis, [(i, (i + step) % count) for i in range(count)])


def scatter(chunks, axis):
    return [chunks[0]] + [shift(chunk, axis, step) for step, chunk in enumerate(chunks[1:], 1)]


def shift_slots(axis):
    count = lax.axis_size(axis)
    return ((lax.axis_index(axis) + jnp.arange(count)) % count).astype(jnp.int32)


def gather(value, axis):
    return [value] + [shift(value, axis, step) for step in range(1, lax.axis_size(axis))]


def swap_cores(value, axis):
    return lax.ppermute(value, axis, [(i, i ^ 1) for i in range(lax.axis_size(axis))])


def twin_ids(axis):
    count = lax.axis_size(axis)
    return ((lax.axis_index(axis) - 2 * jnp.arange(count // 2)) % count).astype(jnp.int32)


def owner_order(owners, source, patches):
    listed = lax.dynamic_index_in_dim(owners, source, 0, keepdims=False)
    count = listed.shape[0]
    block = patches // count
    index = jnp.arange(count, dtype=jnp.int32)
    before = (listed[None, :] < listed[:, None]) | (
        (listed[None, :] == listed[:, None]) & (index[None, :] < index[:, None])
    )
    slot = jnp.sum(before, axis=1).astype(jnp.int32)
    row = jnp.arange(patches, dtype=jnp.int32)
    spread = jnp.sum(jnp.where(row[:, None] // block == index[None, :], slot[None, :], 0), axis=1).astype(jnp.int32)
    place = spread * block + row % block
    return (row[:, None] == place[None, :]).astype(BF16)


def on_device(
    byte_in,
    local_gain,
    local_qkv,
    local_out,
    mlp_up,
    mlp_down,
    local_scale,
    patch_proj,
    global_gain,
    global_qkv,
    global_out,
    global_scale,
    back_proj,
    owners,
):
    patches, span, width = byte_in.shape
    ways = lax.axis_size("head")
    own = span // ways
    me = lax.axis_index("head").astype(jnp.int32)
    seq = lax.axis_index("seq").astype(jnp.int32)
    depth = global_qkv.shape[2] // global_scale.shape[0]

    slots = shift_slots("head")
    rows = byte_in.reshape(-1, width)
    weights = [jnp.transpose(local_qkv, (1, 0, 2)), mlp_up, local_out, mlp_down, patch_proj]
    gain = local_gain.reshape(1, -1)
    early, _ = local_part(local_scale, rows, gain, weights, span, ways, False)
    early = scatter(early, "head")
    parts, chunks = local_part(local_scale, rows, gain, weights, span, ways, True)
    chunks, early[1] = lax.optimization_barrier((chunks, early[1]))
    chunks = scatter(chunks, "head")
    early, early_share = finish_state(patch_proj, early, own)
    early_shares = gather(early_share, "head")
    late_share = sum(p.astype(F32) for p in chunks).astype(BF16)
    weight = jnp.transpose(global_qkv, (1, 0, 2))
    weight, late_share, parts = lax.optimization_barrier((weight, late_share, parts))
    late_shares = gather(late_share, "head")
    residual = jnp.concatenate([early_share, late_share], axis=0)
    ids = (me - jnp.arange(ways, dtype=jnp.int32)) % ways
    core = (seq % 2).reshape(1)
    kept, given = global_heads(depth, core, ids, global_gain.reshape(ways, 1, -1), early_shares, late_shares, fetch(weight))
    received = swap_cores(given, "seq")
    parts[1] = shift(parts[1], "head", 1)
    received, *parts = lax.optimization_barrier((received, *parts))
    half = kept.shape[1] // 3
    keyed = jnp.concatenate([kept[:, half:], received[:, half:]], axis=0)
    pieces = [shift(keyed, "seq", 2 * step) for step in range(1, lax.axis_size("seq") // 2)]
    parts[2:] = [shift(part, "head", step) for step, part in enumerate(parts[2:], 2)]
    own_heads, other_heads = attend(depth, seq.reshape(1), twin_ids("seq"), global_scale, kept, received, pieces)
    other_heads, parts[2:] = lax.optimization_barrier((swap_cores(other_heads, "seq"), parts[2:]))
    updates = scatter(project(core, slots, own_heads, other_heads, global_out), "head")
    result, routed = finish_result(owner_order(owners, seq, patches), residual, updates)
    global_state = lax.all_to_all(routed, "seq", split_axis=0, concat_axis=0, tiled=True)
    byte_out = finish_bytes(result, back_proj, [early] + parts)
    return byte_out.reshape(patches, own, width), global_state


def solution(mesh):
    placed = (
        P("seq", None, None),
        P(),
        P(None, None, "head"),
        P("head", None),
        P(None, "head"),
        P("head", None),
        P("head"),
        P(),
        P(),
        P(None, None, "head"),
        P("head", None),
        P("head"),
        P(),
        P(),
    )
    return jax.shard_map(
        on_device,
        mesh=mesh,
        in_specs=placed,
        out_specs=(P("seq", "head", None), P("seq", "head")),
        check_vma=False,
    )
```

```python
import functools
import math

import jax
import jax.numpy as jnp
from jax import lax
from jax.experimental import pallas as pl
from jax.experimental.pallas import tpu as pltpu
from jax.sharding import PartitionSpec as P

EPSILON = 1e-06
NEGATIVE = -1e30
F32 = jnp.float32
BF16 = jnp.bfloat16
BRIEF = pl.CostEstimate(flops=1, bytes_accessed=1, transcendentals=0)
VMEM = pl.BlockSpec(memory_space=pltpu.VMEM)
HBM = pl.BlockSpec(memory_space=pltpu.HBM)
SMEM = pl.BlockSpec(memory_space=pltpu.SMEM)


def dot(left, right):
    return jnp.dot(left, right, preferred_element_type=F32)


def dot_t(left, right):
    return lax.dot_general(left, right, (((1,), (1,)), ((), ())), preferred_element_type=F32)


def unit(values):
    return (values * lax.rsqrt(jnp.mean(values * values, axis=-1, keepdims=True) + EPSILON)).astype(BF16)


def gelu(values):
    inner = math.sqrt(2.0 / math.pi) * (values + 0.044715 * (values * values * values))
    return 0.5 * values * (1.0 + jnp.tanh(inner))


def local_kernel(span, ways, piece, last, scale_ref, gain_ref, x_hbm, *refs):
    sources, parts, others = refs[:5], refs[5 : 5 + ways], refs[5 + ways : -11]
    held, (x_ref, part_ref, share_ref, in_sem, x_sem, part_sem) = refs[-11:-6], refs[-6:]
    patches = share_ref.shape[1]
    own = span // ways
    rows = piece * span
    pieces = patches // piece
    cuts = [slice(i * rows, (i + 1) * rows) for i in range(pieces)]
    skip = x_ref.shape[0] if last else 0
    loads = [
        pltpu.make_async_copy(x_hbm.at[pl.ds(skip + c.start, rows)], x_ref.at[pl.ds(c.start, rows)], x_sem.at[i])
        for i, c in enumerate(cuts)
    ]
    loads += [pltpu.make_async_copy(s, h, in_sem.at[i]) for i, (s, h) in enumerate(zip(sources, held))]
    for copy in loads:
        copy.start()
    me = lax.axis_index("head")
    at = lax.broadcasted_iota(jnp.int32, (rows, rows), 0)
    to = lax.broadcasted_iota(jnp.int32, (rows, rows), 1)
    order = (to == (at % piece) * span + at // piece).astype(F32).astype(BF16)
    kept = lax.broadcasted_iota(jnp.int32, (rows, 1), 0) // piece // own == me
    for copy in loads:
        copy.wait()
    qkv_ref, up_ref, out_ref, down_ref, proj_ref = held
    xs, normed = [], []
    for cut in cuts:
        x = dot(order, x_ref[cut])
        xs.append(jnp.where(kept, x, 0.0).astype(BF16))
        factor = lax.rsqrt(jnp.mean(x * x, axis=-1, keepdims=True) + EPSILON)
        normed.append((x * factor * gain_ref[...]).astype(BF16))
    xs, normed = jnp.concatenate(xs, axis=0), jnp.concatenate(normed, axis=0)
    query, key, value = (dot(normed, qkv_ref[i]) for i in range(3))
    seen = (at % piece == to % piece) & (to <= at)
    heads = scale_ref.shape[0]
    depth = query.shape[1] // heads
    attended = []
    for cut in cuts:
        columns = []
        for h in range(heads):
            head = slice(h * depth, (h + 1) * depth)
            scores = dot_t(unit(query[cut, head]), unit(key[cut, head])) * (scale_ref[h] / math.sqrt(depth))
            scores = jnp.where(seen, scores, NEGATIVE)
            weights = jnp.exp(scores - jnp.max(scores, axis=-1, keepdims=True))
            total = jnp.sum(weights, axis=-1, keepdims=True)
            columns.append((dot(weights.astype(BF16), value[cut, head].astype(BF16)) / total).astype(BF16))
        attended.append(jnp.concatenate(columns, axis=1))
    act = gelu(dot(normed, up_ref[...])).astype(BF16)
    mixed = jnp.concatenate([jnp.concatenate(attended, axis=0), act], axis=1)
    partial = dot(mixed, jnp.concatenate([out_ref[...], down_ref[...]], axis=0)) + xs.astype(F32)
    partial = partial.astype(BF16)
    for i, cut in enumerate(cuts):
        for b in range(span):
            put = (b % own) * patches + i * piece
            part_ref[b // own, put : put + piece] = partial[cut][b * piece : (b + 1) * piece]
    stores = []
    for slot, part in enumerate(parts):
        stores.append(pltpu.make_async_copy(part_ref.at[lax.rem(me + slot, ways)], part, part_sem.at[slot]))
        stores[-1].start()
    if last:
        share = dot(partial, proj_ref[...]).astype(BF16)
        size = share.shape[1]
        for i, cut in enumerate(cuts):
            for b in range(span):
                put = slice((b % own) * size, (b % own + 1) * size)
                share_ref[b // own, i * piece : (i + 1) * piece, put] = share[cut][b * piece : (b + 1) * piece]
        for slot, out in enumerate(others):
            out[...] = share_ref[lax.rem(me + slot, ways)]
    for copy in stores:
        copy.wait()


def local_part(scale, x, gain, weights, span, ways, last):
    rows, width = x.shape[0] // 2, x.shape[1]
    patches = rows // span
    own = span // ways
    piece = math.gcd(patches, 32)
    part = (own * patches, width)
    share = (patches, own * weights[-1].shape[1])
    others = [pltpu.VMEM(share, BF16)] * (ways if last else 0)
    outs = pl.pallas_call(
        functools.partial(local_kernel, span, ways, piece, last),
        in_specs=[SMEM, VMEM, HBM] + [HBM] * len(weights),
        out_specs=[HBM] * ways + [VMEM] * len(others),
        out_shape=[jax.ShapeDtypeStruct(part, BF16)] * ways + others,
        scratch_shapes=[pltpu.VMEM(w.shape, w.dtype) for w in weights]
        + [
            pltpu.VMEM((rows, width), BF16),
            pltpu.VMEM((ways, *part), BF16),
            pltpu.VMEM((ways, *share), BF16),
            pltpu.SemaphoreType.DMA((len(weights),)),
            pltpu.SemaphoreType.DMA((patches // piece,)),
            pltpu.SemaphoreType.DMA((ways,)),
        ],
        compiler_params=pltpu.CompilerParams(vmem_limit_bytes=60 * 2**20),
        cost_estimate=pl.CostEstimate(flops=8 * rows * width * width, bytes_accessed=10 * 2**20, transcendentals=rows * width),
        name="local_part",
    )(scale, gain, x, *weights)
    return list(outs[:ways]), list(outs[ways:])


def state_kernel(count, proj_ref, *refs):
    pieces, (state_ref, share_ref) = refs[:count], refs[count:]
    state = sum(p[...].astype(F32) for p in pieces).astype(BF16)
    state_ref[...] = state
    patches = share_ref.shape[0]
    width = proj_ref.shape[1]
    for b in range(state.shape[0] // patches):
        share_ref[:, b * width : (b + 1) * width] = dot(state[b * patches : (b + 1) * patches], proj_ref[...]).astype(BF16)


def finish_state(proj, pieces, own):
    rows, width = pieces[0].shape
    return pl.pallas_call(
        functools.partial(state_kernel, len(pieces)),
        in_specs=[VMEM] * (1 + len(pieces)),
        out_specs=(VMEM, VMEM),
        out_shape=(
            jax.ShapeDtypeStruct((rows, width), BF16),
            jax.ShapeDtypeStruct((rows // own, own * proj.shape[1]), BF16),
        ),
        compiler_params=pltpu.CompilerParams(vmem_limit_bytes=8 * 2**20),
        name="finish_state",
    )(proj, *pieces)


def fetch_kernel(source, held, sems):
    parts = source.shape[0]
    copies = [pltpu.make_async_copy(source.at[i], held.at[i], sems.at[i]) for i in range(parts)]
    for copy in copies:
        copy.start()
    for copy in copies:
        copy.wait()


def fetch(weight):
    return pl.pallas_call(
        fetch_kernel,
        in_specs=[HBM],
        out_specs=VMEM,
        out_shape=pltpu.VMEM(weight.shape, weight.dtype),
        scratch_shapes=[pltpu.SemaphoreType.DMA((weight.shape[0],))],
        compiler_params=pltpu.CompilerParams(vmem_limit_bytes=50 * 2**20),
        name="fetch",
    )(weight)


def heads_kernel(depth, core_ref, ids_ref, gain_ref, *refs):
    ways = gain_ref.shape[0]
    early, late, weight, outs = refs[:ways], refs[ways : 2 * ways], refs[2 * ways], refs[2 * ways + 1 :]
    width = early[0].shape[1]
    values = [jnp.concatenate([a[...], b[...]], axis=0).astype(F32) for a, b in zip(early, late)]
    square = sum(jnp.sum(v * v, axis=-1, keepdims=True) for v in values)
    factor = lax.rsqrt(square / (ways * width) + EPSILON)
    normed = [(v * factor * gain_ref[ids_ref[c]]).astype(BF16) for c, v in enumerate(values)]
    size = outs[0].shape[1] // 3
    for kind in range(3):
        for i, out in ((1, outs[1]), (0, outs[0])):
            columns = pl.ds(pl.multiple_of((core_ref[0] ^ i) * size, size), size)
            mixed = sum(
                dot(n, weight[kind, pl.ds(pl.multiple_of(ids_ref[c] * width, width), width), columns])
                for c, n in enumerate(normed)
            )
            if kind < 2:
                mixed = jnp.concatenate([unit(mixed[:, c : c + depth]) for c in range(0, size, depth)], axis=1)
            out[:, kind * size : (kind + 1) * size] = mixed.astype(BF16)


def global_heads(depth, core, ids, gain, early, late, qkv):
    shape = jax.ShapeDtypeStruct((2 * early[0].shape[0], 3 * qkv.shape[2] // 2), BF16)
    return pl.pallas_call(
        functools.partial(heads_kernel, depth),
        in_specs=[SMEM, SMEM] + [VMEM] * (2 + len(early) + len(late)),
        out_specs=(VMEM, VMEM),
        out_shape=(shape, shape),
        compiler_params=pltpu.CompilerParams(vmem_limit_bytes=8 * 2**20),
        name="global_heads",
    )(core, ids, gain, *early, *late, qkv)


def attend_kernel(depth, me_ref, ids_ref, scale_ref, kept_ref, given_ref, *refs):
    pieces, (own_ref, other_ref) = refs[:-2], refs[-2:]
    rows = kept_ref.shape[0]
    size = own_ref.shape[1]
    heads = size // depth
    me = me_ref[0]

    def places(index, shape, axis):
        row = lax.broadcasted_iota(jnp.int32, shape, axis)
        return jnp.where(row < rows, index * rows + row, (index ^ 1) * rows + row - rows)

    at = places(me, (2 * rows, 1), 0)
    seen = [places(i, (1, 2 * rows), 1) <= at for i in [me] + [ids_ref[p + 1] for p in range(len(pieces))]]
    own = jnp.concatenate([kept_ref[...], given_ref[...]], axis=0)
    query = own[:, :size]
    pieces = [own[:, size:]] + [p[...] for p in pieces]
    for h in range(heads):
        cut = slice(h * depth, (h + 1) * depth)
        factor = scale_ref[(me % 2) * heads + h] / math.sqrt(depth)
        scores = [jnp.where(s, dot_t(query[:, cut], p[:, cut]) * factor, NEGATIVE) for s, p in zip(seen, pieces)]
        top = functools.reduce(jnp.maximum, [jnp.max(s, axis=-1, keepdims=True) for s in scores])
        weights = [jnp.exp(s - top) for s in scores]
        total = sum(jnp.sum(w, axis=-1, keepdims=True) for w in weights)
        values = slice(size + h * depth, size + (h + 1) * depth)
        summed = sum(dot(w.astype(BF16), p[:, values]) for w, p in zip(weights, pieces))
        attended = (summed / total).astype(BF16)
        own_ref[:, cut] = attended[:rows]
        other_ref[:, cut] = attended[rows:]


def attend(depth, me, ids, scale, kept, given, pieces):
    rows = kept.shape[0]
    shape = jax.ShapeDtypeStruct((rows, kept.shape[1] // 3), BF16)
    return pl.pallas_call(
        functools.partial(attend_kernel, depth),
        in_specs=[SMEM, SMEM, SMEM] + [VMEM] * (2 + len(pieces)),
        out_specs=(VMEM, VMEM),
        out_shape=(shape, shape),
        compiler_params=pltpu.CompilerParams(vmem_limit_bytes=20 * 2**20),
        cost_estimate=BRIEF,
        name="attend",
    )(me, ids, scale, kept, given, *pieces)


def project_kernel(core_ref, slots_ref, own_ref, other_ref, proj_ref, *outs):
    size = own_ref.shape[1]
    own_rows = pl.ds(pl.multiple_of(core_ref[0] * size, size), size)
    other_rows = pl.ds(pl.multiple_of((core_ref[0] ^ 1) * size, size), size)
    for slot, out in enumerate(outs):
        width = out.shape[1]
        columns = pl.ds(pl.multiple_of(slots_ref[slot] * width, width), width)
        out[...] = (dot(own_ref[...], proj_ref[own_rows, columns]) + dot(other_ref[...], proj_ref[other_rows, columns])).astype(BF16)


def project(core, slots, own, other, proj):
    ways = slots.shape[0]
    return pl.pallas_call(
        project_kernel,
        in_specs=[SMEM, SMEM] + [VMEM] * 3,
        out_specs=[VMEM] * ways,
        out_shape=[jax.ShapeDtypeStruct((own.shape[0], proj.shape[1] // ways), BF16)] * ways,
        compiler_params=pltpu.CompilerParams(vmem_limit_bytes=6 * 2**20),
        cost_estimate=BRIEF,
        name="project",
    )(core, slots, own, other, proj)


def result_kernel(count, order_ref, own_ref, *refs):
    pieces, (result_ref, routed_ref) = refs[:count], refs[count:]
    total = own_ref[...].astype(F32) + sum(p[...].astype(F32) for p in pieces)
    result = total.astype(BF16)
    result_ref[...] = result
    routed_ref[...] = dot(order_ref[...], result).astype(BF16)


def finish_result(order, residual, pieces):
    shape = jax.ShapeDtypeStruct(residual.shape, BF16)
    return pl.pallas_call(
        functools.partial(result_kernel, len(pieces)),
        in_specs=[VMEM] * (2 + len(pieces)),
        out_specs=(VMEM, VMEM),
        out_shape=(shape, shape),
        compiler_params=pltpu.CompilerParams(vmem_limit_bytes=4 * 2**20),
        cost_estimate=BRIEF,
        name="finish_result",
    )(order, residual, *pieces)


def bytes_kernel(count, result_ref, proj_ref, *refs):
    sources, (out_ref, held, sems) = refs[:count], refs[count:]
    copies = [pltpu.make_async_copy(p, held.at[i], sems.at[i]) for i, p in enumerate(sources)]
    for copy in copies:
        copy.start()
    rows = result_ref.shape[0]
    half = rows // 2
    width = proj_ref.shape[0]
    own = out_ref.shape[0] // rows
    back = [dot(result_ref[:, b * width : (b + 1) * width], proj_ref[...]) for b in range(own)]
    back = jnp.concatenate([b[:half] for b in back] + [b[half:] for b in back], axis=0)
    at = lax.broadcasted_iota(jnp.int32, (rows * own, rows * own), 0)
    to = lax.broadcasted_iota(jnp.int32, (rows * own, rows * own), 1)
    patch = at // own
    order = (to == patch // half * half * own + at % own * half + patch % half).astype(F32).astype(BF16)
    for copy in copies:
        copy.wait()
    late = sum(held[i].astype(F32) for i in range(1, count)).astype(BF16)
    state = jnp.concatenate([held[0], late], axis=0).astype(F32)
    out_ref[...] = dot(order, (state + back).astype(BF16)).astype(BF16)


def finish_bytes(result, proj, pieces):
    rows, width = pieces[0].shape
    return pl.pallas_call(
        functools.partial(bytes_kernel, len(pieces)),
        in_specs=[VMEM, VMEM] + [pl.BlockSpec(memory_space=pl.ANY)] * len(pieces),
        out_specs=VMEM,
        out_shape=jax.ShapeDtypeStruct((2 * rows, width), BF16),
        scratch_shapes=[pltpu.VMEM((len(pieces), rows, width), BF16), pltpu.SemaphoreType.DMA((len(pieces),))],
        compiler_params=pltpu.CompilerParams(vmem_limit_bytes=16 * 2**20),
        cost_estimate=BRIEF,
        name="finish_bytes",
    )(result, proj, *pieces)


def shift(value, axis, step):
    count = lax.axis_size(axis)
    return lax.ppermute(value, axis, [(i, (i + step) % count) for i in range(count)])


def scatter(chunks, axis):
    return [chunks[0]] + [shift(chunk, axis, step) for step, chunk in enumerate(chunks[1:], 1)]


def shift_slots(axis):
    count = lax.axis_size(axis)
    return ((lax.axis_index(axis) + jnp.arange(count)) % count).astype(jnp.int32)


def gather(value, axis):
    return [value] + [shift(value, axis, step) for step in range(1, lax.axis_size(axis))]


def swap_cores(value, axis):
    return lax.ppermute(value, axis, [(i, i ^ 1) for i in range(lax.axis_size(axis))])


def twin_ids(axis):
    count = lax.axis_size(axis)
    return ((lax.axis_index(axis) - 2 * jnp.arange(count // 2)) % count).astype(jnp.int32)


def owner_order(owners, source, patches):
    listed = lax.dynamic_index_in_dim(owners, source, 0, keepdims=False)
    count = listed.shape[0]
    block = patches // count
    index = jnp.arange(count, dtype=jnp.int32)
    before = (listed[None, :] < listed[:, None]) | (
        (listed[None, :] == listed[:, None]) & (index[None, :] < index[:, None])
    )
    slot = jnp.sum(before, axis=1).astype(jnp.int32)
    row = jnp.arange(patches, dtype=jnp.int32)
    spread = jnp.sum(jnp.where(row[:, None] // block == index[None, :], slot[None, :], 0), axis=1).astype(jnp.int32)
    place = spread * block + row % block
    return (row[:, None] == place[None, :]).astype(BF16)


def on_device(
    byte_in,
    local_gain,
    local_qkv,
    local_out,
    mlp_up,
    mlp_down,
    local_scale,
    patch_proj,
    global_gain,
    global_qkv,
    global_out,
    global_scale,
    back_proj,
    owners,
):
    patches, span, width = byte_in.shape
    ways = lax.axis_size("head")
    own = span // ways
    me = lax.axis_index("head").astype(jnp.int32)
    seq = lax.axis_index("seq").astype(jnp.int32)
    depth = global_qkv.shape[2] // global_scale.shape[0]

    slots = shift_slots("head")
    rows = byte_in.reshape(-1, width)
    weights = [jnp.transpose(local_qkv, (1, 0, 2)), mlp_up, local_out, mlp_down, patch_proj]
    gain = local_gain.reshape(1, -1)
    early, _ = local_part(local_scale, rows, gain, weights, span, ways, False)
    early = scatter(early, "head")
    parts, chunks = local_part(local_scale, rows, gain, weights, span, ways, True)
    chunks, early[1] = lax.optimization_barrier((chunks, early[1]))
    chunks = scatter(chunks, "head")
    early, early_share = finish_state(patch_proj, early, own)
    early_shares = gather(early_share, "head")
    late_share = sum(p.astype(F32) for p in chunks).astype(BF16)
    weight = jnp.transpose(global_qkv, (1, 0, 2))
    weight, late_share = lax.optimization_barrier((weight, late_share))
    late_shares = gather(late_share, "head")
    residual = jnp.concatenate([early_share, late_share], axis=0)
    ids = (me - jnp.arange(ways, dtype=jnp.int32)) % ways
    core = (seq % 2).reshape(1)
    kept, given = global_heads(depth, core, ids, global_gain.reshape(ways, 1, -1), early_shares, late_shares, fetch(weight))
    received = swap_cores(given, "seq")
    received, *parts = lax.optimization_barrier((received, *parts))
    half = kept.shape[1] // 3
    keyed = jnp.concatenate([kept[:, half:], received[:, half:]], axis=0)
    pieces = [shift(keyed, "seq", 2 * step) for step in range(1, lax.axis_size("seq") // 2)]
    parts[2:] = [shift(part, "head", step) for step, part in enumerate(parts[2:], 2)]
    own_heads, other_heads = attend(depth, seq.reshape(1), twin_ids("seq"), global_scale, kept, received, pieces)
    other_heads, parts[2:] = lax.optimization_barrier((swap_cores(other_heads, "seq"), parts[2:]))
    updates = scatter(project(core, slots, own_heads, other_heads, global_out), "head")
    updates, parts[1] = lax.optimization_barrier((updates, parts[1]))
    parts[1] = shift(parts[1], "head", 1)
    result, routed = finish_result(owner_order(owners, seq, patches), residual, updates)
    global_state = lax.all_to_all(routed, "seq", split_axis=0, concat_axis=0, tiled=True)
    byte_out = finish_bytes(result, back_proj, [early] + parts)
    return byte_out.reshape(patches, own, width), global_state


def solution(mesh):
    placed = (
        P("seq", None, None),
        P(),
        P(None, None, "head"),
        P("head", None),
        P(None, "head"),
        P("head", None),
        P("head"),
        P(),
        P(),
        P(None, None, "head"),
        P("head", None),
        P("head"),
        P(),
        P(),
    )
    return jax.shard_map(
        on_device,
        mesh=mesh,
        in_specs=placed,
        out_specs=(P("seq", "head", None), P("seq", "head")),
        check_vma=False,
    )
```

```python
import functools
import math

import jax
import jax.numpy as jnp
from jax import lax
from jax.experimental import pallas as pl
from jax.experimental.pallas import tpu as pltpu
from jax.sharding import PartitionSpec as P

EPSILON = 1e-06
NEGATIVE = -1e30
F32 = jnp.float32
BF16 = jnp.bfloat16
BRIEF = pl.CostEstimate(flops=1, bytes_accessed=1, transcendentals=0)
VMEM = pl.BlockSpec(memory_space=pltpu.VMEM)
HBM = pl.BlockSpec(memory_space=pltpu.HBM)
SMEM = pl.BlockSpec(memory_space=pltpu.SMEM)


def dot(left, right):
    return jnp.dot(left, right, preferred_element_type=F32)


def dot_t(left, right):
    return lax.dot_general(left, right, (((1,), (1,)), ((), ())), preferred_element_type=F32)


def unit(values):
    return (values * lax.rsqrt(jnp.mean(values * values, axis=-1, keepdims=True) + EPSILON)).astype(BF16)


def gelu(values):
    inner = math.sqrt(2.0 / math.pi) * (values + 0.044715 * (values * values * values))
    return 0.5 * values * (1.0 + jnp.tanh(inner))


def local_kernel(span, ways, piece, last, scale_ref, gain_ref, x_hbm, *refs):
    sources, parts, others = refs[:5], refs[5 : 5 + ways], refs[5 + ways : -11]
    held, (x_ref, part_ref, share_ref, in_sem, x_sem, part_sem) = refs[-11:-6], refs[-6:]
    patches = share_ref.shape[1]
    own = span // ways
    rows = piece * span
    pieces = patches // piece
    cuts = [slice(i * rows, (i + 1) * rows) for i in range(pieces)]
    skip = x_ref.shape[0] if last else 0
    loads = [
        pltpu.make_async_copy(x_hbm.at[pl.ds(skip + c.start, rows)], x_ref.at[pl.ds(c.start, rows)], x_sem.at[i])
        for i, c in enumerate(cuts)
    ]
    loads += [pltpu.make_async_copy(s, h, in_sem.at[i]) for i, (s, h) in enumerate(zip(sources, held))]
    for copy in loads:
        copy.start()
    me = lax.axis_index("head")
    at = lax.broadcasted_iota(jnp.int32, (rows, rows), 0)
    to = lax.broadcasted_iota(jnp.int32, (rows, rows), 1)
    order = (to == (at % piece) * span + at // piece).astype(F32).astype(BF16)
    kept = lax.broadcasted_iota(jnp.int32, (rows, 1), 0) // piece // own == me
    for copy in loads:
        copy.wait()
    qkv_ref, up_ref, out_ref, down_ref, proj_ref = held
    xs, normed = [], []
    for cut in cuts:
        x = dot(order, x_ref[cut])
        xs.append(jnp.where(kept, x, 0.0).astype(BF16))
        factor = lax.rsqrt(jnp.mean(x * x, axis=-1, keepdims=True) + EPSILON)
        normed.append((x * factor * gain_ref[...]).astype(BF16))
    xs, normed = jnp.concatenate(xs, axis=0), jnp.concatenate(normed, axis=0)
    query, key, value = (dot(normed, qkv_ref[i]) for i in range(3))
    seen = (at % piece == to % piece) & (to <= at)
    heads = scale_ref.shape[0]
    depth = query.shape[1] // heads
    attended = []
    for cut in cuts:
        columns = []
        for h in range(heads):
            head = slice(h * depth, (h + 1) * depth)
            scores = dot_t(unit(query[cut, head]), unit(key[cut, head])) * (scale_ref[h] / math.sqrt(depth))
            scores = jnp.where(seen, scores, NEGATIVE)
            weights = jnp.exp(scores - jnp.max(scores, axis=-1, keepdims=True))
            total = jnp.sum(weights, axis=-1, keepdims=True)
            columns.append((dot(weights.astype(BF16), value[cut, head].astype(BF16)) / total).astype(BF16))
        attended.append(jnp.concatenate(columns, axis=1))
    act = gelu(dot(normed, up_ref[...])).astype(BF16)
    mixed = jnp.concatenate([jnp.concatenate(attended, axis=0), act], axis=1)
    partial = dot(mixed, jnp.concatenate([out_ref[...], down_ref[...]], axis=0)) + xs.astype(F32)
    partial = partial.astype(BF16)
    for i, cut in enumerate(cuts):
        for b in range(span):
            put = (b % own) * patches + i * piece
            part_ref[b // own, put : put + piece] = partial[cut][b * piece : (b + 1) * piece]
    stores = []
    for slot, part in enumerate(parts):
        stores.append(pltpu.make_async_copy(part_ref.at[lax.rem(me + slot, ways)], part, part_sem.at[slot]))
        stores[-1].start()
    if last:
        share = dot(partial, proj_ref[...]).astype(BF16)
        size = share.shape[1]
        for i, cut in enumerate(cuts):
            for b in range(span):
                put = slice((b % own) * size, (b % own + 1) * size)
                share_ref[b // own, i * piece : (i + 1) * piece, put] = share[cut][b * piece : (b + 1) * piece]
        for slot, out in enumerate(others):
            out[...] = share_ref[lax.rem(me + slot, ways)]
    for copy in stores:
        copy.wait()


def local_part(scale, x, gain, weights, span, ways, last):
    rows, width = x.shape[0] // 2, x.shape[1]
    patches = rows // span
    own = span // ways
    piece = math.gcd(patches, 32)
    part = (own * patches, width)
    share = (patches, own * weights[-1].shape[1])
    others = [pltpu.VMEM(share, BF16)] * (ways if last else 0)
    outs = pl.pallas_call(
        functools.partial(local_kernel, span, ways, piece, last),
        in_specs=[SMEM, VMEM, HBM] + [HBM] * len(weights),
        out_specs=[HBM] * ways + [VMEM] * len(others),
        out_shape=[jax.ShapeDtypeStruct(part, BF16)] * ways + others,
        scratch_shapes=[pltpu.VMEM(w.shape, w.dtype) for w in weights]
        + [
            pltpu.VMEM((rows, width), BF16),
            pltpu.VMEM((ways, *part), BF16),
            pltpu.VMEM((ways, *share), BF16),
            pltpu.SemaphoreType.DMA((len(weights),)),
            pltpu.SemaphoreType.DMA((patches // piece,)),
            pltpu.SemaphoreType.DMA((ways,)),
        ],
        compiler_params=pltpu.CompilerParams(vmem_limit_bytes=60 * 2**20),
        cost_estimate=pl.CostEstimate(flops=8 * rows * width * width, bytes_accessed=10 * 2**20, transcendentals=rows * width),
        name="local_part",
    )(scale, gain, x, *weights)
    return list(outs[:ways]), list(outs[ways:])


def state_kernel(count, proj_ref, *refs):
    pieces, (state_ref, share_ref) = refs[:count], refs[count:]
    state = sum(p[...].astype(F32) for p in pieces).astype(BF16)
    state_ref[...] = state
    patches = share_ref.shape[0]
    width = proj_ref.shape[1]
    for b in range(state.shape[0] // patches):
        share_ref[:, b * width : (b + 1) * width] = dot(state[b * patches : (b + 1) * patches], proj_ref[...]).astype(BF16)


def finish_state(proj, pieces, own):
    rows, width = pieces[0].shape
    return pl.pallas_call(
        functools.partial(state_kernel, len(pieces)),
        in_specs=[VMEM] * (1 + len(pieces)),
        out_specs=(VMEM, VMEM),
        out_shape=(
            jax.ShapeDtypeStruct((rows, width), BF16),
            jax.ShapeDtypeStruct((rows // own, own * proj.shape[1]), BF16),
        ),
        compiler_params=pltpu.CompilerParams(vmem_limit_bytes=8 * 2**20),
        name="finish_state",
    )(proj, *pieces)


def fetch_kernel(source, held, sems):
    parts = source.shape[0]
    copies = [pltpu.make_async_copy(source.at[i], held.at[i], sems.at[i]) for i in range(parts)]
    for copy in copies:
        copy.start()
    for copy in copies:
        copy.wait()


def fetch(weight):
    return pl.pallas_call(
        fetch_kernel,
        in_specs=[HBM],
        out_specs=VMEM,
        out_shape=pltpu.VMEM(weight.shape, weight.dtype),
        scratch_shapes=[pltpu.SemaphoreType.DMA((weight.shape[0],))],
        compiler_params=pltpu.CompilerParams(vmem_limit_bytes=50 * 2**20),
        name="fetch",
    )(weight)


def heads_kernel(depth, core_ref, ids_ref, gain_ref, *refs):
    ways = gain_ref.shape[0]
    early, late, weight, outs = refs[:ways], refs[ways : 2 * ways], refs[2 * ways], refs[2 * ways + 1 :]
    width = early[0].shape[1]
    values = [jnp.concatenate([a[...], b[...]], axis=0).astype(F32) for a, b in zip(early, late)]
    square = sum(jnp.sum(v * v, axis=-1, keepdims=True) for v in values)
    factor = lax.rsqrt(square / (ways * width) + EPSILON)
    normed = [(v * factor * gain_ref[ids_ref[c]]).astype(BF16) for c, v in enumerate(values)]
    size = outs[0].shape[1] // 3
    for kind in range(3):
        for i, out in ((1, outs[1]), (0, outs[0])):
            columns = pl.ds(pl.multiple_of((core_ref[0] ^ i) * size, size), size)
            mixed = sum(
                dot(n, weight[kind, pl.ds(pl.multiple_of(ids_ref[c] * width, width), width), columns])
                for c, n in enumerate(normed)
            )
            if kind < 2:
                mixed = jnp.concatenate([unit(mixed[:, c : c + depth]) for c in range(0, size, depth)], axis=1)
            out[:, kind * size : (kind + 1) * size] = mixed.astype(BF16)


def global_heads(depth, core, ids, gain, early, late, qkv):
    shape = jax.ShapeDtypeStruct((2 * early[0].shape[0], 3 * qkv.shape[2] // 2), BF16)
    return pl.pallas_call(
        functools.partial(heads_kernel, depth),
        in_specs=[SMEM, SMEM] + [VMEM] * (2 + len(early) + len(late)),
        out_specs=(VMEM, VMEM),
        out_shape=(shape, shape),
        compiler_params=pltpu.CompilerParams(vmem_limit_bytes=8 * 2**20),
        name="global_heads",
    )(core, ids, gain, *early, *late, qkv)


def attend_kernel(depth, me_ref, ids_ref, scale_ref, kept_ref, given_ref, *refs):
    pieces, (own_ref, other_ref) = refs[:-2], refs[-2:]
    rows = kept_ref.shape[0]
    size = own_ref.shape[1]
    heads = size // depth
    me = me_ref[0]

    def places(index, shape, axis):
        row = lax.broadcasted_iota(jnp.int32, shape, axis)
        return jnp.where(row < rows, index * rows + row, (index ^ 1) * rows + row - rows)

    at = places(me, (2 * rows, 1), 0)
    seen = [places(i, (1, 2 * rows), 1) <= at for i in [me] + [ids_ref[p + 1] for p in range(len(pieces))]]
    own = jnp.concatenate([kept_ref[...], given_ref[...]], axis=0)
    query = own[:, :size]
    pieces = [own[:, size:]] + [p[...] for p in pieces]
    for h in range(heads):
        cut = slice(h * depth, (h + 1) * depth)
        factor = scale_ref[(me % 2) * heads + h] / math.sqrt(depth)
        scores = [jnp.where(s, dot_t(query[:, cut], p[:, cut]) * factor, NEGATIVE) for s, p in zip(seen, pieces)]
        top = functools.reduce(jnp.maximum, [jnp.max(s, axis=-1, keepdims=True) for s in scores])
        weights = [jnp.exp(s - top) for s in scores]
        total = sum(jnp.sum(w, axis=-1, keepdims=True) for w in weights)
        values = slice(size + h * depth, size + (h + 1) * depth)
        summed = sum(dot(w.astype(BF16), p[:, values]) for w, p in zip(weights, pieces))
        attended = (summed / total).astype(BF16)
        own_ref[:, cut] = attended[:rows]
        other_ref[:, cut] = attended[rows:]


def attend(depth, me, ids, scale, kept, given, pieces):
    rows = kept.shape[0]
    shape = jax.ShapeDtypeStruct((rows, kept.shape[1] // 3), BF16)
    return pl.pallas_call(
        functools.partial(attend_kernel, depth),
        in_specs=[SMEM, SMEM, SMEM] + [VMEM] * (2 + len(pieces)),
        out_specs=(VMEM, VMEM),
        out_shape=(shape, shape),
        compiler_params=pltpu.CompilerParams(vmem_limit_bytes=20 * 2**20),
        cost_estimate=BRIEF,
        name="attend",
    )(me, ids, scale, kept, given, *pieces)


def project_kernel(core_ref, slots_ref, own_ref, other_ref, proj_ref, *outs):
    size = own_ref.shape[1]
    own_rows = pl.ds(pl.multiple_of(core_ref[0] * size, size), size)
    other_rows = pl.ds(pl.multiple_of((core_ref[0] ^ 1) * size, size), size)
    for slot, out in enumerate(outs):
        width = out.shape[1]
        columns = pl.ds(pl.multiple_of(slots_ref[slot] * width, width), width)
        out[...] = (dot(own_ref[...], proj_ref[own_rows, columns]) + dot(other_ref[...], proj_ref[other_rows, columns])).astype(BF16)


def project(core, slots, own, other, proj):
    ways = slots.shape[0]
    return pl.pallas_call(
        project_kernel,
        in_specs=[SMEM, SMEM] + [VMEM] * 3,
        out_specs=[VMEM] * ways,
        out_shape=[jax.ShapeDtypeStruct((own.shape[0], proj.shape[1] // ways), BF16)] * ways,
        compiler_params=pltpu.CompilerParams(vmem_limit_bytes=6 * 2**20),
        cost_estimate=BRIEF,
        name="project",
    )(core, slots, own, other, proj)


def result_kernel(count, order_ref, own_ref, *refs):
    pieces, (result_ref, kept_ref, given_ref) = refs[:count], refs[count:]
    total = own_ref[...].astype(F32) + sum(p[...].astype(F32) for p in pieces)
    result = total.astype(BF16)
    result_ref[...] = result
    routed = dot(order_ref[...], result).astype(BF16)
    half = kept_ref.shape[0]
    kept_ref[...] = routed[:half]
    given_ref[...] = routed[half:]


def finish_result(order, residual, pieces):
    rows, width = residual.shape
    shape = jax.ShapeDtypeStruct(residual.shape, BF16)
    half = jax.ShapeDtypeStruct((rows // 2, width), BF16)
    return pl.pallas_call(
        functools.partial(result_kernel, len(pieces)),
        in_specs=[VMEM] * (2 + len(pieces)),
        out_specs=(VMEM, VMEM, VMEM),
        out_shape=(shape, half, half),
        compiler_params=pltpu.CompilerParams(vmem_limit_bytes=4 * 2**20),
        cost_estimate=BRIEF,
        name="finish_result",
    )(order, residual, *pieces)


def sort_kernel(block, devices, rows_ref, out_ref):
    me = lax.axis_index("seq")
    rows = rows_ref.shape[0]
    to = lax.broadcasted_iota(jnp.int32, (rows, rows), 0)
    at = lax.broadcasted_iota(jnp.int32, (rows, rows), 1)
    twin = lax.rem(me - at // (2 * block) * 2 + devices, devices)
    source = twin ^ (at // block % 2)
    order = (to == source * block + at % block).astype(F32).astype(BF16)
    out_ref[...] = dot(order, rows_ref[...]).astype(BF16)


def sort_rows(rows, devices):
    return pl.pallas_call(
        functools.partial(sort_kernel, rows.shape[0] // devices, devices),
        in_specs=[VMEM],
        out_specs=VMEM,
        out_shape=jax.ShapeDtypeStruct(rows.shape, BF16),
        compiler_params=pltpu.CompilerParams(vmem_limit_bytes=4 * 2**20),
        cost_estimate=BRIEF,
        name="sort_rows",
    )(rows)


def bytes_kernel(count, result_ref, proj_ref, *refs):
    sources, (out_ref, held, sems) = refs[:count], refs[count:]
    copies = [pltpu.make_async_copy(p, held.at[i], sems.at[i]) for i, p in enumerate(sources)]
    for copy in copies:
        copy.start()
    rows = result_ref.shape[0]
    half = rows // 2
    width = proj_ref.shape[0]
    own = out_ref.shape[0] // rows
    back = [dot(result_ref[:, b * width : (b + 1) * width], proj_ref[...]) for b in range(own)]
    back = jnp.concatenate([b[:half] for b in back] + [b[half:] for b in back], axis=0)
    at = lax.broadcasted_iota(jnp.int32, (rows * own, rows * own), 0)
    to = lax.broadcasted_iota(jnp.int32, (rows * own, rows * own), 1)
    patch = at // own
    order = (to == patch // half * half * own + at % own * half + patch % half).astype(F32).astype(BF16)
    for copy in copies:
        copy.wait()
    late = sum(held[i].astype(F32) for i in range(1, count)).astype(BF16)
    state = jnp.concatenate([held[0], late], axis=0).astype(F32)
    out_ref[...] = dot(order, (state + back).astype(BF16)).astype(BF16)


def finish_bytes(result, proj, pieces):
    rows, width = pieces[0].shape
    return pl.pallas_call(
        functools.partial(bytes_kernel, len(pieces)),
        in_specs=[VMEM, VMEM] + [pl.BlockSpec(memory_space=pl.ANY)] * len(pieces),
        out_specs=VMEM,
        out_shape=jax.ShapeDtypeStruct((2 * rows, width), BF16),
        scratch_shapes=[pltpu.VMEM((len(pieces), rows, width), BF16), pltpu.SemaphoreType.DMA((len(pieces),))],
        compiler_params=pltpu.CompilerParams(vmem_limit_bytes=16 * 2**20),
        cost_estimate=BRIEF,
        name="finish_bytes",
    )(result, proj, *pieces)


def shift(value, axis, step):
    count = lax.axis_size(axis)
    return lax.ppermute(value, axis, [(i, (i + step) % count) for i in range(count)])


def scatter(chunks, axis):
    return [chunks[0]] + [shift(chunk, axis, step) for step, chunk in enumerate(chunks[1:], 1)]


def shift_slots(axis):
    count = lax.axis_size(axis)
    return ((lax.axis_index(axis) + jnp.arange(count)) % count).astype(jnp.int32)


def gather(value, axis):
    return [value] + [shift(value, axis, step) for step in range(1, lax.axis_size(axis))]


def swap_cores(value, axis):
    return lax.ppermute(value, axis, [(i, i ^ 1) for i in range(lax.axis_size(axis))])


def twin_ids(axis):
    count = lax.axis_size(axis)
    return ((lax.axis_index(axis) - 2 * jnp.arange(count // 2)) % count).astype(jnp.int32)


def owner_order(owners, source, patches):
    devices, count = owners.shape
    listed = lax.dynamic_index_in_dim(owners, source, 0, keepdims=False)
    block = patches // count
    index = jnp.arange(count, dtype=jnp.int32)
    rank = jnp.sum((listed[None, :] == listed[:, None]) & (index[None, :] < index[:, None]), axis=1).astype(jnp.int32)
    chips = devices // 2
    order = (listed % 2 ^ source % 2) * chips + (listed // 2 - source // 2 + chips) % chips
    slot = order * (count // devices) + rank
    row = jnp.arange(patches, dtype=jnp.int32)
    spread = jnp.sum(jnp.where(row[:, None] // block == index[None, :], slot[None, :], 0), axis=1).astype(jnp.int32)
    place = spread * block + row % block
    return (row[:, None] == place[None, :]).astype(BF16)


def route(kept, given, axis):
    devices = lax.axis_size(axis)
    chips = devices // 2
    width = kept.shape[1]
    received = swap_cores(given, axis)
    bundles = jnp.concatenate([a.reshape(chips, -1, width) for a in (kept, received)], axis=1)
    arrived = [bundles[0]] + [shift(bundles[step], axis, 2 * step) for step in range(1, chips)]
    return sort_rows(jnp.concatenate(arrived, axis=0), devices)


def on_device(
    byte_in,
    local_gain,
    local_qkv,
    local_out,
    mlp_up,
    mlp_down,
    local_scale,
    patch_proj,
    global_gain,
    global_qkv,
    global_out,
    global_scale,
    back_proj,
    owners,
):
    patches, span, width = byte_in.shape
    ways = lax.axis_size("head")
    own = span // ways
    me = lax.axis_index("head").astype(jnp.int32)
    seq = lax.axis_index("seq").astype(jnp.int32)
    depth = global_qkv.shape[2] // global_scale.shape[0]

    slots = shift_slots("head")
    rows = byte_in.reshape(-1, width)
    weights = [jnp.transpose(local_qkv, (1, 0, 2)), mlp_up, local_out, mlp_down, patch_proj]
    gain = local_gain.reshape(1, -1)
    early, _ = local_part(local_scale, rows, gain, weights, span, ways, False)
    early = scatter(early, "head")
    parts, chunks = local_part(local_scale, rows, gain, weights, span, ways, True)
    chunks, early[1] = lax.optimization_barrier((chunks, early[1]))
    chunks = scatter(chunks, "head")
    early, early_share = finish_state(patch_proj, early, own)
    early_shares = gather(early_share, "head")
    late_share = sum(p.astype(F32) for p in chunks).astype(BF16)
    weight = jnp.transpose(global_qkv, (1, 0, 2))
    weight, late_share = lax.optimization_barrier((weight, late_share))
    late_shares = gather(late_share, "head")
    residual = jnp.concatenate([early_share, late_share], axis=0)
    ids = (me - jnp.arange(ways, dtype=jnp.int32)) % ways
    core = (seq % 2).reshape(1)
    kept, given = global_heads(depth, core, ids, global_gain.reshape(ways, 1, -1), early_shares, late_shares, fetch(weight))
    received = swap_cores(given, "seq")
    received, *parts = lax.optimization_barrier((received, *parts))
    half = kept.shape[1] // 3
    keyed = jnp.concatenate([kept[:, half:], received[:, half:]], axis=0)
    pieces = [shift(keyed, "seq", 2 * step) for step in range(1, lax.axis_size("seq") // 2)]
    parts[2:] = [shift(part, "head", step) for step, part in enumerate(parts[2:], 2)]
    own_heads, other_heads = attend(depth, seq.reshape(1), twin_ids("seq"), global_scale, kept, received, pieces)
    other_heads, parts[2:] = lax.optimization_barrier((swap_cores(other_heads, "seq"), parts[2:]))
    updates = scatter(project(core, slots, own_heads, other_heads, global_out), "head")
    updates, parts[1] = lax.optimization_barrier((updates, parts[1]))
    parts[1] = shift(parts[1], "head", 1)
    result, kept, given = finish_result(owner_order(owners, seq, patches), residual, updates)
    global_state = route(kept, given, "seq")
    byte_out = finish_bytes(result, back_proj, [early] + parts)
    return byte_out.reshape(patches, own, width), global_state


def solution(mesh):
    placed = (
        P("seq", None, None),
        P(),
        P(None, None, "head"),
        P("head", None),
        P(None, "head"),
        P("head", None),
        P("head"),
        P(),
        P(),
        P(None, None, "head"),
        P("head", None),
        P("head"),
        P(),
        P(),
    )
    return jax.shard_map(
        on_device,
        mesh=mesh,
        in_specs=placed,
        out_specs=(P("seq", "head", None), P("seq", "head")),
        check_vma=False,
    )
```

```python
import functools
import math

import jax
import jax.numpy as jnp
from jax import lax
from jax.experimental import pallas as pl
from jax.experimental.pallas import tpu as pltpu
from jax.sharding import PartitionSpec as P

EPSILON = 1e-06
NEGATIVE = -1e30
F32 = jnp.float32
BF16 = jnp.bfloat16
BRIEF = pl.CostEstimate(flops=1, bytes_accessed=1, transcendentals=0)
VMEM = pl.BlockSpec(memory_space=pltpu.VMEM)
HBM = pl.BlockSpec(memory_space=pltpu.HBM)
SMEM = pl.BlockSpec(memory_space=pltpu.SMEM)


def dot(left, right):
    return jnp.dot(left, right, preferred_element_type=F32)


def dot_t(left, right):
    return lax.dot_general(left, right, (((1,), (1,)), ((), ())), preferred_element_type=F32)


def unit(values):
    return (values * lax.rsqrt(jnp.mean(values * values, axis=-1, keepdims=True) + EPSILON)).astype(BF16)


def gelu(values):
    inner = math.sqrt(2.0 / math.pi) * (values + 0.044715 * (values * values * values))
    return 0.5 * values * (1.0 + jnp.tanh(inner))


def local_kernel(span, ways, piece, last, scale_ref, gain_ref, x_hbm, *refs):
    sources, parts, others = refs[:5], refs[5 : 5 + ways], refs[5 + ways : -11]
    held, (x_ref, part_ref, share_ref, in_sem, x_sem, part_sem) = refs[-11:-6], refs[-6:]
    patches = share_ref.shape[1]
    own = span // ways
    rows = piece * span
    pieces = patches // piece
    cuts = [slice(i * rows, (i + 1) * rows) for i in range(pieces)]
    skip = x_ref.shape[0] if last else 0
    loads = [
        pltpu.make_async_copy(x_hbm.at[pl.ds(skip + c.start, rows)], x_ref.at[pl.ds(c.start, rows)], x_sem.at[i])
        for i, c in enumerate(cuts)
    ]
    loads += [pltpu.make_async_copy(s, h, in_sem.at[i]) for i, (s, h) in enumerate(zip(sources, held))]
    for copy in loads:
        copy.start()
    me = lax.axis_index("head")
    at = lax.broadcasted_iota(jnp.int32, (rows, rows), 0)
    to = lax.broadcasted_iota(jnp.int32, (rows, rows), 1)
    order = (to == (at % piece) * span + at // piece).astype(F32).astype(BF16)
    kept = lax.broadcasted_iota(jnp.int32, (rows, 1), 0) // piece // own == me
    for copy in loads:
        copy.wait()
    qkv_ref, up_ref, out_ref, down_ref, proj_ref = held
    xs, normed = [], []
    for cut in cuts:
        x = dot(order, x_ref[cut])
        xs.append(jnp.where(kept, x, 0.0).astype(BF16))
        factor = lax.rsqrt(jnp.mean(x * x, axis=-1, keepdims=True) + EPSILON)
        normed.append((x * factor * gain_ref[...]).astype(BF16))
    xs, normed = jnp.concatenate(xs, axis=0), jnp.concatenate(normed, axis=0)
    query, key, value = (dot(normed, qkv_ref[i]) for i in range(3))
    seen = (at % piece == to % piece) & (to <= at)
    heads = scale_ref.shape[0]
    depth = query.shape[1] // heads
    attended = []
    for cut in cuts:
        columns = []
        for h in range(heads):
            head = slice(h * depth, (h + 1) * depth)
            scores = dot_t(unit(query[cut, head]), unit(key[cut, head])) * (scale_ref[h] / math.sqrt(depth))
            scores = jnp.where(seen, scores, NEGATIVE)
            weights = jnp.exp(scores - jnp.max(scores, axis=-1, keepdims=True))
            total = jnp.sum(weights, axis=-1, keepdims=True)
            columns.append((dot(weights.astype(BF16), value[cut, head].astype(BF16)) / total).astype(BF16))
        attended.append(jnp.concatenate(columns, axis=1))
    act = gelu(dot(normed, up_ref[...])).astype(BF16)
    mixed = jnp.concatenate([jnp.concatenate(attended, axis=0), act], axis=1)
    partial = dot(mixed, jnp.concatenate([out_ref[...], down_ref[...]], axis=0)) + xs.astype(F32)
    partial = partial.astype(BF16)
    for i, cut in enumerate(cuts):
        for b in range(span):
            put = (b % own) * patches + i * piece
            part_ref[b // own, put : put + piece] = partial[cut][b * piece : (b + 1) * piece]
    stores = []
    for slot, part in enumerate(parts):
        stores.append(pltpu.make_async_copy(part_ref.at[lax.rem(me + slot, ways)], part, part_sem.at[slot]))
        stores[-1].start()
    if last:
        share = dot(partial, proj_ref[...]).astype(BF16)
        size = share.shape[1]
        for i, cut in enumerate(cuts):
            for b in range(span):
                put = slice((b % own) * size, (b % own + 1) * size)
                share_ref[b // own, i * piece : (i + 1) * piece, put] = share[cut][b * piece : (b + 1) * piece]
        for slot, out in enumerate(others):
            out[...] = share_ref[lax.rem(me + slot, ways)]
    for copy in stores:
        copy.wait()


def local_part(scale, x, gain, weights, span, ways, last):
    rows, width = x.shape[0] // 2, x.shape[1]
    patches = rows // span
    own = span // ways
    piece = math.gcd(patches, 32)
    part = (own * patches, width)
    share = (patches, own * weights[-1].shape[1])
    others = [pltpu.VMEM(share, BF16)] * (ways if last else 0)
    outs = pl.pallas_call(
        functools.partial(local_kernel, span, ways, piece, last),
        in_specs=[SMEM, VMEM, HBM] + [HBM] * len(weights),
        out_specs=[HBM] * ways + [VMEM] * len(others),
        out_shape=[jax.ShapeDtypeStruct(part, BF16)] * ways + others,
        scratch_shapes=[pltpu.VMEM(w.shape, w.dtype) for w in weights]
        + [
            pltpu.VMEM((rows, width), BF16),
            pltpu.VMEM((ways, *part), BF16),
            pltpu.VMEM((ways, *share), BF16),
            pltpu.SemaphoreType.DMA((len(weights),)),
            pltpu.SemaphoreType.DMA((patches // piece,)),
            pltpu.SemaphoreType.DMA((ways,)),
        ],
        compiler_params=pltpu.CompilerParams(vmem_limit_bytes=60 * 2**20),
        cost_estimate=pl.CostEstimate(flops=8 * rows * width * width, bytes_accessed=10 * 2**20, transcendentals=rows * width),
        name="local_part",
    )(scale, gain, x, *weights)
    return list(outs[:ways]), list(outs[ways:])


def state_kernel(count, proj_ref, *refs):
    pieces, (state_ref, share_ref) = refs[:count], refs[count:]
    state = sum(p[...].astype(F32) for p in pieces).astype(BF16)
    state_ref[...] = state
    patches = share_ref.shape[0]
    width = proj_ref.shape[1]
    for b in range(state.shape[0] // patches):
        share_ref[:, b * width : (b + 1) * width] = dot(state[b * patches : (b + 1) * patches], proj_ref[...]).astype(BF16)


def finish_state(proj, pieces, own):
    rows, width = pieces[0].shape
    return pl.pallas_call(
        functools.partial(state_kernel, len(pieces)),
        in_specs=[VMEM] * (1 + len(pieces)),
        out_specs=(VMEM, VMEM),
        out_shape=(
            jax.ShapeDtypeStruct((rows, width), BF16),
            jax.ShapeDtypeStruct((rows // own, own * proj.shape[1]), BF16),
        ),
        compiler_params=pltpu.CompilerParams(vmem_limit_bytes=8 * 2**20),
        name="finish_state",
    )(proj, *pieces)


def fetch_kernel(source, held, sems):
    parts = source.shape[0]
    copies = [pltpu.make_async_copy(source.at[i], held.at[i], sems.at[i]) for i in range(parts)]
    for copy in copies:
        copy.start()
    for copy in copies:
        copy.wait()


def fetch(weight):
    return pl.pallas_call(
        fetch_kernel,
        in_specs=[HBM],
        out_specs=VMEM,
        out_shape=pltpu.VMEM(weight.shape, weight.dtype),
        scratch_shapes=[pltpu.SemaphoreType.DMA((weight.shape[0],))],
        compiler_params=pltpu.CompilerParams(vmem_limit_bytes=50 * 2**20),
        name="fetch",
    )(weight)


def heads_kernel(depth, core_ref, ids_ref, gain_ref, *refs):
    ways = gain_ref.shape[0]
    early, late, weight, outs = refs[:ways], refs[ways : 2 * ways], refs[2 * ways], refs[2 * ways + 1 :]
    width = early[0].shape[1]
    values = [jnp.concatenate([a[...], b[...]], axis=0).astype(F32) for a, b in zip(early, late)]
    square = sum(jnp.sum(v * v, axis=-1, keepdims=True) for v in values)
    factor = lax.rsqrt(square / (ways * width) + EPSILON)
    normed = [(v * factor * gain_ref[ids_ref[c]]).astype(BF16) for c, v in enumerate(values)]
    size = outs[0].shape[1] // 3
    for kind in range(3):
        for i, out in ((1, outs[1]), (0, outs[0])):
            columns = pl.ds(pl.multiple_of((core_ref[0] ^ i) * size, size), size)
            mixed = sum(
                dot(n, weight[kind, pl.ds(pl.multiple_of(ids_ref[c] * width, width), width), columns])
                for c, n in enumerate(normed)
            )
            if kind < 2:
                mixed = jnp.concatenate([unit(mixed[:, c : c + depth]) for c in range(0, size, depth)], axis=1)
            out[:, kind * size : (kind + 1) * size] = mixed.astype(BF16)


def global_heads(depth, core, ids, gain, early, late, qkv):
    shape = jax.ShapeDtypeStruct((2 * early[0].shape[0], 3 * qkv.shape[2] // 2), BF16)
    return pl.pallas_call(
        functools.partial(heads_kernel, depth),
        in_specs=[SMEM, SMEM] + [VMEM] * (2 + len(early) + len(late)),
        out_specs=(VMEM, VMEM),
        out_shape=(shape, shape),
        compiler_params=pltpu.CompilerParams(vmem_limit_bytes=8 * 2**20),
        name="global_heads",
    )(core, ids, gain, *early, *late, qkv)


def attend_kernel(depth, me_ref, ids_ref, scale_ref, kept_ref, given_ref, *refs):
    pieces, (own_ref, other_ref) = refs[:-2], refs[-2:]
    rows = kept_ref.shape[0]
    size = own_ref.shape[1]
    heads = size // depth
    me = me_ref[0]

    def places(index, shape, axis):
        row = lax.broadcasted_iota(jnp.int32, shape, axis)
        return jnp.where(row < rows, index * rows + row, (index ^ 1) * rows + row - rows)

    at = places(me, (2 * rows, 1), 0)
    seen = [places(i, (1, 2 * rows), 1) <= at for i in [me] + [ids_ref[p + 1] for p in range(len(pieces))]]
    own = jnp.concatenate([kept_ref[...], given_ref[...]], axis=0)
    query = own[:, :size]
    pieces = [own[:, size:]] + [p[...] for p in pieces]
    for h in range(heads):
        cut = slice(h * depth, (h + 1) * depth)
        factor = scale_ref[(me % 2) * heads + h] / math.sqrt(depth)
        scores = [jnp.where(s, dot_t(query[:, cut], p[:, cut]) * factor, NEGATIVE) for s, p in zip(seen, pieces)]
        top = functools.reduce(jnp.maximum, [jnp.max(s, axis=-1, keepdims=True) for s in scores])
        weights = [jnp.exp(s - top) for s in scores]
        total = sum(jnp.sum(w, axis=-1, keepdims=True) for w in weights)
        values = slice(size + h * depth, size + (h + 1) * depth)
        summed = sum(dot(w.astype(BF16), p[:, values]) for w, p in zip(weights, pieces))
        attended = (summed / total).astype(BF16)
        own_ref[:, cut] = attended[:rows]
        other_ref[:, cut] = attended[rows:]


def attend(depth, me, ids, scale, kept, given, pieces):
    rows = kept.shape[0]
    shape = jax.ShapeDtypeStruct((rows, kept.shape[1] // 3), BF16)
    return pl.pallas_call(
        functools.partial(attend_kernel, depth),
        in_specs=[SMEM, SMEM, SMEM] + [VMEM] * (2 + len(pieces)),
        out_specs=(VMEM, VMEM),
        out_shape=(shape, shape),
        compiler_params=pltpu.CompilerParams(vmem_limit_bytes=20 * 2**20),
        cost_estimate=BRIEF,
        name="attend",
    )(me, ids, scale, kept, given, *pieces)


def project_kernel(core_ref, slots_ref, own_ref, other_ref, proj_ref, *outs):
    size = own_ref.shape[1]
    own_rows = pl.ds(pl.multiple_of(core_ref[0] * size, size), size)
    other_rows = pl.ds(pl.multiple_of((core_ref[0] ^ 1) * size, size), size)
    for slot, out in enumerate(outs):
        width = out.shape[1]
        columns = pl.ds(pl.multiple_of(slots_ref[slot] * width, width), width)
        out[...] = (dot(own_ref[...], proj_ref[own_rows, columns]) + dot(other_ref[...], proj_ref[other_rows, columns])).astype(BF16)


def project(core, slots, own, other, proj):
    ways = slots.shape[0]
    return pl.pallas_call(
        project_kernel,
        in_specs=[SMEM, SMEM] + [VMEM] * 3,
        out_specs=[VMEM] * ways,
        out_shape=[jax.ShapeDtypeStruct((own.shape[0], proj.shape[1] // ways), BF16)] * ways,
        compiler_params=pltpu.CompilerParams(vmem_limit_bytes=6 * 2**20),
        cost_estimate=BRIEF,
        name="project",
    )(core, slots, own, other, proj)


def result_kernel(count, order_ref, own_ref, *refs):
    pieces, (result_ref, kept_ref, given_ref) = refs[:count], refs[count:]
    total = own_ref[...].astype(F32) + sum(p[...].astype(F32) for p in pieces)
    result = total.astype(BF16)
    result_ref[...] = result
    routed = dot(order_ref[...], result).astype(BF16)
    half = kept_ref.shape[0]
    kept_ref[...] = routed[:half]
    given_ref[...] = routed[half:]


def finish_result(order, residual, pieces):
    rows, width = residual.shape
    shape = jax.ShapeDtypeStruct(residual.shape, BF16)
    half = jax.ShapeDtypeStruct((rows // 2, width), BF16)
    return pl.pallas_call(
        functools.partial(result_kernel, len(pieces)),
        in_specs=[VMEM] * (2 + len(pieces)),
        out_specs=(VMEM, VMEM, VMEM),
        out_shape=(shape, half, half),
        compiler_params=pltpu.CompilerParams(vmem_limit_bytes=4 * 2**20),
        cost_estimate=BRIEF,
        name="finish_result",
    )(order, residual, *pieces)


def sort_kernel(block, devices, rows_ref, out_ref):
    me = lax.axis_index("seq")
    rows = rows_ref.shape[0]
    to = lax.broadcasted_iota(jnp.int32, (rows, rows), 0)
    at = lax.broadcasted_iota(jnp.int32, (rows, rows), 1)
    twin = lax.rem(me - at // (2 * block) * 2 + devices, devices)
    source = twin ^ (at // block % 2)
    order = (to == source * block + at % block).astype(F32).astype(BF16)
    out_ref[...] = dot(order, rows_ref[...]).astype(BF16)


def sort_rows(rows, devices):
    return pl.pallas_call(
        functools.partial(sort_kernel, rows.shape[0] // devices, devices),
        in_specs=[VMEM],
        out_specs=VMEM,
        out_shape=jax.ShapeDtypeStruct(rows.shape, BF16),
        compiler_params=pltpu.CompilerParams(vmem_limit_bytes=4 * 2**20),
        cost_estimate=BRIEF,
        name="sort_rows",
    )(rows)


def bytes_kernel(count, result_ref, proj_ref, *refs):
    sources, (out_ref, held, sems) = refs[:count], refs[count:]
    copies = [pltpu.make_async_copy(p, held.at[i], sems.at[i]) for i, p in enumerate(sources)]
    for copy in copies:
        copy.start()
    rows = result_ref.shape[0]
    half = rows // 2
    width = proj_ref.shape[0]
    own = out_ref.shape[0] // rows
    back = [dot(result_ref[:, b * width : (b + 1) * width], proj_ref[...]) for b in range(own)]
    back = jnp.concatenate([b[:half] for b in back] + [b[half:] for b in back], axis=0)
    at = lax.broadcasted_iota(jnp.int32, (rows * own, rows * own), 0)
    to = lax.broadcasted_iota(jnp.int32, (rows * own, rows * own), 1)
    patch = at // own
    order = (to == patch // half * half * own + at % own * half + patch % half).astype(F32).astype(BF16)
    for copy in copies:
        copy.wait()
    late = sum(held[i].astype(F32) for i in range(1, count)).astype(BF16)
    state = jnp.concatenate([held[0], late], axis=0).astype(F32)
    out_ref[...] = dot(order, (state + back).astype(BF16)).astype(BF16)


def finish_bytes(result, proj, pieces):
    rows, width = pieces[0].shape
    return pl.pallas_call(
        functools.partial(bytes_kernel, len(pieces)),
        in_specs=[VMEM, VMEM] + [pl.BlockSpec(memory_space=pl.ANY)] * len(pieces),
        out_specs=VMEM,
        out_shape=jax.ShapeDtypeStruct((2 * rows, width), BF16),
        scratch_shapes=[pltpu.VMEM((len(pieces), rows, width), BF16), pltpu.SemaphoreType.DMA((len(pieces),))],
        compiler_params=pltpu.CompilerParams(vmem_limit_bytes=16 * 2**20),
        cost_estimate=BRIEF,
        name="finish_bytes",
    )(result, proj, *pieces)


def shift(value, axis, step):
    count = lax.axis_size(axis)
    return lax.ppermute(value, axis, [(i, (i + step) % count) for i in range(count)])


def scatter(chunks, axis):
    return [chunks[0]] + [shift(chunk, axis, step) for step, chunk in enumerate(chunks[1:], 1)]


def shift_slots(axis):
    count = lax.axis_size(axis)
    return ((lax.axis_index(axis) + jnp.arange(count)) % count).astype(jnp.int32)


def gather(value, axis):
    return [value] + [shift(value, axis, step) for step in range(1, lax.axis_size(axis))]


def swap_cores(value, axis):
    return lax.ppermute(value, axis, [(i, i ^ 1) for i in range(lax.axis_size(axis))])


def twin_ids(axis):
    count = lax.axis_size(axis)
    return ((lax.axis_index(axis) - 2 * jnp.arange(count // 2)) % count).astype(jnp.int32)


def owner_order(owners, source, patches):
    devices, count = owners.shape
    listed = lax.dynamic_index_in_dim(owners, source, 0, keepdims=False)
    block = patches // count
    index = jnp.arange(count, dtype=jnp.int32)
    rank = jnp.sum((listed[None, :] == listed[:, None]) & (index[None, :] < index[:, None]), axis=1).astype(jnp.int32)
    chips = devices // 2
    order = (listed % 2 ^ source % 2) * chips + (listed // 2 - source // 2 + chips) % chips
    slot = order * (count // devices) + rank
    row = jnp.arange(patches, dtype=jnp.int32)
    spread = jnp.sum(jnp.where(row[:, None] // block == index[None, :], slot[None, :], 0), axis=1).astype(jnp.int32)
    place = spread * block + row % block
    return (row[:, None] == place[None, :]).astype(BF16)


def route(kept, given, axis):
    devices = lax.axis_size(axis)
    chips = devices // 2
    width = kept.shape[1]
    received = swap_cores(given, axis)
    bundles = jnp.concatenate([a.reshape(chips, -1, width) for a in (kept, received)], axis=1)
    arrived = [bundles[0]] + [shift(bundles[step], axis, 2 * step) for step in range(1, chips)]
    return sort_rows(jnp.concatenate(arrived, axis=0), devices)


def on_device(
    byte_in,
    local_gain,
    local_qkv,
    local_out,
    mlp_up,
    mlp_down,
    local_scale,
    patch_proj,
    global_gain,
    global_qkv,
    global_out,
    global_scale,
    back_proj,
    owners,
):
    patches, span, width = byte_in.shape
    ways = lax.axis_size("head")
    own = span // ways
    me = lax.axis_index("head").astype(jnp.int32)
    seq = lax.axis_index("seq").astype(jnp.int32)
    depth = global_qkv.shape[2] // global_scale.shape[0]

    slots = shift_slots("head")
    rows = byte_in.reshape(-1, width)
    weights = [jnp.transpose(local_qkv, (1, 0, 2)), mlp_up, local_out, mlp_down, patch_proj]
    gain = local_gain.reshape(1, -1)
    early, _ = local_part(local_scale, rows, gain, weights, span, ways, False)
    early = scatter(early, "head")
    parts, chunks = local_part(local_scale, rows, gain, weights, span, ways, True)
    chunks, early[1] = lax.optimization_barrier((chunks, early[1]))
    chunks = scatter(chunks, "head")
    early, early_share = finish_state(patch_proj, early, own)
    early_shares = gather(early_share, "head")
    late_share = sum(p.astype(F32) for p in chunks).astype(BF16)
    weight = jnp.transpose(global_qkv, (1, 0, 2))
    weight, late_share = lax.optimization_barrier((weight, late_share))
    late_shares = gather(late_share, "head")
    early_shares, late_shares, weight, parts[1] = lax.optimization_barrier(
        (early_shares, late_shares, fetch(weight), parts[1])
    )
    parts[1] = shift(parts[1], "head", 1)
    residual = jnp.concatenate([early_share, late_share], axis=0)
    ids = (me - jnp.arange(ways, dtype=jnp.int32)) % ways
    core = (seq % 2).reshape(1)
    kept, given = global_heads(depth, core, ids, global_gain.reshape(ways, 1, -1), early_shares, late_shares, weight)
    received = swap_cores(given, "seq")
    received, *parts = lax.optimization_barrier((received, *parts))
    half = kept.shape[1] // 3
    keyed = jnp.concatenate([kept[:, half:], received[:, half:]], axis=0)
    pieces = [shift(keyed, "seq", 2 * step) for step in range(1, lax.axis_size("seq") // 2)]
    parts[2:] = [shift(part, "head", step) for step, part in enumerate(parts[2:], 2)]
    own_heads, other_heads = attend(depth, seq.reshape(1), twin_ids("seq"), global_scale, kept, received, pieces)
    other_heads, parts[2:] = lax.optimization_barrier((swap_cores(other_heads, "seq"), parts[2:]))
    updates = scatter(project(core, slots, own_heads, other_heads, global_out), "head")
    result, kept, given = finish_result(owner_order(owners, seq, patches), residual, updates)
    global_state = route(kept, given, "seq")
    byte_out = finish_bytes(result, back_proj, [early] + parts)
    return byte_out.reshape(patches, own, width), global_state


def solution(mesh):
    placed = (
        P("seq", None, None),
        P(),
        P(None, None, "head"),
        P("head", None),
        P(None, "head"),
        P("head", None),
        P("head"),
        P(),
        P(),
        P(None, None, "head"),
        P("head", None),
        P("head"),
        P(),
        P(),
    )
    return jax.shard_map(
        on_device,
        mesh=mesh,
        in_specs=placed,
        out_specs=(P("seq", "head", None), P("seq", "head")),
        check_vma=False,
    )
```

```python
import functools
import math

import jax
import jax.numpy as jnp
from jax import lax
from jax.experimental import pallas as pl
from jax.experimental.pallas import tpu as pltpu
from jax.sharding import PartitionSpec as P

EPSILON = 1e-06
NEGATIVE = -1e30
F32 = jnp.float32
BF16 = jnp.bfloat16
BRIEF = pl.CostEstimate(flops=1, bytes_accessed=1, transcendentals=0)
VMEM = pl.BlockSpec(memory_space=pltpu.VMEM)
HBM = pl.BlockSpec(memory_space=pltpu.HBM)
SMEM = pl.BlockSpec(memory_space=pltpu.SMEM)


def dot(left, right):
    return jnp.dot(left, right, preferred_element_type=F32)


def dot_t(left, right):
    return lax.dot_general(left, right, (((1,), (1,)), ((), ())), preferred_element_type=F32)


def unit(values):
    return (values * lax.rsqrt(jnp.mean(values * values, axis=-1, keepdims=True) + EPSILON)).astype(BF16)


def gelu(values):
    inner = math.sqrt(2.0 / math.pi) * (values + 0.044715 * (values * values * values))
    return 0.5 * values * (1.0 + jnp.tanh(inner))


def local_kernel(span, ways, piece, last, scale_ref, gain_ref, x_hbm, *refs):
    sources, parts, others = refs[:5], refs[5 : 5 + ways], refs[5 + ways : -11]
    held, (x_ref, part_ref, share_ref, in_sem, x_sem, part_sem) = refs[-11:-6], refs[-6:]
    patches = share_ref.shape[1]
    own = span // ways
    rows = piece * span
    pieces = patches // piece
    cuts = [slice(i * rows, (i + 1) * rows) for i in range(pieces)]
    skip = x_ref.shape[0] if last else 0
    loads = [
        pltpu.make_async_copy(x_hbm.at[pl.ds(skip + c.start, rows)], x_ref.at[pl.ds(c.start, rows)], x_sem.at[i])
        for i, c in enumerate(cuts)
    ]
    loads += [pltpu.make_async_copy(s, h, in_sem.at[i]) for i, (s, h) in enumerate(zip(sources, held))]
    for copy in loads:
        copy.start()
    me = lax.axis_index("head")
    at = lax.broadcasted_iota(jnp.int32, (rows, rows), 0)
    to = lax.broadcasted_iota(jnp.int32, (rows, rows), 1)
    order = (to == (at % piece) * span + at // piece).astype(F32).astype(BF16)
    kept = lax.broadcasted_iota(jnp.int32, (rows, 1), 0) // piece // own == me
    for copy in loads:
        copy.wait()
    qkv_ref, up_ref, out_ref, down_ref, proj_ref = held
    xs, normed = [], []
    for cut in cuts:
        x = dot(order, x_ref[cut])
        xs.append(jnp.where(kept, x, 0.0).astype(BF16))
        factor = lax.rsqrt(jnp.mean(x * x, axis=-1, keepdims=True) + EPSILON)
        normed.append((x * factor * gain_ref[...]).astype(BF16))
    xs, normed = jnp.concatenate(xs, axis=0), jnp.concatenate(normed, axis=0)
    query, key, value = (dot(normed, qkv_ref[i]) for i in range(3))
    seen = (at % piece == to % piece) & (to <= at)
    heads = scale_ref.shape[0]
    depth = query.shape[1] // heads
    attended = []
    for cut in cuts:
        columns = []
        for h in range(heads):
            head = slice(h * depth, (h + 1) * depth)
            scores = dot_t(unit(query[cut, head]), unit(key[cut, head])) * (scale_ref[h] / math.sqrt(depth))
            scores = jnp.where(seen, scores, NEGATIVE)
            weights = jnp.exp(scores - jnp.max(scores, axis=-1, keepdims=True))
            total = jnp.sum(weights, axis=-1, keepdims=True)
            columns.append((dot(weights.astype(BF16), value[cut, head].astype(BF16)) / total).astype(BF16))
        attended.append(jnp.concatenate(columns, axis=1))
    act = gelu(dot(normed, up_ref[...])).astype(BF16)
    mixed = jnp.concatenate([jnp.concatenate(attended, axis=0), act], axis=1)
    partial = dot(mixed, jnp.concatenate([out_ref[...], down_ref[...]], axis=0)) + xs.astype(F32)
    partial = partial.astype(BF16)
    for i, cut in enumerate(cuts):
        for b in range(span):
            put = (b % own) * patches + i * piece
            part_ref[b // own, put : put + piece] = partial[cut][b * piece : (b + 1) * piece]
    stores = []
    for slot, part in enumerate(parts):
        stores.append(pltpu.make_async_copy(part_ref.at[lax.rem(me + slot, ways)], part, part_sem.at[slot]))
        stores[-1].start()
    if last:
        share = dot(partial, proj_ref[...]).astype(BF16)
        size = share.shape[1]
        for i, cut in enumerate(cuts):
            for b in range(span):
                put = slice((b % own) * size, (b % own + 1) * size)
                share_ref[b // own, i * piece : (i + 1) * piece, put] = share[cut][b * piece : (b + 1) * piece]
        for slot, out in enumerate(others):
            out[...] = share_ref[lax.rem(me + slot, ways)]
    for copy in stores:
        copy.wait()


def local_part(scale, x, gain, weights, span, ways, last):
    rows, width = x.shape[0] // 2, x.shape[1]
    patches = rows // span
    own = span // ways
    piece = math.gcd(patches, 32)
    part = (own * patches, width)
    share = (patches, own * weights[-1].shape[1])
    others = [pltpu.VMEM(share, BF16)] * (ways if last else 0)
    outs = pl.pallas_call(
        functools.partial(local_kernel, span, ways, piece, last),
        in_specs=[SMEM, VMEM, HBM] + [HBM] * len(weights),
        out_specs=[HBM] * ways + [VMEM] * len(others),
        out_shape=[jax.ShapeDtypeStruct(part, BF16)] * ways + others,
        scratch_shapes=[pltpu.VMEM(w.shape, w.dtype) for w in weights]
        + [
            pltpu.VMEM((rows, width), BF16),
            pltpu.VMEM((ways, *part), BF16),
            pltpu.VMEM((ways, *share), BF16),
            pltpu.SemaphoreType.DMA((len(weights),)),
            pltpu.SemaphoreType.DMA((patches // piece,)),
            pltpu.SemaphoreType.DMA((ways,)),
        ],
        compiler_params=pltpu.CompilerParams(vmem_limit_bytes=60 * 2**20),
        cost_estimate=pl.CostEstimate(flops=8 * rows * width * width, bytes_accessed=10 * 2**20, transcendentals=rows * width),
        name="local_part",
    )(scale, gain, x, *weights)
    return list(outs[:ways]), list(outs[ways:])


def state_kernel(count, proj_ref, *refs):
    pieces, (state_ref, share_ref) = refs[:count], refs[count:]
    state = sum(p[...].astype(F32) for p in pieces).astype(BF16)
    state_ref[...] = state
    patches = share_ref.shape[0]
    width = proj_ref.shape[1]
    for b in range(state.shape[0] // patches):
        share_ref[:, b * width : (b + 1) * width] = dot(state[b * patches : (b + 1) * patches], proj_ref[...]).astype(BF16)


def finish_state(proj, pieces, own):
    rows, width = pieces[0].shape
    return pl.pallas_call(
        functools.partial(state_kernel, len(pieces)),
        in_specs=[VMEM] * (1 + len(pieces)),
        out_specs=(VMEM, VMEM),
        out_shape=(
            jax.ShapeDtypeStruct((rows, width), BF16),
            jax.ShapeDtypeStruct((rows // own, own * proj.shape[1]), BF16),
        ),
        compiler_params=pltpu.CompilerParams(vmem_limit_bytes=8 * 2**20),
        name="finish_state",
    )(proj, *pieces)


def fetch_kernel(source, held, sems):
    parts = source.shape[0]
    copies = [pltpu.make_async_copy(source.at[i], held.at[i], sems.at[i]) for i in range(parts)]
    for copy in copies:
        copy.start()
    for copy in copies:
        copy.wait()


def fetch(weight):
    return pl.pallas_call(
        fetch_kernel,
        in_specs=[HBM],
        out_specs=VMEM,
        out_shape=pltpu.VMEM(weight.shape, weight.dtype),
        scratch_shapes=[pltpu.SemaphoreType.DMA((weight.shape[0],))],
        compiler_params=pltpu.CompilerParams(vmem_limit_bytes=50 * 2**20),
        name="fetch",
    )(weight)


def heads_kernel(depth, core_ref, ids_ref, gain_ref, *refs):
    ways = gain_ref.shape[0]
    early, late, weight, outs = refs[:ways], refs[ways : 2 * ways], refs[2 * ways], refs[2 * ways + 1 :]
    width = early[0].shape[1]
    values = [jnp.concatenate([a[...], b[...]], axis=0).astype(F32) for a, b in zip(early, late)]
    square = sum(jnp.sum(v * v, axis=-1, keepdims=True) for v in values)
    factor = lax.rsqrt(square / (ways * width) + EPSILON)
    normed = [(v * factor * gain_ref[ids_ref[c]]).astype(BF16) for c, v in enumerate(values)]
    size = outs[0].shape[1] // 3
    for kind in range(3):
        for i, out in ((1, outs[1]), (0, outs[0])):
            columns = pl.ds(pl.multiple_of((core_ref[0] ^ i) * size, size), size)
            mixed = sum(
                dot(n, weight[kind, pl.ds(pl.multiple_of(ids_ref[c] * width, width), width), columns])
                for c, n in enumerate(normed)
            )
            if kind < 2:
                mixed = jnp.concatenate([unit(mixed[:, c : c + depth]) for c in range(0, size, depth)], axis=1)
            out[:, kind * size : (kind + 1) * size] = mixed.astype(BF16)


def global_heads(depth, core, ids, gain, early, late, qkv):
    shape = jax.ShapeDtypeStruct((2 * early[0].shape[0], 3 * qkv.shape[2] // 2), BF16)
    return pl.pallas_call(
        functools.partial(heads_kernel, depth),
        in_specs=[SMEM, SMEM] + [VMEM] * (2 + len(early) + len(late)),
        out_specs=(VMEM, VMEM),
        out_shape=(shape, shape),
        compiler_params=pltpu.CompilerParams(vmem_limit_bytes=8 * 2**20),
        name="global_heads",
    )(core, ids, gain, *early, *late, qkv)


def attend_kernel(depth, me_ref, ids_ref, scale_ref, kept_ref, given_ref, *refs):
    pieces, (own_ref, other_ref) = refs[:-2], refs[-2:]
    rows = kept_ref.shape[0]
    size = own_ref.shape[1]
    heads = size // depth
    me = me_ref[0]

    def places(index, shape, axis):
        row = lax.broadcasted_iota(jnp.int32, shape, axis)
        return jnp.where(row < rows, index * rows + row, (index ^ 1) * rows + row - rows)

    at = places(me, (2 * rows, 1), 0)
    seen = [places(i, (1, 2 * rows), 1) <= at for i in [me] + [ids_ref[p + 1] for p in range(len(pieces))]]
    own = jnp.concatenate([kept_ref[...], given_ref[...]], axis=0)
    query = own[:, :size]
    pieces = [own[:, size:]] + [p[...] for p in pieces]
    for h in range(heads):
        cut = slice(h * depth, (h + 1) * depth)
        factor = scale_ref[(me % 2) * heads + h] / math.sqrt(depth)
        scores = [jnp.where(s, dot_t(query[:, cut], p[:, cut]) * factor, NEGATIVE) for s, p in zip(seen, pieces)]
        top = functools.reduce(jnp.maximum, [jnp.max(s, axis=-1, keepdims=True) for s in scores])
        weights = [jnp.exp(s - top) for s in scores]
        total = sum(jnp.sum(w, axis=-1, keepdims=True) for w in weights)
        values = slice(size + h * depth, size + (h + 1) * depth)
        summed = sum(dot(w.astype(BF16), p[:, values]) for w, p in zip(weights, pieces))
        attended = (summed / total).astype(BF16)
        own_ref[:, cut] = attended[:rows]
        other_ref[:, cut] = attended[rows:]


def attend(depth, me, ids, scale, kept, given, pieces):
    rows = kept.shape[0]
    shape = jax.ShapeDtypeStruct((rows, kept.shape[1] // 3), BF16)
    return pl.pallas_call(
        functools.partial(attend_kernel, depth),
        in_specs=[SMEM, SMEM, SMEM] + [VMEM] * (2 + len(pieces)),
        out_specs=(VMEM, VMEM),
        out_shape=(shape, shape),
        compiler_params=pltpu.CompilerParams(vmem_limit_bytes=20 * 2**20),
        cost_estimate=BRIEF,
        name="attend",
    )(me, ids, scale, kept, given, *pieces)


def project_kernel(core_ref, slots_ref, own_ref, other_ref, proj_ref, *outs):
    size = own_ref.shape[1]
    own_rows = pl.ds(pl.multiple_of(core_ref[0] * size, size), size)
    other_rows = pl.ds(pl.multiple_of((core_ref[0] ^ 1) * size, size), size)
    for slot, out in enumerate(outs):
        width = out.shape[1]
        columns = pl.ds(pl.multiple_of(slots_ref[slot] * width, width), width)
        out[...] = (dot(own_ref[...], proj_ref[own_rows, columns]) + dot(other_ref[...], proj_ref[other_rows, columns])).astype(BF16)


def project(core, slots, own, other, proj):
    ways = slots.shape[0]
    return pl.pallas_call(
        project_kernel,
        in_specs=[SMEM, SMEM] + [VMEM] * 3,
        out_specs=[VMEM] * ways,
        out_shape=[jax.ShapeDtypeStruct((own.shape[0], proj.shape[1] // ways), BF16)] * ways,
        compiler_params=pltpu.CompilerParams(vmem_limit_bytes=6 * 2**20),
        cost_estimate=BRIEF,
        name="project",
    )(core, slots, own, other, proj)


def result_kernel(count, order_ref, own_ref, *refs):
    pieces, (result_ref, kept_ref, given_ref) = refs[:count], refs[count:]
    total = own_ref[...].astype(F32) + sum(p[...].astype(F32) for p in pieces)
    result = total.astype(BF16)
    result_ref[...] = result
    routed = dot(order_ref[...], result).astype(BF16)
    half = kept_ref.shape[0]
    kept_ref[...] = routed[:half]
    given_ref[...] = routed[half:]


def finish_result(order, residual, pieces):
    rows, width = residual.shape
    shape = jax.ShapeDtypeStruct(residual.shape, BF16)
    half = jax.ShapeDtypeStruct((rows // 2, width), BF16)
    return pl.pallas_call(
        functools.partial(result_kernel, len(pieces)),
        in_specs=[VMEM] * (2 + len(pieces)),
        out_specs=(VMEM, VMEM, VMEM),
        out_shape=(shape, half, half),
        compiler_params=pltpu.CompilerParams(vmem_limit_bytes=4 * 2**20),
        cost_estimate=BRIEF,
        name="finish_result",
    )(order, residual, *pieces)


def sort_kernel(block, devices, rows_ref, out_ref):
    me = lax.axis_index("seq")
    rows = rows_ref.shape[0]
    to = lax.broadcasted_iota(jnp.int32, (rows, rows), 0)
    at = lax.broadcasted_iota(jnp.int32, (rows, rows), 1)
    twin = lax.rem(me - at // (2 * block) * 2 + devices, devices)
    source = twin ^ (at // block % 2)
    order = (to == source * block + at % block).astype(F32).astype(BF16)
    out_ref[...] = dot(order, rows_ref[...]).astype(BF16)


def sort_rows(rows, devices):
    return pl.pallas_call(
        functools.partial(sort_kernel, rows.shape[0] // devices, devices),
        in_specs=[VMEM],
        out_specs=VMEM,
        out_shape=jax.ShapeDtypeStruct(rows.shape, BF16),
        compiler_params=pltpu.CompilerParams(vmem_limit_bytes=4 * 2**20),
        cost_estimate=BRIEF,
        name="sort_rows",
    )(rows)


def bytes_kernel(count, result_ref, proj_ref, *refs):
    sources, (out_ref, held, sems) = refs[:count], refs[count:]
    copies = [pltpu.make_async_copy(p, held.at[i], sems.at[i]) for i, p in enumerate(sources)]
    for copy in copies:
        copy.start()
    rows = result_ref.shape[0]
    half = rows // 2
    width = proj_ref.shape[0]
    own = out_ref.shape[0] // rows
    back = [dot(result_ref[:, b * width : (b + 1) * width], proj_ref[...]) for b in range(own)]
    back = jnp.concatenate([b[:half] for b in back] + [b[half:] for b in back], axis=0)
    at = lax.broadcasted_iota(jnp.int32, (rows * own, rows * own), 0)
    to = lax.broadcasted_iota(jnp.int32, (rows * own, rows * own), 1)
    patch = at // own
    order = (to == patch // half * half * own + at % own * half + patch % half).astype(F32).astype(BF16)
    for copy in copies:
        copy.wait()
    late = sum(held[i].astype(F32) for i in range(1, count)).astype(BF16)
    state = jnp.concatenate([held[0], late], axis=0).astype(F32)
    out_ref[...] = dot(order, (state + back).astype(BF16)).astype(BF16)


def finish_bytes(result, proj, pieces):
    rows, width = pieces[0].shape
    return pl.pallas_call(
        functools.partial(bytes_kernel, len(pieces)),
        in_specs=[VMEM, VMEM] + [pl.BlockSpec(memory_space=pl.ANY)] * len(pieces),
        out_specs=VMEM,
        out_shape=jax.ShapeDtypeStruct((2 * rows, width), BF16),
        scratch_shapes=[pltpu.VMEM((len(pieces), rows, width), BF16), pltpu.SemaphoreType.DMA((len(pieces),))],
        compiler_params=pltpu.CompilerParams(vmem_limit_bytes=16 * 2**20),
        cost_estimate=BRIEF,
        name="finish_bytes",
    )(result, proj, *pieces)


def shift(value, axis, step):
    count = lax.axis_size(axis)
    return lax.ppermute(value, axis, [(i, (i + step) % count) for i in range(count)])


def scatter(chunks, axis):
    return [chunks[0]] + [shift(chunk, axis, step) for step, chunk in enumerate(chunks[1:], 1)]


def shift_slots(axis):
    count = lax.axis_size(axis)
    return ((lax.axis_index(axis) + jnp.arange(count)) % count).astype(jnp.int32)


def gather(value, axis):
    return [value] + [shift(value, axis, step) for step in range(1, lax.axis_size(axis))]


def swap_cores(value, axis):
    return lax.ppermute(value, axis, [(i, i ^ 1) for i in range(lax.axis_size(axis))])


def twin_ids(axis):
    count = lax.axis_size(axis)
    return ((lax.axis_index(axis) - 2 * jnp.arange(count // 2)) % count).astype(jnp.int32)


def owner_order(owners, source, patches):
    devices, count = owners.shape
    listed = lax.dynamic_index_in_dim(owners, source, 0, keepdims=False)
    block = patches // count
    index = jnp.arange(count, dtype=jnp.int32)
    rank = jnp.sum((listed[None, :] == listed[:, None]) & (index[None, :] < index[:, None]), axis=1).astype(jnp.int32)
    chips = devices // 2
    order = (listed % 2 ^ source % 2) * chips + (listed // 2 - source // 2 + chips) % chips
    slot = order * (count // devices) + rank
    row = jnp.arange(patches, dtype=jnp.int32)
    spread = jnp.sum(jnp.where(row[:, None] // block == index[None, :], slot[None, :], 0), axis=1).astype(jnp.int32)
    place = spread * block + row % block
    return (row[:, None] == place[None, :]).astype(BF16)


def route(kept, given, axis):
    devices = lax.axis_size(axis)
    chips = devices // 2
    width = kept.shape[1]
    received = swap_cores(given, axis)
    bundles = jnp.concatenate([a.reshape(chips, -1, width) for a in (kept, received)], axis=1)
    arrived = [bundles[0]] + [shift(bundles[step], axis, 2 * step) for step in range(1, chips)]
    return sort_rows(jnp.concatenate(arrived, axis=0), devices)


def on_device(
    byte_in,
    local_gain,
    local_qkv,
    local_out,
    mlp_up,
    mlp_down,
    local_scale,
    patch_proj,
    global_gain,
    global_qkv,
    global_out,
    global_scale,
    back_proj,
    owners,
):
    patches, span, width = byte_in.shape
    ways = lax.axis_size("head")
    own = span // ways
    me = lax.axis_index("head").astype(jnp.int32)
    seq = lax.axis_index("seq").astype(jnp.int32)
    depth = global_qkv.shape[2] // global_scale.shape[0]

    slots = shift_slots("head")
    rows = byte_in.reshape(-1, width)
    weights = [jnp.transpose(local_qkv, (1, 0, 2)), mlp_up, local_out, mlp_down, patch_proj]
    gain = local_gain.reshape(1, -1)
    early, _ = local_part(local_scale, rows, gain, weights, span, ways, False)
    early = scatter(early, "head")
    parts, chunks = local_part(local_scale, rows, gain, weights, span, ways, True)
    chunks, early[1] = lax.optimization_barrier((chunks, early[1]))
    chunks = scatter(chunks, "head")
    early, early_share = finish_state(patch_proj, early, own)
    early_shares = gather(early_share, "head")
    late_share = sum(p.astype(F32) for p in chunks).astype(BF16)
    weight = jnp.transpose(global_qkv, (1, 0, 2))
    weight, late_share = lax.optimization_barrier((weight, late_share))
    late_shares = gather(late_share, "head")
    early_shares, late_shares, weight, parts[1] = lax.optimization_barrier(
        (early_shares, late_shares, fetch(weight), parts[1])
    )
    parts[1] = shift(parts[1], "head", 1)
    residual = jnp.concatenate([early_share, late_share], axis=0)
    ids = (me - jnp.arange(ways, dtype=jnp.int32)) % ways
    core = (seq % 2).reshape(1)
    kept, given = global_heads(depth, core, ids, global_gain.reshape(ways, 1, -1), early_shares, late_shares, weight)
    received = swap_cores(given, "seq")
    received, parts[2:] = lax.optimization_barrier((received, parts[2:]))
    half = kept.shape[1] // 3
    keyed = jnp.concatenate([kept[:, half:], received[:, half:]], axis=0)
    pieces = [shift(keyed, "seq", 2 * step) for step in range(1, lax.axis_size("seq") // 2)]
    parts[2:] = [shift(part, "head", step) for step, part in enumerate(parts[2:], 2)]
    kept, parts[1] = lax.optimization_barrier((kept, parts[1]))
    own_heads, other_heads = attend(depth, seq.reshape(1), twin_ids("seq"), global_scale, kept, received, pieces)
    other_heads, parts[2:] = lax.optimization_barrier((swap_cores(other_heads, "seq"), parts[2:]))
    updates = scatter(project(core, slots, own_heads, other_heads, global_out), "head")
    result, kept, given = finish_result(owner_order(owners, seq, patches), residual, updates)
    global_state = route(kept, given, "seq")
    byte_out = finish_bytes(result, back_proj, [early] + parts)
    return byte_out.reshape(patches, own, width), global_state


def solution(mesh):
    placed = (
        P("seq", None, None),
        P(),
        P(None, None, "head"),
        P("head", None),
        P(None, "head"),
        P("head", None),
        P("head"),
        P(),
        P(),
        P(None, None, "head"),
        P("head", None),
        P("head"),
        P(),
        P(),
    )
    return jax.shard_map(
        on_device,
        mesh=mesh,
        in_specs=placed,
        out_specs=(P("seq", "head", None), P("seq", "head")),
        check_vma=False,
    )
```

```python
import functools
import math

import jax
import jax.numpy as jnp
from jax import lax
from jax.experimental import pallas as pl
from jax.experimental.pallas import tpu as pltpu
from jax.sharding import PartitionSpec as P

EPSILON = 1e-06
NEGATIVE = -1e30
F32 = jnp.float32
BF16 = jnp.bfloat16
BRIEF = pl.CostEstimate(flops=1, bytes_accessed=1, transcendentals=0)
VMEM = pl.BlockSpec(memory_space=pltpu.VMEM)
HBM = pl.BlockSpec(memory_space=pltpu.HBM)
SMEM = pl.BlockSpec(memory_space=pltpu.SMEM)


def dot(left, right):
    return jnp.dot(left, right, preferred_element_type=F32)


def dot_t(left, right):
    return lax.dot_general(left, right, (((1,), (1,)), ((), ())), preferred_element_type=F32)


def unit(values):
    return (values * lax.rsqrt(jnp.mean(values * values, axis=-1, keepdims=True) + EPSILON)).astype(BF16)


def gelu(values):
    inner = math.sqrt(2.0 / math.pi) * (values + 0.044715 * (values * values * values))
    return 0.5 * values * (1.0 + jnp.tanh(inner))


def local_kernel(span, ways, piece, last, scale_ref, gain_ref, x_hbm, *refs):
    sources, parts, others = refs[:5], refs[5 : 5 + ways], refs[5 + ways : -11]
    held, (x_ref, part_ref, share_ref, in_sem, x_sem, part_sem) = refs[-11:-6], refs[-6:]
    patches = share_ref.shape[1]
    own = span // ways
    rows = piece * span
    pieces = patches // piece
    cuts = [slice(i * rows, (i + 1) * rows) for i in range(pieces)]
    skip = x_ref.shape[0] if last else 0
    loads = [
        pltpu.make_async_copy(x_hbm.at[pl.ds(skip + c.start, rows)], x_ref.at[pl.ds(c.start, rows)], x_sem.at[i])
        for i, c in enumerate(cuts)
    ]
    loads += [pltpu.make_async_copy(s, h, in_sem.at[i]) for i, (s, h) in enumerate(zip(sources, held))]
    for copy in loads:
        copy.start()
    me = lax.axis_index("head")
    at = lax.broadcasted_iota(jnp.int32, (rows, rows), 0)
    to = lax.broadcasted_iota(jnp.int32, (rows, rows), 1)
    order = (to == (at % piece) * span + at // piece).astype(F32).astype(BF16)
    kept = lax.broadcasted_iota(jnp.int32, (rows, 1), 0) // piece // own == me
    for copy in loads:
        copy.wait()
    qkv_ref, up_ref, out_ref, down_ref, proj_ref = held
    xs, normed = [], []
    for cut in cuts:
        x = dot(order, x_ref[cut])
        xs.append(jnp.where(kept, x, 0.0).astype(BF16))
        factor = lax.rsqrt(jnp.mean(x * x, axis=-1, keepdims=True) + EPSILON)
        normed.append((x * factor * gain_ref[...]).astype(BF16))
    xs, normed = jnp.concatenate(xs, axis=0), jnp.concatenate(normed, axis=0)
    query, key, value = (dot(normed, qkv_ref[i]) for i in range(3))
    seen = (at % piece == to % piece) & (to <= at)
    heads = scale_ref.shape[0]
    depth = query.shape[1] // heads
    attended = []
    for cut in cuts:
        columns = []
        for h in range(heads):
            head = slice(h * depth, (h + 1) * depth)
            scores = dot_t(unit(query[cut, head]), unit(key[cut, head])) * (scale_ref[h] / math.sqrt(depth))
            scores = jnp.where(seen, scores, NEGATIVE)
            weights = jnp.exp(scores - jnp.max(scores, axis=-1, keepdims=True))
            total = jnp.sum(weights, axis=-1, keepdims=True)
            columns.append((dot(weights.astype(BF16), value[cut, head].astype(BF16)) / total).astype(BF16))
        attended.append(jnp.concatenate(columns, axis=1))
    act = gelu(dot(normed, up_ref[...])).astype(BF16)
    mixed = jnp.concatenate([jnp.concatenate(attended, axis=0), act], axis=1)
    partial = dot(mixed, jnp.concatenate([out_ref[...], down_ref[...]], axis=0)) + xs.astype(F32)
    partial = partial.astype(BF16)
    for i, cut in enumerate(cuts):
        for b in range(span):
            put = (b % own) * patches + i * piece
            part_ref[b // own, put : put + piece] = partial[cut][b * piece : (b + 1) * piece]
    stores = []
    for slot, part in enumerate(parts):
        stores.append(pltpu.make_async_copy(part_ref.at[lax.rem(me + slot, ways)], part, part_sem.at[slot]))
        stores[-1].start()
    if last:
        share = dot(partial, proj_ref[...]).astype(BF16)
        size = share.shape[1]
        for i, cut in enumerate(cuts):
            for b in range(span):
                put = slice((b % own) * size, (b % own + 1) * size)
                share_ref[b // own, i * piece : (i + 1) * piece, put] = share[cut][b * piece : (b + 1) * piece]
        for slot, out in enumerate(others):
            out[...] = share_ref[lax.rem(me + slot, ways)]
    for copy in stores:
        copy.wait()


def local_part(scale, x, gain, weights, span, ways, last):
    rows, width = x.shape[0] // 2, x.shape[1]
    patches = rows // span
    own = span // ways
    piece = math.gcd(patches, 32)
    part = (own * patches, width)
    share = (patches, own * weights[-1].shape[1])
    others = [pltpu.VMEM(share, BF16)] * (ways if last else 0)
    outs = pl.pallas_call(
        functools.partial(local_kernel, span, ways, piece, last),
        in_specs=[SMEM, VMEM, HBM] + [HBM] * len(weights),
        out_specs=[HBM] * ways + [VMEM] * len(others),
        out_shape=[jax.ShapeDtypeStruct(part, BF16)] * ways + others,
        scratch_shapes=[pltpu.VMEM(w.shape, w.dtype) for w in weights]
        + [
            pltpu.VMEM((rows, width), BF16),
            pltpu.VMEM((ways, *part), BF16),
            pltpu.VMEM((ways, *share), BF16),
            pltpu.SemaphoreType.DMA((len(weights),)),
            pltpu.SemaphoreType.DMA((patches // piece,)),
            pltpu.SemaphoreType.DMA((ways,)),
        ],
        compiler_params=pltpu.CompilerParams(vmem_limit_bytes=60 * 2**20),
        cost_estimate=pl.CostEstimate(flops=8 * rows * width * width, bytes_accessed=10 * 2**20, transcendentals=rows * width),
        name="local_part",
    )(scale, gain, x, *weights)
    return list(outs[:ways]), list(outs[ways:])


def state_kernel(count, proj_ref, *refs):
    pieces, (state_ref, share_ref) = refs[:count], refs[count:]
    state = sum(p[...].astype(F32) for p in pieces).astype(BF16)
    state_ref[...] = state
    patches = share_ref.shape[0]
    width = proj_ref.shape[1]
    for b in range(state.shape[0] // patches):
        share_ref[:, b * width : (b + 1) * width] = dot(state[b * patches : (b + 1) * patches], proj_ref[...]).astype(BF16)


def finish_state(proj, pieces, own):
    rows, width = pieces[0].shape
    return pl.pallas_call(
        functools.partial(state_kernel, len(pieces)),
        in_specs=[VMEM] * (1 + len(pieces)),
        out_specs=(VMEM, VMEM),
        out_shape=(
            jax.ShapeDtypeStruct((rows, width), BF16),
            jax.ShapeDtypeStruct((rows // own, own * proj.shape[1]), BF16),
        ),
        compiler_params=pltpu.CompilerParams(vmem_limit_bytes=8 * 2**20),
        name="finish_state",
    )(proj, *pieces)


def fetch_kernel(source, held, sems):
    parts = source.shape[0]
    copies = [pltpu.make_async_copy(source.at[i], held.at[i], sems.at[i]) for i in range(parts)]
    for copy in copies:
        copy.start()
    for copy in copies:
        copy.wait()


def fetch(weight):
    return pl.pallas_call(
        fetch_kernel,
        in_specs=[HBM],
        out_specs=VMEM,
        out_shape=pltpu.VMEM(weight.shape, weight.dtype),
        scratch_shapes=[pltpu.SemaphoreType.DMA((weight.shape[0],))],
        compiler_params=pltpu.CompilerParams(vmem_limit_bytes=50 * 2**20),
        name="fetch",
    )(weight)


def heads_kernel(depth, core_ref, ids_ref, gain_ref, *refs):
    ways = gain_ref.shape[0]
    early, late, weight, outs = refs[:ways], refs[ways : 2 * ways], refs[2 * ways], refs[2 * ways + 1 :]
    width = early[0].shape[1]
    values = [jnp.concatenate([a[...], b[...]], axis=0).astype(F32) for a, b in zip(early, late)]
    square = sum(jnp.sum(v * v, axis=-1, keepdims=True) for v in values)
    factor = lax.rsqrt(square / (ways * width) + EPSILON)
    normed = [(v * factor * gain_ref[ids_ref[c]]).astype(BF16) for c, v in enumerate(values)]
    size = outs[0].shape[1] // 3
    for kind in range(3):
        for i, out in ((1, outs[1]), (0, outs[0])):
            columns = pl.ds(pl.multiple_of((core_ref[0] ^ i) * size, size), size)
            mixed = sum(
                dot(n, weight[kind, pl.ds(pl.multiple_of(ids_ref[c] * width, width), width), columns])
                for c, n in enumerate(normed)
            )
            if kind < 2:
                mixed = jnp.concatenate([unit(mixed[:, c : c + depth]) for c in range(0, size, depth)], axis=1)
            out[:, kind * size : (kind + 1) * size] = mixed.astype(BF16)


def global_heads(depth, core, ids, gain, early, late, qkv):
    shape = jax.ShapeDtypeStruct((2 * early[0].shape[0], 3 * qkv.shape[2] // 2), BF16)
    return pl.pallas_call(
        functools.partial(heads_kernel, depth),
        in_specs=[SMEM, SMEM] + [VMEM] * (2 + len(early) + len(late)),
        out_specs=(VMEM, VMEM),
        out_shape=(shape, shape),
        compiler_params=pltpu.CompilerParams(vmem_limit_bytes=8 * 2**20),
        name="global_heads",
    )(core, ids, gain, *early, *late, qkv)


def attend_kernel(depth, me_ref, ids_ref, scale_ref, kept_ref, given_ref, *refs):
    pieces, (own_ref, other_ref) = refs[:-2], refs[-2:]
    rows = kept_ref.shape[0]
    size = own_ref.shape[1]
    heads = size // depth
    me = me_ref[0]

    def places(index, shape, axis):
        row = lax.broadcasted_iota(jnp.int32, shape, axis)
        return jnp.where(row < rows, index * rows + row, (index ^ 1) * rows + row - rows)

    at = places(me, (2 * rows, 1), 0)
    seen = [places(i, (1, 2 * rows), 1) <= at for i in [me] + [ids_ref[p + 1] for p in range(len(pieces))]]
    own = jnp.concatenate([kept_ref[...], given_ref[...]], axis=0)
    query = own[:, :size]
    pieces = [own[:, size:]] + [p[...] for p in pieces]
    for h in range(heads):
        cut = slice(h * depth, (h + 1) * depth)
        factor = scale_ref[(me % 2) * heads + h] / math.sqrt(depth)
        scores = [jnp.where(s, dot_t(query[:, cut], p[:, cut]) * factor, NEGATIVE) for s, p in zip(seen, pieces)]
        top = functools.reduce(jnp.maximum, [jnp.max(s, axis=-1, keepdims=True) for s in scores])
        weights = [jnp.exp(s - top) for s in scores]
        total = sum(jnp.sum(w, axis=-1, keepdims=True) for w in weights)
        values = slice(size + h * depth, size + (h + 1) * depth)
        summed = sum(dot(w.astype(BF16), p[:, values]) for w, p in zip(weights, pieces))
        attended = (summed / total).astype(BF16)
        own_ref[:, cut] = attended[:rows]
        other_ref[:, cut] = attended[rows:]


def attend(depth, me, ids, scale, kept, given, pieces):
    rows = kept.shape[0]
    shape = jax.ShapeDtypeStruct((rows, kept.shape[1] // 3), BF16)
    return pl.pallas_call(
        functools.partial(attend_kernel, depth),
        in_specs=[SMEM, SMEM, SMEM] + [VMEM] * (2 + len(pieces)),
        out_specs=(VMEM, VMEM),
        out_shape=(shape, shape),
        compiler_params=pltpu.CompilerParams(vmem_limit_bytes=20 * 2**20),
        cost_estimate=BRIEF,
        name="attend",
    )(me, ids, scale, kept, given, *pieces)


def project_kernel(core_ref, slots_ref, own_ref, other_ref, proj_ref, *outs):
    size = own_ref.shape[1]
    own_rows = pl.ds(pl.multiple_of(core_ref[0] * size, size), size)
    other_rows = pl.ds(pl.multiple_of((core_ref[0] ^ 1) * size, size), size)
    for slot, out in enumerate(outs):
        width = out.shape[1]
        columns = pl.ds(pl.multiple_of(slots_ref[slot] * width, width), width)
        out[...] = (dot(own_ref[...], proj_ref[own_rows, columns]) + dot(other_ref[...], proj_ref[other_rows, columns])).astype(BF16)


def project(core, slots, own, other, proj):
    ways = slots.shape[0]
    return pl.pallas_call(
        project_kernel,
        in_specs=[SMEM, SMEM] + [VMEM] * 3,
        out_specs=[VMEM] * ways,
        out_shape=[jax.ShapeDtypeStruct((own.shape[0], proj.shape[1] // ways), BF16)] * ways,
        compiler_params=pltpu.CompilerParams(vmem_limit_bytes=6 * 2**20),
        cost_estimate=BRIEF,
        name="project",
    )(core, slots, own, other, proj)


def result_kernel(count, order_ref, own_ref, *refs):
    pieces, (result_ref, kept_ref, given_ref) = refs[:count], refs[count:]
    total = own_ref[...].astype(F32) + sum(p[...].astype(F32) for p in pieces)
    result = total.astype(BF16)
    result_ref[...] = result
    routed = dot(order_ref[...], result).astype(BF16)
    half = kept_ref.shape[0]
    kept_ref[...] = routed[:half]
    given_ref[...] = routed[half:]


def finish_result(order, residual, pieces):
    rows, width = residual.shape
    shape = jax.ShapeDtypeStruct(residual.shape, BF16)
    half = jax.ShapeDtypeStruct((rows // 2, width), BF16)
    return pl.pallas_call(
        functools.partial(result_kernel, len(pieces)),
        in_specs=[VMEM] * (2 + len(pieces)),
        out_specs=(VMEM, VMEM, VMEM),
        out_shape=(shape, half, half),
        compiler_params=pltpu.CompilerParams(vmem_limit_bytes=4 * 2**20),
        cost_estimate=BRIEF,
        name="finish_result",
    )(order, residual, *pieces)


def sort_kernel(block, devices, rows_ref, out_ref):
    me = lax.axis_index("seq")
    rows = rows_ref.shape[0]
    to = lax.broadcasted_iota(jnp.int32, (rows, rows), 0)
    at = lax.broadcasted_iota(jnp.int32, (rows, rows), 1)
    twin = lax.rem(me - at // (2 * block) * 2 + devices, devices)
    source = twin ^ (at // block % 2)
    order = (to == source * block + at % block).astype(F32).astype(BF16)
    out_ref[...] = dot(order, rows_ref[...]).astype(BF16)


def sort_rows(rows, devices):
    return pl.pallas_call(
        functools.partial(sort_kernel, rows.shape[0] // devices, devices),
        in_specs=[VMEM],
        out_specs=VMEM,
        out_shape=jax.ShapeDtypeStruct(rows.shape, BF16),
        compiler_params=pltpu.CompilerParams(vmem_limit_bytes=4 * 2**20),
        cost_estimate=BRIEF,
        name="sort_rows",
    )(rows)


def bytes_kernel(count, result_ref, proj_ref, *refs):
    sources, (out_ref, held, sems) = refs[:count], refs[count:]
    copies = [pltpu.make_async_copy(p, held.at[i], sems.at[i]) for i, p in enumerate(sources)]
    for copy in copies:
        copy.start()
    rows = result_ref.shape[0]
    half = rows // 2
    width = proj_ref.shape[0]
    own = out_ref.shape[0] // rows
    back = [dot(result_ref[:, b * width : (b + 1) * width], proj_ref[...]) for b in range(own)]
    back = jnp.concatenate([b[:half] for b in back] + [b[half:] for b in back], axis=0)
    at = lax.broadcasted_iota(jnp.int32, (rows * own, rows * own), 0)
    to = lax.broadcasted_iota(jnp.int32, (rows * own, rows * own), 1)
    patch = at // own
    order = (to == patch // half * half * own + at % own * half + patch % half).astype(F32).astype(BF16)
    for copy in copies:
        copy.wait()
    late = sum(held[i].astype(F32) for i in range(1, count)).astype(BF16)
    state = jnp.concatenate([held[0], late], axis=0).astype(F32)
    out_ref[...] = dot(order, (state + back).astype(BF16)).astype(BF16)


def finish_bytes(result, proj, pieces):
    rows, width = pieces[0].shape
    return pl.pallas_call(
        functools.partial(bytes_kernel, len(pieces)),
        in_specs=[VMEM, VMEM] + [pl.BlockSpec(memory_space=pl.ANY)] * len(pieces),
        out_specs=VMEM,
        out_shape=jax.ShapeDtypeStruct((2 * rows, width), BF16),
        scratch_shapes=[pltpu.VMEM((len(pieces), rows, width), BF16), pltpu.SemaphoreType.DMA((len(pieces),))],
        compiler_params=pltpu.CompilerParams(vmem_limit_bytes=16 * 2**20),
        cost_estimate=BRIEF,
        name="finish_bytes",
    )(result, proj, *pieces)


def shift(value, axis, step):
    count = lax.axis_size(axis)
    return lax.ppermute(value, axis, [(i, (i + step) % count) for i in range(count)])


def scatter(chunks, axis):
    return [chunks[0]] + [shift(chunk, axis, step) for step, chunk in enumerate(chunks[1:], 1)]


def shift_slots(axis):
    count = lax.axis_size(axis)
    return ((lax.axis_index(axis) + jnp.arange(count)) % count).astype(jnp.int32)


def gather(value, axis):
    return [value] + [shift(value, axis, step) for step in range(1, lax.axis_size(axis))]


def swap_cores(value, axis):
    return lax.ppermute(value, axis, [(i, i ^ 1) for i in range(lax.axis_size(axis))])


def twin_ids(axis):
    count = lax.axis_size(axis)
    return ((lax.axis_index(axis) - 2 * jnp.arange(count // 2)) % count).astype(jnp.int32)


def owner_order(owners, source, patches):
    devices, count = owners.shape
    listed = lax.dynamic_index_in_dim(owners, source, 0, keepdims=False)
    block = patches // count
    index = jnp.arange(count, dtype=jnp.int32)
    rank = jnp.sum((listed[None, :] == listed[:, None]) & (index[None, :] < index[:, None]), axis=1).astype(jnp.int32)
    chips = devices // 2
    order = (listed % 2 ^ source % 2) * chips + (listed // 2 - source // 2 + chips) % chips
    slot = order * (count // devices) + rank
    row = jnp.arange(patches, dtype=jnp.int32)
    spread = jnp.sum(jnp.where(row[:, None] // block == index[None, :], slot[None, :], 0), axis=1).astype(jnp.int32)
    place = spread * block + row % block
    return (row[:, None] == place[None, :]).astype(BF16)


def route(kept, given, axis):
    devices = lax.axis_size(axis)
    chips = devices // 2
    width = kept.shape[1]
    received = swap_cores(given, axis)
    bundles = jnp.concatenate([a.reshape(chips, -1, width) for a in (kept, received)], axis=1)
    arrived = [bundles[0]] + [shift(bundles[step], axis, 2 * step) for step in range(1, chips)]
    return sort_rows(jnp.concatenate(arrived, axis=0), devices)


def on_device(
    byte_in,
    local_gain,
    local_qkv,
    local_out,
    mlp_up,
    mlp_down,
    local_scale,
    patch_proj,
    global_gain,
    global_qkv,
    global_out,
    global_scale,
    back_proj,
    owners,
):
    patches, span, width = byte_in.shape
    ways = lax.axis_size("head")
    own = span // ways
    me = lax.axis_index("head").astype(jnp.int32)
    seq = lax.axis_index("seq").astype(jnp.int32)
    depth = global_qkv.shape[2] // global_scale.shape[0]

    slots = shift_slots("head")
    rows = byte_in.reshape(-1, width)
    weights = [jnp.transpose(local_qkv, (1, 0, 2)), mlp_up, local_out, mlp_down, patch_proj]
    gain = local_gain.reshape(1, -1)
    early, _ = local_part(local_scale, rows, gain, weights, span, ways, False)
    early = scatter(early, "head")
    parts, chunks = local_part(local_scale, rows, gain, weights, span, ways, True)
    chunks, early[1] = lax.optimization_barrier((chunks, early[1]))
    chunks = scatter(chunks, "head")
    early, early_share = finish_state(patch_proj, early, own)
    early_shares = gather(early_share, "head")
    late_share = sum(p.astype(F32) for p in chunks).astype(BF16)
    weight = jnp.transpose(global_qkv, (1, 0, 2))
    weight, late_share = lax.optimization_barrier((weight, late_share))
    late_shares = gather(late_share, "head")
    early_shares, late_shares, weight, parts[1] = lax.optimization_barrier(
        (early_shares, late_shares, fetch(weight), parts[1])
    )
    parts[1] = shift(parts[1], "head", 1)
    residual = jnp.concatenate([early_share, late_share], axis=0)
    ids = (me - jnp.arange(ways, dtype=jnp.int32)) % ways
    core = (seq % 2).reshape(1)
    kept, given = global_heads(depth, core, ids, global_gain.reshape(ways, 1, -1), early_shares, late_shares, weight)
    received = swap_cores(given, "seq")
    received, parts[2:] = lax.optimization_barrier((received, parts[2:]))
    half = kept.shape[1] // 3
    keyed = jnp.concatenate([kept[:, half:], received[:, half:]], axis=0)
    pieces = [shift(keyed, "seq", 2 * step) for step in range(1, lax.axis_size("seq") // 2)]
    parts[2:] = [shift(part, "head", step) for step, part in enumerate(parts[2:], 2)]
    kept, parts[1] = lax.optimization_barrier((kept, parts[1]))
    own_heads, other_heads = attend(depth, seq.reshape(1), twin_ids("seq"), global_scale, kept, received, pieces)
    other_heads, parts[2] = lax.optimization_barrier((swap_cores(other_heads, "seq"), parts[2]))
    updates = scatter(project(core, slots, own_heads, other_heads, global_out), "head")
    updates, parts[3:] = lax.optimization_barrier((updates, parts[3:]))
    result, kept, given = finish_result(owner_order(owners, seq, patches), residual, updates)
    global_state = route(kept, given, "seq")
    byte_out = finish_bytes(result, back_proj, [early] + parts)
    return byte_out.reshape(patches, own, width), global_state


def solution(mesh):
    placed = (
        P("seq", None, None),
        P(),
        P(None, None, "head"),
        P("head", None),
        P(None, "head"),
        P("head", None),
        P("head"),
        P(),
        P(),
        P(None, None, "head"),
        P("head", None),
        P("head"),
        P(),
        P(),
    )
    return jax.shard_map(
        on_device,
        mesh=mesh,
        in_specs=placed,
        out_specs=(P("seq", "head", None), P("seq", "head")),
        check_vma=False,
    )
```

```python
import functools
import math

import jax
import jax.numpy as jnp
from jax import lax
from jax.experimental import pallas as pl
from jax.experimental.pallas import tpu as pltpu
from jax.sharding import PartitionSpec as P

EPSILON = 1e-06
NEGATIVE = -1e30
F32 = jnp.float32
BF16 = jnp.bfloat16
BRIEF = pl.CostEstimate(flops=1, bytes_accessed=1, transcendentals=0)
VMEM = pl.BlockSpec(memory_space=pltpu.VMEM)
HBM = pl.BlockSpec(memory_space=pltpu.HBM)
SMEM = pl.BlockSpec(memory_space=pltpu.SMEM)


def dot(left, right):
    return jnp.dot(left, right, preferred_element_type=F32)


def dot_t(left, right):
    return lax.dot_general(left, right, (((1,), (1,)), ((), ())), preferred_element_type=F32)


def unit(values):
    return (values * lax.rsqrt(jnp.mean(values * values, axis=-1, keepdims=True) + EPSILON)).astype(BF16)


def gelu(values):
    inner = math.sqrt(2.0 / math.pi) * (values + 0.044715 * (values * values * values))
    return 0.5 * values * (1.0 + jnp.tanh(inner))


def local_kernel(span, ways, piece, last, scale_ref, gain_ref, x_hbm, *refs):
    sources, parts, others = refs[:5], refs[5 : 5 + ways], refs[5 + ways : -11]
    held, (x_ref, part_ref, share_ref, in_sem, x_sem, part_sem) = refs[-11:-6], refs[-6:]
    patches = share_ref.shape[1]
    own = span // ways
    rows = piece * span
    pieces = patches // piece
    cuts = [slice(i * rows, (i + 1) * rows) for i in range(pieces)]
    skip = x_ref.shape[0] if last else 0
    loads = [
        pltpu.make_async_copy(x_hbm.at[pl.ds(skip + c.start, rows)], x_ref.at[pl.ds(c.start, rows)], x_sem.at[i])
        for i, c in enumerate(cuts)
    ]
    loads += [pltpu.make_async_copy(s, h, in_sem.at[i]) for i, (s, h) in enumerate(zip(sources, held))]
    for copy in loads:
        copy.start()
    me = lax.axis_index("head")
    at = lax.broadcasted_iota(jnp.int32, (rows, rows), 0)
    to = lax.broadcasted_iota(jnp.int32, (rows, rows), 1)
    order = (to == (at % piece) * span + at // piece).astype(F32).astype(BF16)
    kept = lax.broadcasted_iota(jnp.int32, (rows, 1), 0) // piece // own == me
    for copy in loads:
        copy.wait()
    qkv_ref, up_ref, out_ref, down_ref, proj_ref = held
    xs, normed = [], []
    for cut in cuts:
        x = dot(order, x_ref[cut])
        xs.append(jnp.where(kept, x, 0.0).astype(BF16))
        factor = lax.rsqrt(jnp.mean(x * x, axis=-1, keepdims=True) + EPSILON)
        normed.append((x * factor * gain_ref[...]).astype(BF16))
    xs, normed = jnp.concatenate(xs, axis=0), jnp.concatenate(normed, axis=0)
    query, key, value = (dot(normed, qkv_ref[i]) for i in range(3))
    seen = (at % piece == to % piece) & (to <= at)
    heads = scale_ref.shape[0]
    depth = query.shape[1] // heads
    attended = []
    for cut in cuts:
        columns = []
        for h in range(heads):
            head = slice(h * depth, (h + 1) * depth)
            scores = dot_t(unit(query[cut, head]), unit(key[cut, head])) * (scale_ref[h] / math.sqrt(depth))
            scores = jnp.where(seen, scores, NEGATIVE)
            weights = jnp.exp(scores - jnp.max(scores, axis=-1, keepdims=True))
            total = jnp.sum(weights, axis=-1, keepdims=True)
            columns.append((dot(weights.astype(BF16), value[cut, head].astype(BF16)) / total).astype(BF16))
        attended.append(jnp.concatenate(columns, axis=1))
    act = gelu(dot(normed, up_ref[...])).astype(BF16)
    mixed = jnp.concatenate([jnp.concatenate(attended, axis=0), act], axis=1)
    partial = dot(mixed, jnp.concatenate([out_ref[...], down_ref[...]], axis=0)) + xs.astype(F32)
    partial = partial.astype(BF16)
    for i, cut in enumerate(cuts):
        for b in range(span):
            put = (b % own) * patches + i * piece
            part_ref[b // own, put : put + piece] = partial[cut][b * piece : (b + 1) * piece]
    stores = []
    for slot, part in enumerate(parts):
        stores.append(pltpu.make_async_copy(part_ref.at[lax.rem(me + slot, ways)], part, part_sem.at[slot]))
        stores[-1].start()
    if last:
        share = dot(partial, proj_ref[...]).astype(BF16)
        size = share.shape[1]
        for i, cut in enumerate(cuts):
            for b in range(span):
                put = slice((b % own) * size, (b % own + 1) * size)
                share_ref[b // own, i * piece : (i + 1) * piece, put] = share[cut][b * piece : (b + 1) * piece]
        for slot, out in enumerate(others):
            out[...] = share_ref[lax.rem(me + slot, ways)]
    for copy in stores:
        copy.wait()


def local_part(scale, x, gain, weights, span, ways, last):
    rows, width = x.shape[0] // 2, x.shape[1]
    patches = rows // span
    own = span // ways
    piece = math.gcd(patches, 32)
    part = (own * patches, width)
    share = (patches, own * weights[-1].shape[1])
    others = [pltpu.VMEM(share, BF16)] * (ways if last else 0)
    outs = pl.pallas_call(
        functools.partial(local_kernel, span, ways, piece, last),
        in_specs=[SMEM, VMEM, HBM] + [HBM] * len(weights),
        out_specs=[HBM] * ways + [VMEM] * len(others),
        out_shape=[jax.ShapeDtypeStruct(part, BF16)] * ways + others,
        scratch_shapes=[pltpu.VMEM(w.shape, w.dtype) for w in weights]
        + [
            pltpu.VMEM((rows, width), BF16),
            pltpu.VMEM((ways, *part), BF16),
            pltpu.VMEM((ways, *share), BF16),
            pltpu.SemaphoreType.DMA((len(weights),)),
            pltpu.SemaphoreType.DMA((patches // piece,)),
            pltpu.SemaphoreType.DMA((ways,)),
        ],
        compiler_params=pltpu.CompilerParams(vmem_limit_bytes=60 * 2**20),
        cost_estimate=pl.CostEstimate(flops=8 * rows * width * width, bytes_accessed=10 * 2**20, transcendentals=rows * width),
        name="local_part",
    )(scale, gain, x, *weights)
    return list(outs[:ways]), list(outs[ways:])


def state_kernel(count, proj_ref, *refs):
    pieces, (state_ref, share_ref) = refs[:count], refs[count:]
    state = sum(p[...].astype(F32) for p in pieces).astype(BF16)
    state_ref[...] = state
    patches = share_ref.shape[0]
    width = proj_ref.shape[1]
    for b in range(state.shape[0] // patches):
        share_ref[:, b * width : (b + 1) * width] = dot(state[b * patches : (b + 1) * patches], proj_ref[...]).astype(BF16)


def finish_state(proj, pieces, own):
    rows, width = pieces[0].shape
    return pl.pallas_call(
        functools.partial(state_kernel, len(pieces)),
        in_specs=[VMEM] * (1 + len(pieces)),
        out_specs=(VMEM, VMEM),
        out_shape=(
            jax.ShapeDtypeStruct((rows, width), BF16),
            jax.ShapeDtypeStruct((rows // own, own * proj.shape[1]), BF16),
        ),
        compiler_params=pltpu.CompilerParams(vmem_limit_bytes=8 * 2**20),
        name="finish_state",
    )(proj, *pieces)


def fetch_kernel(source, held, sems):
    parts = source.shape[0]
    copies = [pltpu.make_async_copy(source.at[i], held.at[i], sems.at[i]) for i in range(parts)]
    for copy in copies:
        copy.start()
    for copy in copies:
        copy.wait()


def fetch(weight):
    return pl.pallas_call(
        fetch_kernel,
        in_specs=[HBM],
        out_specs=VMEM,
        out_shape=pltpu.VMEM(weight.shape, weight.dtype),
        scratch_shapes=[pltpu.SemaphoreType.DMA((weight.shape[0],))],
        compiler_params=pltpu.CompilerParams(vmem_limit_bytes=50 * 2**20),
        name="fetch",
    )(weight)


def heads_kernel(depth, core_ref, ids_ref, gain_ref, *refs):
    ways = gain_ref.shape[0]
    early, late, weight, outs = refs[:ways], refs[ways : 2 * ways], refs[2 * ways], refs[2 * ways + 1 :]
    width = early[0].shape[1]
    values = [jnp.concatenate([a[...], b[...]], axis=0).astype(F32) for a, b in zip(early, late)]
    square = sum(jnp.sum(v * v, axis=-1, keepdims=True) for v in values)
    factor = lax.rsqrt(square / (ways * width) + EPSILON)
    normed = [(v * factor * gain_ref[ids_ref[c]]).astype(BF16) for c, v in enumerate(values)]
    size = outs[0].shape[1] // 3
    for kind in range(3):
        for i, out in ((1, outs[1]), (0, outs[0])):
            columns = pl.ds(pl.multiple_of((core_ref[0] ^ i) * size, size), size)
            mixed = sum(
                dot(n, weight[kind, pl.ds(pl.multiple_of(ids_ref[c] * width, width), width), columns])
                for c, n in enumerate(normed)
            )
            if kind < 2:
                mixed = jnp.concatenate([unit(mixed[:, c : c + depth]) for c in range(0, size, depth)], axis=1)
            out[:, kind * size : (kind + 1) * size] = mixed.astype(BF16)


def global_heads(depth, core, ids, gain, early, late, qkv):
    shape = jax.ShapeDtypeStruct((2 * early[0].shape[0], 3 * qkv.shape[2] // 2), BF16)
    return pl.pallas_call(
        functools.partial(heads_kernel, depth),
        in_specs=[SMEM, SMEM] + [VMEM] * (2 + len(early) + len(late)),
        out_specs=(VMEM, VMEM),
        out_shape=(shape, shape),
        compiler_params=pltpu.CompilerParams(vmem_limit_bytes=8 * 2**20),
        name="global_heads",
    )(core, ids, gain, *early, *late, qkv)


def attend_kernel(depth, me_ref, ids_ref, scale_ref, kept_ref, given_ref, *refs):
    pieces, (own_ref, other_ref) = refs[:-2], refs[-2:]
    rows = kept_ref.shape[0]
    size = own_ref.shape[1]
    heads = size // depth
    me = me_ref[0]

    def places(index, shape, axis):
        row = lax.broadcasted_iota(jnp.int32, shape, axis)
        return jnp.where(row < rows, index * rows + row, (index ^ 1) * rows + row - rows)

    at = places(me, (2 * rows, 1), 0)
    seen = [places(i, (1, 2 * rows), 1) <= at for i in [me] + [ids_ref[p + 1] for p in range(len(pieces))]]
    own = jnp.concatenate([kept_ref[...], given_ref[...]], axis=0)
    query = own[:, :size]
    pieces = [own[:, size:]] + [p[...] for p in pieces]
    for h in range(heads):
        cut = slice(h * depth, (h + 1) * depth)
        factor = scale_ref[(me % 2) * heads + h] / math.sqrt(depth)
        scores = [jnp.where(s, dot_t(query[:, cut], p[:, cut]) * factor, NEGATIVE) for s, p in zip(seen, pieces)]
        top = functools.reduce(jnp.maximum, [jnp.max(s, axis=-1, keepdims=True) for s in scores])
        weights = [jnp.exp(s - top) for s in scores]
        total = sum(jnp.sum(w, axis=-1, keepdims=True) for w in weights)
        values = slice(size + h * depth, size + (h + 1) * depth)
        summed = sum(dot(w.astype(BF16), p[:, values]) for w, p in zip(weights, pieces))
        attended = (summed / total).astype(BF16)
        own_ref[:, cut] = attended[:rows]
        other_ref[:, cut] = attended[rows:]


def attend(depth, me, ids, scale, kept, given, pieces):
    rows = kept.shape[0]
    shape = jax.ShapeDtypeStruct((rows, kept.shape[1] // 3), BF16)
    return pl.pallas_call(
        functools.partial(attend_kernel, depth),
        in_specs=[SMEM, SMEM, SMEM] + [VMEM] * (2 + len(pieces)),
        out_specs=(VMEM, VMEM),
        out_shape=(shape, shape),
        compiler_params=pltpu.CompilerParams(vmem_limit_bytes=20 * 2**20),
        cost_estimate=BRIEF,
        name="attend",
    )(me, ids, scale, kept, given, *pieces)


def project_kernel(core_ref, slots_ref, own_ref, other_ref, proj_ref, *outs):
    size = own_ref.shape[1]
    own_rows = pl.ds(pl.multiple_of(core_ref[0] * size, size), size)
    other_rows = pl.ds(pl.multiple_of((core_ref[0] ^ 1) * size, size), size)
    for slot, out in enumerate(outs):
        width = out.shape[1]
        columns = pl.ds(pl.multiple_of(slots_ref[slot] * width, width), width)
        out[...] = (dot(own_ref[...], proj_ref[own_rows, columns]) + dot(other_ref[...], proj_ref[other_rows, columns])).astype(BF16)


def project(core, slots, own, other, proj):
    ways = slots.shape[0]
    return pl.pallas_call(
        project_kernel,
        in_specs=[SMEM, SMEM] + [VMEM] * 3,
        out_specs=[VMEM] * ways,
        out_shape=[jax.ShapeDtypeStruct((own.shape[0], proj.shape[1] // ways), BF16)] * ways,
        compiler_params=pltpu.CompilerParams(vmem_limit_bytes=6 * 2**20),
        cost_estimate=BRIEF,
        name="project",
    )(core, slots, own, other, proj)


def result_kernel(count, order_ref, own_ref, *refs):
    pieces, (result_ref, kept_ref, given_ref) = refs[:count], refs[count:]
    total = own_ref[...].astype(F32) + sum(p[...].astype(F32) for p in pieces)
    result = total.astype(BF16)
    result_ref[...] = result
    routed = dot(order_ref[...], result).astype(BF16)
    half = kept_ref.shape[0]
    kept_ref[...] = routed[:half]
    given_ref[...] = routed[half:]


def finish_result(order, residual, pieces):
    rows, width = residual.shape
    shape = jax.ShapeDtypeStruct(residual.shape, BF16)
    half = jax.ShapeDtypeStruct((rows // 2, width), BF16)
    return pl.pallas_call(
        functools.partial(result_kernel, len(pieces)),
        in_specs=[VMEM] * (2 + len(pieces)),
        out_specs=(VMEM, VMEM, VMEM),
        out_shape=(shape, half, half),
        compiler_params=pltpu.CompilerParams(vmem_limit_bytes=4 * 2**20),
        cost_estimate=BRIEF,
        name="finish_result",
    )(order, residual, *pieces)


def sort_kernel(block, devices, rows_ref, out_ref):
    me = lax.axis_index("seq")
    rows = rows_ref.shape[0]
    to = lax.broadcasted_iota(jnp.int32, (rows, rows), 0)
    at = lax.broadcasted_iota(jnp.int32, (rows, rows), 1)
    twin = lax.rem(me - at // (2 * block) * 2 + devices, devices)
    source = twin ^ (at // block % 2)
    order = (to == source * block + at % block).astype(F32).astype(BF16)
    out_ref[...] = dot(order, rows_ref[...]).astype(BF16)


def sort_rows(rows, devices):
    return pl.pallas_call(
        functools.partial(sort_kernel, rows.shape[0] // devices, devices),
        in_specs=[VMEM],
        out_specs=VMEM,
        out_shape=jax.ShapeDtypeStruct(rows.shape, BF16),
        compiler_params=pltpu.CompilerParams(vmem_limit_bytes=4 * 2**20),
        cost_estimate=BRIEF,
        name="sort_rows",
    )(rows)


def bytes_kernel(count, result_ref, proj_ref, *refs):
    sources, (out_ref, held, sems) = refs[:count], refs[count:]
    copies = [pltpu.make_async_copy(p, held.at[i], sems.at[i]) for i, p in enumerate(sources)]
    for copy in copies:
        copy.start()
    rows = result_ref.shape[0]
    half = rows // 2
    width = proj_ref.shape[0]
    own = out_ref.shape[1]
    back = [dot(result_ref[:, b * width : (b + 1) * width], proj_ref[...]) for b in range(own)]
    back = jnp.concatenate([b[:half] for b in back] + [b[half:] for b in back], axis=0)
    at = lax.broadcasted_iota(jnp.int32, (rows * own, rows * own), 0)
    to = lax.broadcasted_iota(jnp.int32, (rows * own, rows * own), 1)
    patch = at // own
    order = (to == patch // half * half * own + at % own * half + patch % half).astype(F32).astype(BF16)
    for copy in copies:
        copy.wait()
    late = sum(held[i].astype(F32) for i in range(1, count)).astype(BF16)
    state = jnp.concatenate([held[0], late], axis=0).astype(F32)
    out_ref[...] = dot(order, (state + back).astype(BF16)).reshape(out_ref.shape).astype(BF16)


def finish_bytes(result, proj, pieces):
    rows, width = pieces[0].shape
    return pl.pallas_call(
        functools.partial(bytes_kernel, len(pieces)),
        in_specs=[VMEM, VMEM] + [pl.BlockSpec(memory_space=pl.ANY)] * len(pieces),
        out_specs=VMEM,
        out_shape=jax.ShapeDtypeStruct((result.shape[0], 2 * rows // result.shape[0], width), BF16),
        scratch_shapes=[pltpu.VMEM((len(pieces), rows, width), BF16), pltpu.SemaphoreType.DMA((len(pieces),))],
        compiler_params=pltpu.CompilerParams(vmem_limit_bytes=16 * 2**20),
        cost_estimate=BRIEF,
        name="finish_bytes",
    )(result, proj, *pieces)


def shift(value, axis, step):
    count = lax.axis_size(axis)
    return lax.ppermute(value, axis, [(i, (i + step) % count) for i in range(count)])


def scatter(chunks, axis):
    return [chunks[0]] + [shift(chunk, axis, step) for step, chunk in enumerate(chunks[1:], 1)]


def shift_slots(axis):
    count = lax.axis_size(axis)
    return ((lax.axis_index(axis) + jnp.arange(count)) % count).astype(jnp.int32)


def gather(value, axis):
    return [value] + [shift(value, axis, step) for step in range(1, lax.axis_size(axis))]


def swap_cores(value, axis):
    return lax.ppermute(value, axis, [(i, i ^ 1) for i in range(lax.axis_size(axis))])


def twin_ids(axis):
    count = lax.axis_size(axis)
    return ((lax.axis_index(axis) - 2 * jnp.arange(count // 2)) % count).astype(jnp.int32)


def owner_order(owners, source, patches):
    devices, count = owners.shape
    listed = lax.dynamic_index_in_dim(owners, source, 0, keepdims=False)
    block = patches // count
    index = jnp.arange(count, dtype=jnp.int32)
    rank = jnp.sum((listed[None, :] == listed[:, None]) & (index[None, :] < index[:, None]), axis=1).astype(jnp.int32)
    chips = devices // 2
    order = (listed % 2 ^ source % 2) * chips + (listed // 2 - source // 2 + chips) % chips
    slot = order * (count // devices) + rank
    row = jnp.arange(patches, dtype=jnp.int32)
    spread = jnp.sum(jnp.where(row[:, None] // block == index[None, :], slot[None, :], 0), axis=1).astype(jnp.int32)
    place = spread * block + row % block
    return (row[:, None] == place[None, :]).astype(BF16)


def route(kept, given, axis):
    devices = lax.axis_size(axis)
    chips = devices // 2
    width = kept.shape[1]
    received = swap_cores(given, axis)
    bundles = jnp.concatenate([a.reshape(chips, -1, width) for a in (kept, received)], axis=1)
    arrived = [bundles[0]] + [shift(bundles[step], axis, 2 * step) for step in range(1, chips)]
    return sort_rows(jnp.concatenate(arrived, axis=0), devices)


def on_device(
    byte_in,
    local_gain,
    local_qkv,
    local_out,
    mlp_up,
    mlp_down,
    local_scale,
    patch_proj,
    global_gain,
    global_qkv,
    global_out,
    global_scale,
    back_proj,
    owners,
):
    patches, span, width = byte_in.shape
    ways = lax.axis_size("head")
    own = span // ways
    me = lax.axis_index("head").astype(jnp.int32)
    seq = lax.axis_index("seq").astype(jnp.int32)
    depth = global_qkv.shape[2] // global_scale.shape[0]

    slots = shift_slots("head")
    rows = byte_in.reshape(-1, width)
    weights = [jnp.transpose(local_qkv, (1, 0, 2)), mlp_up, local_out, mlp_down, patch_proj]
    gain = local_gain.reshape(1, -1)
    early, _ = local_part(local_scale, rows, gain, weights, span, ways, False)
    early = scatter(early, "head")
    parts, chunks = local_part(local_scale, rows, gain, weights, span, ways, True)
    chunks, early[1] = lax.optimization_barrier((chunks, early[1]))
    chunks = scatter(chunks, "head")
    early, early_share = finish_state(patch_proj, early, own)
    early_shares = gather(early_share, "head")
    late_share = sum(p.astype(F32) for p in chunks).astype(BF16)
    weight = jnp.transpose(global_qkv, (1, 0, 2))
    weight, late_share = lax.optimization_barrier((weight, late_share))
    late_shares = gather(late_share, "head")
    early_shares, late_shares, weight, parts[1] = lax.optimization_barrier(
        (early_shares, late_shares, fetch(weight), parts[1])
    )
    parts[1] = shift(parts[1], "head", 1)
    residual = jnp.concatenate([early_share, late_share], axis=0)
    ids = (me - jnp.arange(ways, dtype=jnp.int32)) % ways
    core = (seq % 2).reshape(1)
    kept, given = global_heads(depth, core, ids, global_gain.reshape(ways, 1, -1), early_shares, late_shares, weight)
    received = swap_cores(given, "seq")
    received, parts[2:] = lax.optimization_barrier((received, parts[2:]))
    half = kept.shape[1] // 3
    keyed = jnp.concatenate([kept[:, half:], received[:, half:]], axis=0)
    pieces = [shift(keyed, "seq", 2 * step) for step in range(1, lax.axis_size("seq") // 2)]
    parts[2:] = [shift(part, "head", step) for step, part in enumerate(parts[2:], 2)]
    kept, parts[1] = lax.optimization_barrier((kept, parts[1]))
    own_heads, other_heads = attend(depth, seq.reshape(1), twin_ids("seq"), global_scale, kept, received, pieces)
    other_heads, parts[2] = lax.optimization_barrier((swap_cores(other_heads, "seq"), parts[2]))
    updates = scatter(project(core, slots, own_heads, other_heads, global_out), "head")
    updates, parts[3:] = lax.optimization_barrier((updates, parts[3:]))
    result, kept, given = finish_result(owner_order(owners, seq, patches), residual, updates)
    global_state = route(kept, given, "seq")
    byte_out = finish_bytes(result, back_proj, [early] + parts)
    return byte_out, global_state


def solution(mesh):
    placed = (
        P("seq", None, None),
        P(),
        P(None, None, "head"),
        P("head", None),
        P(None, "head"),
        P("head", None),
        P("head"),
        P(),
        P(),
        P(None, None, "head"),
        P("head", None),
        P("head"),
        P(),
        P(),
    )
    return jax.shard_map(
        on_device,
        mesh=mesh,
        in_specs=placed,
        out_specs=(P("seq", "head", None), P("seq", "head")),
        check_vma=False,
    )
```
